32 devices in a mesh: dp: 4 (over y, x), seq: 8 (over z, core).
Axes of the slice: x: 2, y: 2, z: 4, core: 2. Of those that a mesh axis runs over, the one named last changes fastest.
Arguments:
- tokens: bfloat16 [12, 1024, 512], P('dp', 'seq'), may hold values from -6 to 6
- grad_out: bfloat16 [12, 1024, 512], P('dp', 'seq'), may hold values from -6 to 6
- crop: int32 [12], P('dp'), may hold values from 512 to 1024
- offsets: int32 [12, 4], P('dp'), may hold values from 0 to 1023, as said below
- w_query: bfloat16 [512, 512], replicated, may hold values from -0.25 to 0.25
- w_key: bfloat16 [512, 512], replicated, may hold values from -0.25 to 0.25
- w_value: bfloat16 [512, 512], replicated, may hold values from -0.25 to 0.25
- w_out: bfloat16 [512, 512], replicated, may hold values from -6 to 6
- w_up: bfloat16 [512, 2048], replicated, may hold values from -0.25 to 0.25
- w_down: bfloat16 [2048, 512], replicated, may hold values from -0.125 to 0.125
- b_query: float32 [512], replicated, may hold values from -3 to 3
- b_value: float32 [512], replicated, may hold values from -3 to 3
- b_out: float32 [512], replicated, may hold values from -3 to 3
- b_up: float32 [2048], replicated, may hold values from -3 to 3
- b_down: float32 [512], replicated, may hold values from -3 to 3
- gain_one: float32 [512], replicated, may hold values from 0.5 to 1.5
- shift_one: float32 [512], replicated, may hold values from -3 to 3
- gain_two: float32 [512], replicated, may hold values from 0.5 to 1.5
- shift_two: float32 [512], replicated, may hold values from -3 to 3
Outputs:
- activations: bfloat16 [12, 1024, 512], P('dp', 'seq')
- input_grad: bfloat16 [12, 1024, 512], P('dp', 'seq')
- grad_w_query: float32 [512, 512], replicated
- grad_w_key: float32 [512, 512], replicated
- grad_w_value: float32 [512, 512], replicated
- grad_w_out: float32 [512, 512], replicated
- grad_w_up: float32 [512, 2048], replicated
- grad_w_down: float32 [2048, 512], replicated
- grad_b_query: float32 [512], replicated
- grad_b_value: float32 [512], replicated
- grad_b_out: float32 [512], replicated
- grad_b_up: float32 [2048], replicated
- grad_b_down: float32 [512], replicated
- grad_gain_one: float32 [512], replicated
- grad_shift_one: float32 [512], replicated
- grad_gain_two: float32 [512], replicated
- grad_shift_two: float32 [512], replicated
The draws below stay inside these ranges and needn't reach their ends.
Inputs may be any that keep to these rules, and one draw needn't show every extreme that they name: offsets[r, 0] is 0, a row's offsets do not fall, and each stays below crop[r].
All inputs are finite; a program needn't handle non-finite values.
Results may differ from the reference program's by a relative error of at most 0.013.
Values may be sent and summed in bfloat16 or wider, within the bound.
No kernel may reach another device: no remote copies, remote signals or barrier semaphores. Data moves between devices by JAX's collectives and lax.ppermute only.
A program may use at most 192 MiB of HBM per device.

```python
import jax
import jax.numpy as jnp
from jax import lax

D = 512
HEADS = 8
HEAD_DIM = 64
FF = 2048
SEGS = 4
TOK_DEV = 128
ROWS_DEV = 3
LENGTH = 1024
ROWS = 12


def layout_draw(key):
    pick_key, crop_key, cut_key = jax.random.split(key, 3)
    group_count = ROWS // ROWS_DEV
    picked = jax.random.randint(pick_key, (group_count,), 0, ROWS_DEV)
    row_place = jnp.arange(ROWS, dtype=jnp.int32) % ROWS_DEV
    whole_row = row_place == jnp.repeat(picked, ROWS_DEV)
    crop_short = jax.random.randint(crop_key, (ROWS,), LENGTH // 2, LENGTH + 1)
    crop_rows = jnp.where(whole_row, LENGTH, crop_short).astype(jnp.int32)
    cuts = jax.random.randint(cut_key, (ROWS, SEGS - 1), 0, 1 << 20)
    inner = 1 + cuts % (crop_rows[:, None] - 1)
    half_block = TOK_DEV // 2
    tail = LENGTH - half_block + cuts % half_block
    tail = tail.at[:, SEGS - 2].set(LENGTH - 1)
    chosen = jnp.sort(jnp.where(whole_row[:, None], tail, inner), axis=-1).astype(jnp.int32)
    offset_rows = jnp.concatenate([jnp.zeros((ROWS, 1), jnp.int32), chosen], axis=1)
    return (crop_rows, offset_rows)


def draw_crop(key, part):
    crop_rows, offset_rows = layout_draw(key)
    return crop_rows


def draw_offsets(key, part):
    crop_rows, offset_rows = layout_draw(key)
    return offset_rows


def level_of(key, extent, cuts, smallest, largest):
    level, own = 1.0, jax.random.fold_in(key, 6)
    for axis_at, parts in cuts:
        steps = jnp.exp(jax.random.uniform(jax.random.fold_in(own, axis_at), (parts,), jnp.float32, smallest / len(cuts), largest / len(cuts)))
        level = level * jnp.repeat(steps, extent[axis_at] // parts).reshape([-1 if axis == axis_at else 1 for axis in range(len(extent))])
    return level


def gaussian(stream_key, shape, deviation, reach, pieces=(), held_as=jnp.bfloat16):
    values = deviation * jax.random.normal(stream_key, shape, jnp.float32)
    if pieces:
        values = values * level_of(stream_key, shape, pieces, -0.22, 0.18)
    return jnp.clip(values, -reach, reach).astype(held_as)


def setup_inputs(seed: int = 0) -> dict:
    keys = jax.random.split(jax.random.key(seed), 20)
    return {
        "tokens": gaussian(keys[0], (ROWS, LENGTH, D), 1.0, 6.0, ((0, 4), (1, 8))),
        "grad_out": gaussian(keys[1], (ROWS, LENGTH, D), 1.0, 6.0, ((0, 4), (1, 8))),
        "crop": draw_crop(jax.random.fold_in(keys[19], 71), 0),
        "offsets": draw_offsets(jax.random.fold_in(keys[19], 71), 0),
        "w_query": gaussian(keys[4], (D, D), D ** -0.5, 0.25),
        "w_key": gaussian(keys[5], (D, D), D ** -0.5, 0.25),
        "w_value": gaussian(keys[6], (D, D), D ** -0.5, 0.25),
        "w_out": gaussian(keys[7], (D, D), 1.0, 6.0),
        "w_up": gaussian(keys[8], (D, FF), D ** -0.5, 0.25),
        "w_down": gaussian(keys[9], (FF, D), FF ** -0.5, 0.125),
        "b_query": gaussian(keys[10], (D,), 0.5, 3.0, (), jnp.float32),
        "b_value": gaussian(keys[11], (D,), 0.5, 3.0, (), jnp.float32),
        "b_out": gaussian(keys[12], (D,), 0.3, 3.0, (), jnp.float32),
        "b_up": gaussian(keys[13], (FF,), 0.5, 3.0, (), jnp.float32),
        "b_down": gaussian(keys[14], (D,), 0.3, 3.0, (), jnp.float32),
        "gain_one": jnp.clip(1.0 + 0.1 * jax.random.normal(keys[15], (D,), jnp.float32), 0.5, 1.5),
        "shift_one": gaussian(keys[16], (D,), 0.3, 3.0, (), jnp.float32),
        "gain_two": jnp.clip(1.0 + 0.1 * jax.random.normal(keys[17], (D,), jnp.float32), 0.5, 1.5),
        "shift_two": gaussian(keys[18], (D,), 0.3, 3.0, (), jnp.float32),
    }


EPSILON = 1e-06
MASKED = -1e+30
HIGHEST = lax.Precision.HIGHEST

@jax.custom_vjp
def low(v):
    return lax.optimization_barrier(v.astype(jnp.bfloat16)).astype(jnp.float32)

@jax.custom_vjp
def low_back(v):
    return v

def low_keep(v):
    return (low(v), None)

def low_pass(kept, grad):
    return (grad,)

def back_keep(v):
    return (v, None)

def back_low(kept, grad):
    return (low(grad),)
low.defvjp(low_keep, low_pass)
low_back.defvjp(back_keep, back_low)

def layer_norm(values, gain, shift):
    center = values - lax.optimization_barrier(jnp.mean(values, axis=-1, keepdims=True))
    spread = lax.optimization_barrier(jnp.mean(center * center, axis=-1, keepdims=True))
    return center * lax.rsqrt(spread + EPSILON) * gain + shift

def matmul(left, right):
    return jnp.dot(left, right, precision=HIGHEST)

def segment_row(positions, row_offsets, row_crop):
    after = (positions[:, None] >= row_offsets[None, :]).astype(jnp.int32)
    padded = (positions >= row_crop).astype(jnp.int32)
    return lax.optimization_barrier(jnp.sum(after, axis=-1, dtype=jnp.int32)) + SEGS * padded

def forward(row_input, params, seg_index):
    w_query, w_key, w_value, w_out, w_up, w_down, b_query, b_value, b_out, b_up, b_down, gain_one, shift_one, gain_two, shift_two = params
    normed = low(layer_norm(row_input, gain_one, shift_one))
    queries = low(low_back(matmul(normed, w_query) + b_query)).reshape(LENGTH, HEADS, HEAD_DIM)
    keys_all = low(low_back(matmul(normed, w_key))).reshape(LENGTH, HEADS, HEAD_DIM)
    values_all = low(low_back(matmul(normed, w_value) + b_value)).reshape(LENGTH, HEADS, HEAD_DIM)
    block_rows = min(512, LENGTH)
    block_count = LENGTH // block_rows

    def attend(query_block, query_seg):
        scores = jnp.einsum('qhe,khe->hqk', query_block, keys_all, precision=HIGHEST) * HEAD_DIM ** (-0.5)
        scores = low_back(scores)
        allowed = query_seg[None, :, None] == seg_index[None, None, :]
        probs = jax.nn.softmax(jnp.where(allowed, scores, MASKED), axis=-1)
        return jnp.einsum('hqk,khe->qhe', low(probs), values_all, precision=HIGHEST)
    checked = jax.checkpoint(attend)
    attended = lax.map(lambda blocks_in: checked(blocks_in[0], blocks_in[1]), (queries.reshape(block_count, block_rows, HEADS, HEAD_DIM), seg_index.reshape(block_count, block_rows)))
    attended = low(low_back(attended.reshape(LENGTH, D)))
    mid_stream = row_input + low_back(matmul(attended, w_out) + b_out)
    normed_two = low(layer_norm(mid_stream, gain_two, shift_two))
    hidden_pre = low_back(matmul(normed_two, w_up) + b_up)
    hidden = low(jax.nn.gelu(hidden_pre, approximate=True))
    return mid_stream + matmul(hidden, w_down) + b_down

def reference(tokens, grad_out, crop, offsets, w_query, w_key, w_value, w_out, w_up, w_down, b_query, b_value, b_out, b_up, b_down, gain_one, shift_one, gain_two, shift_two):
    params = tuple((item.astype(jnp.float32) for item in (w_query, w_key, w_value, w_out, w_up, w_down, b_query, b_value, b_out, b_up, b_down, gain_one, shift_one, gain_two, shift_two)))
    positions = jnp.arange(LENGTH, dtype=jnp.int32)

    def per_row(totals, items):
        row_input, row_grad, row_crop, row_offsets = items
        seg_index = segment_row(positions, row_offsets, row_crop)
        result, backward = jax.vjp(lambda xin, pin: forward(xin, pin, seg_index), row_input.astype(jnp.float32), params)
        input_part, param_part = backward(row_grad.astype(jnp.float32))
        totals = tuple((left + right for left, right in zip(totals, param_part)))
        return (totals, (result.astype(jnp.bfloat16), input_part.astype(jnp.bfloat16)))
    start = tuple((jnp.zeros_like(item) for item in params))
    totals, (results, input_grads) = lax.scan(per_row, start, (tokens, grad_out, crop, offsets))
    return (results, input_grads, totals[0], totals[1], totals[2], totals[3], totals[4], totals[5], totals[6], totals[7], totals[8], totals[9], totals[10], totals[11], totals[12], totals[13], totals[14])
```

```python
import functools

import jax
import jax.numpy as jnp
from jax import lax
from jax.experimental import pallas as pl
from jax.experimental.pallas import tpu as pltpu
from jax.sharding import PartitionSpec as P

HEADS = 8
EPSILON = 1e-06
MASKED = -1e30
VMEM_LIMIT = 56 * 1024 * 1024
PIECES = 16
BF16 = jnp.bfloat16
F32 = jnp.float32
GELU_C = 0.7978845608028654
GELU_A = 0.044715


def nn(a, b):
    return jnp.dot(a, b, preferred_element_type=F32)


def nt(a, b):
    return lax.dot_general(a, b, (((1,), (1,)), ((), ())), preferred_element_type=F32)


def tn(a, b):
    return lax.dot_general(a, b, (((0,), (0,)), ((), ())), preferred_element_type=F32)


def normalize(values):
    center = values - jnp.mean(values, axis=-1, keepdims=True)
    scale = lax.rsqrt(jnp.mean(center * center, axis=-1, keepdims=True) + EPSILON)
    return center * scale, scale


def norm_back(cotangent, unit, scale, gain):
    g = cotangent * gain
    return scale * (
        g
        - jnp.mean(g, axis=-1, keepdims=True)
        - unit * jnp.mean(g * unit, axis=-1, keepdims=True)
    )


def segments(pos, sp, layout, row):
    seg = jnp.zeros(pos.shape, jnp.int32)
    for j in range(layout.segs):
        seg += (pos >= sp[layout.offsets + row * layout.segs + j]).astype(jnp.int32)
    return seg + layout.segs * (pos >= sp[layout.crop + row]).astype(jnp.int32)


class Layout:
    def __init__(self, stations, rows, segs):
        self.core, self.other, self.ids = 0, 1, 2
        self.station = 5
        self.offsets = self.station + stations
        self.crop = self.offsets + rows * segs
        self.segs = segs


def positions(sp, layout, chunk, tok, shape, dim):
    start = sp[layout.station + chunk] * (2 * tok)
    i = lax.broadcasted_iota(jnp.int32, shape, dim)
    mine = start + sp[layout.core] * tok
    other = start + sp[layout.other] * tok - tok
    return i + jnp.where(i < tok, mine, other)


def chunk_kernel(layout, chunk, first, last, tok, rows, *refs):
    refs = list(refs)
    sp = refs.pop(0)
    xm, xo, gain, shift, wk, wv, bv = refs[:7]
    refs = refs[7:]
    if first:
        wq, bq = refs[:2]
        refs = refs[2:]
    else:
        qm_in, m_in, l_in, acc_in = refs[:4]
        refs = refs[4:]
    k_out, v_out, kt_out, nt_out, unit_out = refs[:5]
    refs = refs[5:]
    if first:
        qm_out = refs.pop(0)
    if last:
        lse_out, ot_out, att_m, att_o = refs[:4]
        refs = refs[4:]
        m_ref, l_ref, acc_ref = refs
    else:
        m_out, l_out, acc_out = refs
    half = wk.shape[1]
    heads = HEADS // 2
    size = half // heads
    chip = 2 * tok
    for at, x in ((0, xm), (tok, xo)):
        values = x[...].reshape(rows * tok, -1).astype(F32)
        unit, _ = normalize(values)
        normed = (unit * gain[...] + shift[...]).astype(BF16)
        k = nn(normed, wk[...]).astype(BF16)
        v = (nn(normed, wv[...]) + bv[...]).astype(BF16)
        if first:
            q = ((nn(normed, wq[...]) + bq[...]).astype(BF16).astype(F32) * size**-0.5).astype(BF16)
            lane = lax.broadcasted_iota(jnp.int32, (tok, 2 * size), 1)
        for r in range(rows):
            part = slice(r * tok, (r + 1) * tok)
            k_out[0, r, at : at + tok, :] = k[part]
            v_out[0, r, at : at + tok, :] = v[part]
            kt_out[0, r, :, at : at + tok] = k[part].astype(F32).T.astype(BF16)
            nt_out[0, r, :, at : at + tok] = normed[part].astype(F32).T.astype(BF16)
            unit_out[0, r, at : at + tok, :] = unit[part].astype(BF16)
            if first:
                for h in range(heads):
                    pair = q[part, (h // 2) * 2 * size : (h // 2 + 1) * 2 * size]
                    keep = (lane >= size) if h % 2 else (lane < size)
                    qm_out[r * heads + h, at : at + tok, :] = jnp.where(keep, pair, jnp.zeros_like(pair))
    qm = qm_out if first else qm_in
    for r in range(rows):
        key_seg = segments(positions(sp, layout, chunk, tok, (chip, chip), 0), sp, layout, r)
        query_seg = segments(positions(sp, layout, 0, tok, (1, chip), 1), sp, layout, r)
        bias = jnp.where(key_seg == query_seg, 0.0, MASKED)
        for h in range(heads):
            lanes = slice((h // 2) * 2 * size, (h // 2 + 1) * 2 * size)
            at = r * heads + h
            s = nt(k_out[0, r, :, lanes], qm[at]) + bias
            top = jnp.max(s, axis=0, keepdims=True)
            if not first:
                old = m_in[at]
                top = jnp.maximum(old, top)
            p = jnp.exp(s - top)
            total = jnp.sum(p, axis=0, keepdims=True)
            added = tn(v_out[0, r, :, lanes], p.astype(BF16))
            added = added[(h % 2) * size : (h % 2 + 1) * size]
            if not first:
                keep = jnp.exp(old - top)
                total += l_in[at] * keep
                added += acc_in[at] * keep
            if last:
                m_ref[at] = top
                l_ref[at] = total
                acc_ref[at] = added
            else:
                m_out[at] = top
                l_out[at] = total
                acc_out[at] = added
        if last:
            parts = []
            for h in range(heads):
                at = r * heads + h
                lse_out[at] = m_ref[at] + jnp.log(l_ref[at])
                out = acc_ref[at] / l_ref[at]
                ot_out[at] = out
                parts.append(out)
            att = jnp.concatenate(parts, axis=0).T.astype(BF16)
            att_m[r] = att[:tok]
            att_o[r] = att[tok:]


def ffn_kernel(
    sp, att_m, att_o, wo_m, wo_o, tokens, cot, up_m, up_o, down_m, down_o, b_out, bup_m, bup_o,
    b_down, gain, shift, out, hid_m, hid_o, pre_m, pre_o, normed_out, mid_grad, branch, vec
):
    rows, tok, width = tokens.shape
    flat = rows * tok
    x = tokens[...].reshape(flat, width).astype(F32)
    mid = (
        x
        + nn(att_m[...].reshape(flat, -1), wo_m[...])
        + nn(att_o[...].reshape(flat, -1), wo_o[...])
        + b_out[...]
    )
    unit, scale = normalize(mid)
    normed = (unit * gain[...] + shift[...]).astype(BF16)
    normed_out[...] = normed
    g = cot[...].reshape(flat, width)
    total = jnp.zeros((flat, width), F32)
    back = jnp.zeros((flat, width), F32)
    block = 512
    for which, (up, down, bup, hid, pre) in enumerate(
        ((up_m, down_m, bup_m, hid_m, pre_m), (up_o, down_o, bup_o, hid_o, pre_o))
    ):
        for j in range(up.shape[1] // block):
            cols = slice(j * block, (j + 1) * block)
            u = nn(normed, up[:, cols]) + bup[:, cols]
            square = u * u
            t = jnp.tanh(GELU_C * u * (1.0 + GELU_A * square))
            hidden = (0.5 * u * (1.0 + t)).astype(BF16)
            slope = 0.5 * (1.0 + t) + 0.5 * GELU_C * u * (1.0 - t * t) * (1.0 + 3 * GELU_A * square)
            pg = (nt(g, down[cols, :]) * slope).astype(BF16)
            hid[:, cols] = hidden
            pre[:, cols] = pg
            total += nn(hidden, down[cols, :])
            back += nt(pg, up[:, cols])
            n = up.shape[1] // block
            base = sp[1 if which else 0] * n
            vec[pl.ds(base + j, 1), :] = jnp.sum(pg.astype(F32), axis=0, keepdims=True)
    out[...] = (mid + total + b_down[...]).astype(BF16).reshape(rows, tok, width)
    gf = g.astype(F32)
    grad = gf + norm_back(back, unit, scale, gain[...])
    mid_grad[...] = grad
    low = grad.astype(BF16)
    branch[...] = low.reshape(rows, tok, width)
    vec[4:5, :] = jnp.sum(gf, axis=0, keepdims=True)
    vec[5:6, :] = jnp.sum(back * unit, axis=0, keepdims=True)
    vec[6:7, :] = jnp.sum(back, axis=0, keepdims=True)
    vec[7:8, :] = jnp.sum(low.astype(F32), axis=0, keepdims=True)


def ffn_grad_kernel(sp, hid_m, hid_r, g_m, g_o, n_m, n_o, pre_m, pre_r, down, up):
    gd = tn(hid_m[...], g_m[...]) + tn(hid_r[...], g_o[...])
    gu = tn(n_m[...], pre_m[...]) + tn(n_o[...], pre_r[...])
    rd = gd.shape[0] // PIECES
    ru = gu.shape[0] // PIECES
    for p in range(PIECES):
        down[p ^ sp[2]] = gd[p * rd : (p + 1) * rd].astype(BF16)
        up[p ^ sp[3]] = gu[p * ru : (p + 1) * ru].astype(BF16)


def attend_back_kernel(
    layout, tok, rows, sp, br_m, br_o, wo, qm, lse, ot, wq, wk, wv, vec_in, k, v, kt, norm_t, unit,
    dn_m, dn_o, pieces, do, dm, delta, dqt, gk, gv, vec
):
    step = pl.program_id(0)
    steps = pl.num_programs(0)
    heads = HEADS // 2
    half = wq.shape[1]
    size = half // heads
    chip = 2 * tok
    width = wq.shape[0]
    chunk = lax.rem(step + 1, steps)

    @pl.when(step == 0)
    def _():
        dqt[...] = jnp.zeros_like(dqt)
        gk[...] = jnp.zeros_like(gk)
        gv[...] = jnp.zeros_like(gv)
        vec[...] = jnp.zeros_like(vec)
        lane = lax.broadcasted_iota(jnp.int32, (tok, 2 * size), 1)
        for r in range(rows):
            for at, br in ((0, br_m), (tok, br_o)):
                low = nt(br[r], wo[...]).astype(BF16)
                do[r, at : at + tok, :] = low
                for h in range(heads):
                    pair = low[:, (h // 2) * 2 * size : (h // 2 + 1) * 2 * size]
                    keep = (lane >= size) if h % 2 else (lane < size)
                    dm[r * heads + h, at : at + tok, :] = jnp.where(keep, pair, jnp.zeros_like(pair))
            dot = do[r].astype(F32).T
            for h in range(heads):
                at = r * heads + h
                delta[at] = jnp.sum(ot[at] * dot[h * size : (h + 1) * size], axis=0, keepdims=True)

    for r in range(rows):
        key_seg = segments(positions(sp, layout, chunk, tok, (chip, chip), 0), sp, layout, r)
        query_seg = segments(positions(sp, layout, 0, tok, (1, chip), 1), sp, layout, r)
        bias = jnp.where(key_seg == query_seg, 0.0, MASKED)
        dks, dvs = [], []
        for pair in range(heads // 2):
            lanes = slice(pair * 2 * size, (pair + 1) * 2 * size)
            dk = dv = None
            for h in (2 * pair, 2 * pair + 1):
                at = r * heads + h
                p = jnp.exp(nt(k[0, r, :, lanes], qm[at]) + bias - lse[at])
                dp = nt(v[0, r, :, lanes], dm[at])
                ds = (p * (dp - delta[at])).astype(BF16)
                p = p.astype(BF16)
                dv_h, dk_h = nn(p, dm[at]), nn(ds, qm[at])
                dv = dv_h if dv is None else dv + dv_h
                dk = dk_h if dk is None else dk + dk_h
                dqt[r, h * size : (h + 1) * size, :] += nn(kt[0, r, h * size : (h + 1) * size, :], ds)
            dks.append(dk.astype(BF16))
            dvs.append(dv.astype(BF16))
        dk = jnp.concatenate(dks, axis=1)
        dv = jnp.concatenate(dvs, axis=1)
        gk[...] += nn(norm_t[0, r], dk)
        gv[...] += nn(norm_t[0, r], dv)
        vec[1:2, :half] += jnp.sum(dv.astype(F32), axis=0, keepdims=True)
        dn = nt(dk, wk[...]) + nt(dv, wv[...])
        dn_m[0, r] = dn[:tok].astype(BF16)
        dn_o[0, r] = dn[tok:].astype(BF16)
        u = unit[0, r].astype(F32)
        vec[8:9, :] += jnp.sum(dn * u, axis=0, keepdims=True)
        vec[9:10, :] += jnp.sum(dn, axis=0, keepdims=True)

    @pl.when(step == steps - 1)
    def _():
        gq = jnp.zeros((width, half), F32)
        go = jnp.zeros((half, width), F32)
        for r in range(rows):
            dq = (dqt[r] * size**-0.5).T.astype(BF16)
            gq += nn(norm_t[0, r], dq)
            dn = nt(dq, wq[...])
            dn_m[0, r] = (dn_m[0, r].astype(F32) + dn[:tok]).astype(BF16)
            dn_o[0, r] = (dn_o[0, r].astype(F32) + dn[tok:]).astype(BF16)
            u = unit[0, r].astype(F32)
            vec[0:1, :half] += jnp.sum(dq.astype(F32), axis=0, keepdims=True)
            vec[8:9, :] += jnp.sum(dn * u, axis=0, keepdims=True)
            vec[9:10, :] += jnp.sum(dn, axis=0, keepdims=True)
            out_t = jnp.concatenate([ot[r * heads + h] for h in range(heads)], axis=0).astype(BF16)
            go += nn(out_t[:, :tok], br_m[r]) + nn(out_t[:, tok:], br_o[r])
        lane = lax.broadcasted_iota(jnp.int32, (2, width), 1)
        both = vec[0:2, :half]
        both = jnp.concatenate([both, both], axis=1)
        vec[0:2, :] = jnp.where((lane >= half) == (sp[layout.core] == 1), both, 0.0)
        vec[2:3, :] = vec_in[7:8, :]
        vec[3:4, :] = vec_in[4:5, :]
        vec[4:8, :] = vec_in[0:4, :]
        vec[10:12, :] = vec_in[5:7, :]
        n = width // PIECES
        low = n // 2
        for piece in range(PIECES):
            slot = piece ^ sp[4]
            part = slice(piece * n, (piece + 1) * n)
            pieces[slot, 0:n, :half] = gq[part].astype(BF16)
            pieces[slot, 0:n, half:] = gk[part].astype(BF16)
            pieces[slot, n : n + low, :half] = gv[part][:low].astype(BF16)
            pieces[slot, n : n + low, half:] = gv[part][low:].astype(BF16)
            pieces[slot, n + low : 2 * n, :] = go[piece * low : (piece + 1) * low].astype(BF16)
            row = vec[piece : piece + 1, :]
            pad = jnp.concatenate([row, jnp.zeros((15, width), F32)], axis=0)
            pieces[slot, 2 * n : 2 * n + 16, :] = pad.astype(BF16)


def last_kernel(tokens, gain, mid_grad, own, arrived, out):
    rows, tok, width = tokens.shape
    flat = rows * tok
    unit, scale = normalize(tokens[...].reshape(flat, width).astype(F32))
    dn = own[...].astype(F32) + arrived[...].astype(F32)
    grad = mid_grad[...] + norm_back(dn.reshape(flat, width), unit, scale, gain[...])
    out[...] = grad.astype(BF16).reshape(rows, tok, width)


def unpack_ffn_kernel(sp, d_m, d_o, u_m, u_o, down, up):
    rd, ru, cols = d_m.shape[1], u_m.shape[1], u_m.shape[2]
    for p in range(PIECES):
        for which, d, u in ((0, d_m, u_m), (1, d_o, u_o)):
            c = sp[which]
            down[pl.ds(c * (PIECES * rd) + p * rd, rd), :] = d[p ^ sp[2]].astype(F32)
            up[p * ru : (p + 1) * ru, pl.ds(pl.multiple_of(c * cols, 128), cols)] = u[p ^ sp[3]].astype(F32)


def unpack_attend_kernel(sp, a_m, a_o, gq, gk, gv, go, vec):
    width = gq.shape[0]
    half = width // 2
    n = width // PIECES
    low = n // 2
    for p in range(PIECES):
        row = jnp.zeros((1, width), F32)
        for which, a in ((0, a_m), (1, a_o)):
            c = sp[which]
            slot = p ^ sp[4]
            cols = pl.ds(pl.multiple_of(c * half, 128), half)
            gq[p * n : (p + 1) * n, cols] = a[slot, 0:n, :half].astype(F32)
            gk[p * n : (p + 1) * n, cols] = a[slot, 0:n, half:].astype(F32)
            gv[p * n : p * n + low, cols] = a[slot, n : n + low, :half].astype(F32)
            gv[p * n + low : (p + 1) * n, cols] = a[slot, n : n + low, half:].astype(F32)
            go[pl.ds(c * half + p * low, low), :] = a[slot, n + low : 2 * n, :].astype(F32)
            row += a[slot, 2 * n : 2 * n + 16, :].astype(F32)[0:1]
        vec[p : p + 1, :] = row


def whole(shape):
    zeros = (0,) * len(shape)
    return pl.BlockSpec(shape, lambda *_: zeros)


def half_cols(shape, which):
    return pl.BlockSpec((shape[0], shape[1] // 2), lambda i, sp: (0, sp[which]))


def half_rows(shape, which):
    return pl.BlockSpec((shape[0] // 2, shape[1]), lambda i, sp: (sp[which], 0))


def call(kernel, sp, ins, outs, scratch=(), grid=(1,), flops=0, moved=0, name=None):
    return pl.pallas_call(
        kernel,
        grid_spec=pltpu.PrefetchScalarGridSpec(
            num_scalar_prefetch=1,
            grid=grid,
            in_specs=[spec for _, spec in ins],
            out_specs=[spec for _, spec in outs],
            scratch_shapes=list(scratch),
        ),
        out_shape=[shape for shape, _ in outs],
        compiler_params=pltpu.CompilerParams(vmem_limit_bytes=VMEM_LIMIT),
        cost_estimate=pl.CostEstimate(flops=flops, bytes_accessed=moved, transcendentals=0),
        name=name,
    )(sp, *[a for a, _ in ins])


def full(array):
    return (array, whole(array.shape))


def made(shape, dtype):
    return (jax.ShapeDtypeStruct(shape, dtype), whole(shape))


def exchange(array, axis, mask):
    count = lax.axis_size(axis)
    return lax.ppermute(array, axis, [(i, i ^ mask) for i in range(count)])


def ring_order(count):
    return list(range(0, count, 2)) + list(range(1, count, 2))[::-1]


def added(*parts):
    return sum(p.astype(F32) for p in parts).astype(BF16)


def reduce_pieces(buf, bits, rest):
    for axis, mask in bits:
        half = buf.shape[0] // 2
        buf = added(buf[:half], exchange(buf[half:], axis, mask))
    for axis, mask in rest:
        buf = added(buf, exchange(buf, axis, mask))
    return buf


def spread_pieces(buf, bits):
    for axis, mask in reversed(bits):
        buf = jnp.concatenate([buf, exchange(buf, axis, mask)], axis=0)
    return buf


def my_id(bits):
    out = 0
    for axis, mask in bits:
        out = out * 2 + jnp.where((lax.axis_index(axis) & mask) != 0, 1, 0)
    return out


def body(
    tokens, grad_out, crop, offsets, w_query, w_key, w_value, w_out, w_up, w_down, b_query, b_value,
    b_out, b_up, b_down, gain_one, shift_one, gain_two, shift_two,
):
    rows, tok, width = tokens.shape
    seq_count, dp_count = lax.axis_size("seq"), lax.axis_size("dp")
    stations = seq_count // 2
    hidden = w_up.shape[1]
    half = width // 2
    heads = HEADS // 2
    chip = 2 * tok
    flat = rows * tok
    segs = offsets.shape[1]
    layout = Layout(stations, rows, segs)
    seq = lax.axis_index("seq")
    core, station = seq % 2, seq // 2

    order = ring_order(stations)
    place = {s: i for i, s in enumerate(order)}
    table = jnp.array(
        [[order[(place[s] - j) % stations] for j in range(stations)] for s in range(stations)], jnp.int32
    )
    ring = []
    for i, s in enumerate(order):
        after = order[(i + 1) % stations]
        ring += [(2 * s + c, 2 * after + c) for c in range(2)]

    dp_bits = [("dp", 1 << i) for i in range(dp_count.bit_length() - 1)]
    st_bits = [("seq", 2 << i) for i in range(stations.bit_length() - 1)]
    chosen = (dp_bits[:2] + st_bits[:2])[: PIECES.bit_length() - 1]
    rest = dp_bits[2:] + st_bits[2:]
    swapped = [chosen[1], chosen[0]] + chosen[2:]
    bits = (chosen, swapped, chosen)

    sp = jnp.concatenate(
        [
            jnp.stack([core, 1 - core] + [my_id(b) for b in bits]).astype(jnp.int32),
            lax.dynamic_slice(table, (station, 0), (1, stations))[0],
            offsets.reshape(-1),
            crop,
        ]
    )
    line = lambda v: v.reshape(1, -1)

    block = tokens
    k_parts, state = [], None
    keys, values, keys_t, norm_t, units = [], [], [], [], []
    for j in range(stations):
        if j:
            block = lax.ppermute(block, "seq", ring)
        other = exchange(block, "seq", 1)
        first, last = j == 0, j == stations - 1
        ins = [full(block), full(other), full(line(gain_one)), full(line(shift_one))]
        ins += [(w_key, half_cols(w_key.shape, 0)), (w_value, half_cols(w_value.shape, 0))]
        ins += [(line(b_value), half_cols((1, width), 0))]
        if first:
            ins += [(w_query, half_cols(w_query.shape, 0)), (line(b_query), half_cols((1, width), 0))]
        else:
            ins += [full(a) for a in state]
        outs = [
            made((1, rows, chip, half), BF16),
            made((1, rows, chip, half), BF16),
            made((1, rows, half, chip), BF16),
            made((1, rows, width, chip), BF16),
            made((1, rows, chip, width), BF16),
        ]
        if first:
            outs += [made((rows * heads, chip, 2 * half // heads), BF16)]
        stat = made((rows * heads, 1, chip), F32)
        acc = made((rows * heads, half // heads, chip), F32)
        scratch = []
        if last:
            outs += [stat, acc, made((rows, tok, half), BF16), made((rows, tok, half), BF16)]
            scratch = [pltpu.VMEM(s.shape, F32) for s in (stat[0], stat[0], acc[0])]
        else:
            outs += [stat, stat, acc]
        got = call(
            functools.partial(chunk_kernel, layout, j, first, last, tok, rows),
            sp, ins, outs, scratch, flops=6 * 10**8, moved=4 * 10**6, name=f"attend_chunk_{j}",
        )
        for where, array in zip((keys, values, keys_t, norm_t, units), got[:5]):
            where.append(array)
        got = got[5:]
        if first:
            query, got = got[0], got[1:]
        if not last:
            state = [query] + list(got)
    lse, out_t, att_m, att_o = got
    att_r = exchange(att_o, "seq", 1)
    g_other = exchange(grad_out, "seq", 1)

    res = call(
        ffn_kernel, sp,
        [
            full(att_m), full(att_r),
            (w_out, half_rows(w_out.shape, 0)), (w_out, half_rows(w_out.shape, 1)),
            full(tokens), full(grad_out),
            (w_up, half_cols(w_up.shape, 0)), (w_up, half_cols(w_up.shape, 1)),
            (w_down, half_rows(w_down.shape, 0)), (w_down, half_rows(w_down.shape, 1)),
            full(line(b_out)),
            (line(b_up), half_cols((1, hidden), 0)), (line(b_up), half_cols((1, hidden), 1)),
            full(line(b_down)), full(line(gain_two)), full(line(shift_two)),
        ],
        [made((rows, tok, width), BF16)]
        + [made((flat, hidden // 2), BF16)] * 4
        + [made((flat, width), BF16), made((flat, width), F32), made((rows, tok, width), BF16), made((8, width), F32)],
        flops=4 * 10**9, moved=10**7, name="feed_forward",
    )
    outputs, hid_m, hid_o, pre_m, pre_o, normed_two, mid_grad, branch, vec_ffn = res
    branch_r = exchange(branch, "seq", 1)
    hid_r = exchange(hid_o, "seq", 1)
    pre_r = exchange(pre_o, "seq", 1)
    normed_two_r = exchange(normed_two, "seq", 1)

    down, up = call(
        ffn_grad_kernel, sp,
        [
            full(hid_m), full(hid_r), full(grad_out.reshape(flat, width)), full(g_other.reshape(flat, width)),
            full(normed_two), full(normed_two_r), full(pre_m), full(pre_r),
        ],
        [
            made((PIECES, hidden // 2 // PIECES, width), BF16),
            made((PIECES, width // PIECES, hidden // 2), BF16),
        ],
        flops=16 * 10**8, moved=5 * 10**6, name="feed_forward_grad",
    )

    joined = lambda parts: jnp.concatenate(parts, axis=0)
    k_all, v_all, kt_all, nt_all, unit_all = map(joined, (keys, values, keys_t, norm_t, units))

    def per_chunk(array):
        shape = (1,) + array.shape[1:]
        return (array, pl.BlockSpec(shape, lambda i, sp: (lax.rem(i + 1, stations), 0, 0, 0)))

    dn_shape = jax.ShapeDtypeStruct((stations, rows, tok, width), BF16)
    dn_m, dn_o, pieces = call(
        functools.partial(attend_back_kernel, layout, tok, rows), sp,
        [
            full(branch), full(branch_r), (w_out, half_rows(w_out.shape, 0)), full(query), full(lse), full(out_t),
            (w_query, half_cols(w_query.shape, 0)), (w_key, half_cols(w_key.shape, 0)),
            (w_value, half_cols(w_value.shape, 0)), full(vec_ffn),
        ]
        + [per_chunk(a) for a in (k_all, v_all, kt_all, nt_all, unit_all)],
        [per_chunk(dn_shape), per_chunk(dn_shape), made((PIECES, 2 * width // PIECES + 16, width), BF16)],
        scratch=[
            pltpu.VMEM((rows, chip, half), BF16),
            pltpu.VMEM((rows * heads, chip, 2 * half // heads), BF16),
            pltpu.VMEM((rows * heads, 1, chip), F32),
            pltpu.VMEM((rows, half, chip), F32),
            pltpu.VMEM((width, half), F32),
            pltpu.VMEM((width, half), F32),
            pltpu.VMEM((16, width), F32),
        ],
        grid=(stations,), flops=8 * 10**9, moved=10**7, name="attend_back",
    )

    arrived = None
    for j in range(1, stations):
        part = [dn_m[j], exchange(dn_o[j], "seq", 1)]
        if arrived is not None:
            part.append(arrived)
        arrived = lax.ppermute(added(*part), "seq", ring)
    own = added(dn_m[0], exchange(dn_o[0], "seq", 1))

    def reduced(buf, which):
        buf = spread_pieces(reduce_pieces(buf, bits[which], rest), bits[which])
        return buf, exchange(buf, "seq", 1)

    down_m, down_o = reduced(down, 0)
    up_m, up_o = reduced(up, 1)
    att_pieces, att_other = reduced(pieces, 2)

    if arrived is None:
        arrived = jnp.zeros_like(own)
    input_grad = pl.pallas_call(
        last_kernel,
        out_shape=jax.ShapeDtypeStruct((rows, tok, width), BF16),
        compiler_params=pltpu.CompilerParams(vmem_limit_bytes=VMEM_LIMIT),
        name="input_grad",
    )(tokens, line(gain_one), mid_grad, own, arrived)

    grad_down, grad_up = call(
        unpack_ffn_kernel, sp,
        [full(down_m), full(down_o), full(up_m), full(up_o)],
        [made((hidden, width), F32), made((width, hidden), F32)],
        name="unpack_feed_forward",
    )
    square = made((width, width), F32)
    grad_query, grad_key, grad_value, grad_out_proj, vec = call(
        unpack_attend_kernel, sp,
        [full(att_pieces), full(att_other)],
        [square, square, square, square, made((PIECES, width), F32)],
        name="unpack_attend",
    )
    return (
        outputs, input_grad, grad_query, grad_key, grad_value, grad_out_proj, grad_up, grad_down,
        vec[0], vec[1], vec[2], vec[4:8].reshape(-1), vec[3], vec[8], vec[9], vec[10], vec[11],
    )


def solution(mesh):
    split, row, copied = P("dp", "seq", None), P("dp"), P()
    return jax.shard_map(
        body,
        mesh=mesh,
        in_specs=(split, split, row, P("dp", None)) + (copied,) * 15,
        out_specs=(split, split) + (copied,) * 15,
        check_vma=False,
    )
```

```python
import functools

import jax
import jax.numpy as jnp
from jax import lax
from jax.experimental import pallas as pl
from jax.experimental.pallas import tpu as pltpu
from jax.sharding import PartitionSpec as P

HEADS = 8
EPSILON = 1e-06
MASKED = -1e30
MIB = 1024 * 1024
LIMITS = (16, 20, 20, 26, 20)
PIECES = 16
GROUP = 4
BACK_US = 0.05
BF16 = jnp.bfloat16
F32 = jnp.float32
GELU_C = 0.7978845608028654
GELU_A = 0.044715


def nn(a, b):
    return jnp.dot(a, b, preferred_element_type=F32)


def nt(a, b):
    return lax.dot_general(a, b, (((1,), (1,)), ((), ())), preferred_element_type=F32)


def tn(a, b):
    return lax.dot_general(a, b, (((0,), (0,)), ((), ())), preferred_element_type=F32)


def normalize(values):
    center = values - jnp.mean(values, axis=-1, keepdims=True)
    scale = lax.rsqrt(jnp.mean(center * center, axis=-1, keepdims=True) + EPSILON)
    return center * scale, scale


def norm_back(cotangent, unit, scale, gain):
    g = cotangent * gain
    return scale * (
        g
        - jnp.mean(g, axis=-1, keepdims=True)
        - unit * jnp.mean(g * unit, axis=-1, keepdims=True)
    )


def segments(pos, offsets, crop, row):
    count = offsets.shape[1]
    seg = jnp.zeros(pos.shape, jnp.int32)
    for j in range(count):
        seg += (pos >= offsets[row, j]).astype(jnp.int32)
    return seg + count * (pos >= crop[row]).astype(jnp.int32)


def ring_station(place, count):
    return jnp.where(place < count // 2, 2 * place, 2 * (count - 1 - place) + 1)


def ring_place(station, count):
    return jnp.where(station % 2 == 0, station // 2, count - 1 - station // 2)


def positions(sp, stations, chunk, tok, shape, dim):
    place = lax.rem(ring_place(sp[4], stations) + stations - chunk, stations)
    start = ring_station(place, stations) * (2 * tok)
    i = lax.broadcasted_iota(jnp.int32, shape, dim)
    return i + jnp.where(i < tok, start + sp[0] * tok, start + sp[1] * tok - tok)


def half_of(which, width):
    return pl.ds(pl.multiple_of(which * width, 128), width)


def padded(lines):
    return jnp.concatenate(lines + [jnp.zeros((16 - len(lines), lines[0].shape[1]), F32)], axis=0)


def load_kernel(halved, sp, *refs):
    count = len(halved)
    sources, targets, sems = refs[:count], refs[count : 2 * count], refs[2 * count :]
    copies = []
    for half, source, target, sem in zip(halved, sources, targets, sems):
        if half:
            source = source.at[:, half_of(sp[0], source.shape[1] // 2)]
        copies.append(pltpu.make_async_copy(source, target, sem))
    for copy in copies:
        copy.start()
    for copy in copies:
        copy.wait()


def chunk_kernel(stations, chunk, tok, rows, *refs):
    refs = list(refs)
    first, last = chunk == 0, chunk == stations - 1
    sp, offsets, crop, xm, xo, vectors, weights = refs[:7]
    refs = refs[7:]
    if not first:
        qm_in, m_in, l_in, acc_in = refs[:4]
        refs = refs[4:]
    k_out, v_out, kt_out, nt_out = refs[:4]
    refs = refs[4:]
    if first:
        qm_out = refs.pop(0)
    if last:
        lse_out, ot_out, att_m, att_o = refs[:4]
    else:
        m_out, l_out, acc_out = refs
    half = weights.shape[2]
    heads = HEADS // 2
    size = half // heads
    chip = 2 * tok
    for at, x in ((0, xm), (tok, xo)):
        values = x[...].reshape(rows * tok, -1).astype(F32)
        unit, _ = normalize(values)
        normed = unit * vectors[0:1, :] + vectors[1:2, :]
        low = normed.astype(BF16)
        k = nn(low, weights[1])
        v = (nn(low, weights[2]) + vectors[3:4, :half]).astype(BF16)
        if first:
            q = ((nn(low, weights[0]) + vectors[2:3, :half]).astype(BF16).astype(F32) * size**-0.5).astype(BF16)
            lane = lax.broadcasted_iota(jnp.int32, (tok, 2 * size), 1)
        for r in range(rows):
            part = slice(r * tok, (r + 1) * tok)
            k_out[r, at : at + tok, :] = k[part].astype(BF16)
            v_out[r, at : at + tok, :] = v[part]
            kt_out[r, :, at : at + tok] = k[part].T.astype(BF16)
            nt_out[r, :, at : at + tok] = normed[part].T.astype(BF16)
            if first:
                for h in range(heads):
                    pair = q[part, (h // 2) * 2 * size : (h // 2 + 1) * 2 * size]
                    keep = (lane >= size) if h % 2 else (lane < size)
                    qm_out[r * heads + h, at : at + tok, :] = jnp.where(keep, pair, jnp.zeros_like(pair))
    qm = qm_out if first else qm_in
    for r in range(rows):
        key_seg = segments(positions(sp, stations, chunk, tok, (chip, chip), 0), offsets, crop, r)
        query_seg = segments(positions(sp, stations, 0, tok, (1, chip), 1), offsets, crop, r)
        bias = jnp.where(key_seg == query_seg, 0.0, MASKED)
        outs = []
        for h in range(heads):
            lanes = slice((h // 2) * 2 * size, (h // 2 + 1) * 2 * size)
            at = r * heads + h
            s = nt(k_out[r, :, lanes], qm[at]) + bias
            top = jnp.max(s, axis=0, keepdims=True)
            if not first:
                old = m_in[at]
                top = jnp.maximum(old, top)
            p = jnp.exp(s - top)
            total = jnp.sum(p, axis=0, keepdims=True)
            added = tn(v_out[r, :, lanes], p.astype(BF16))
            added = added[(h % 2) * size : (h % 2 + 1) * size]
            if not first:
                keep = jnp.exp(old - top)
                total += l_in[at] * keep
                added += acc_in[at] * keep
            if last:
                lse_out[at] = top + jnp.log(total)
                out = added / total
                ot_out[at] = out
                outs.append(out)
            else:
                m_out[at] = top
                l_out[at] = total
                acc_out[at] = added
        if last:
            att = jnp.concatenate(outs, axis=0).T.astype(BF16)
            att_m[r] = att[:tok]
            att_o[r] = att[tok:]


def feed_forward_block(normed, g, up, down, bup, cols):
    u = nn(normed, up[:, cols]) + bup[:, cols]
    square = u * u
    t = jnp.tanh(GELU_C * u * (1.0 + GELU_A * square))
    hidden = (0.5 * u * (1.0 + t)).astype(BF16)
    slope = 0.5 * (1.0 + t) + 0.5 * GELU_C * u * (1.0 - t * t) * (1.0 + 3 * GELU_A * square)
    pre = (nt(g, down[cols, :]) * slope).astype(BF16)
    return hidden, pre, nn(hidden, down[cols, :]), nt(pre, up[:, cols])


def feed_forward_half(sp, which, normed, g, up, down, bup, hid, pre, at, vec, total, back):
    half = up.shape[1] // 2
    block = min(512, half)
    for j in range(half // block):
        cols = pl.ds(pl.multiple_of(sp[which] * half + j * block, 128), block)
        hidden, grad, more, less = feed_forward_block(normed, g, up, down, bup, cols)
        hid[:, j * block : (j + 1) * block] = hidden
        pre[:, at + j * block : at + (j + 1) * block] = grad
        total = more if total is None else total + more
        back = less if back is None else back + less
        row = jnp.sum(grad.astype(F32), axis=0, keepdims=True)
        vec[pl.ds(sp[which] * (half // block) + j, 1), :] = row
    return total, back


def ffn_first_kernel(
    sp, att_m, att_o, wo, tokens, cot, up, down, b_out, bup, gain, shift, mid_out, normed_out, send, total_out, back_out, vec
):
    rows, tok, width = tokens.shape
    flat = rows * tok
    quarter = width // 2
    mine = pl.ds(pl.multiple_of(sp[0] * quarter, 128), quarter)
    other = pl.ds(pl.multiple_of(sp[1] * quarter, 128), quarter)
    mid = (
        tokens[...].reshape(flat, width).astype(F32)
        + nn(att_m[...].reshape(flat, -1), wo[mine, :])
        + nn(att_o[...].reshape(flat, -1), wo[other, :])
        + b_out[...]
    )
    mid_out[...] = mid
    unit, _ = normalize(mid)
    normed = (unit * gain[...] + shift[...]).astype(BF16)
    normed_out[...] = normed
    half = up.shape[1] // 2
    send[:, 2 * half :] = normed
    vec[...] = jnp.zeros_like(vec)
    g = cot[...].reshape(flat, width)
    total_out[...], back_out[...] = feed_forward_half(
        sp, 1, normed, g, up, down, bup, send, send, half, vec, None, None
    )


def ffn_second_kernel(
    sp, mid_in, normed_in, cot, up, down, bup, b_down, gain, total_in, back_in, vec_in, out, hid, pre, mid_grad, branch, vec
):
    rows, tok, width = cot.shape
    flat = rows * tok
    g = cot[...].reshape(flat, width)
    vec[...] = vec_in[...]
    total, back = feed_forward_half(
        sp, 0, normed_in[...], g, up, down, bup, hid, pre, 0, vec, total_in[...], back_in[...]
    )
    mid = mid_in[...]
    out[...] = (mid + total + b_down[...]).astype(BF16).reshape(rows, tok, width)
    unit, scale = normalize(mid)
    gf = g.astype(F32)
    grad = gf + norm_back(back, unit, scale, gain[...])
    mid_grad[...] = grad
    low = grad.astype(BF16)
    branch[...] = low.reshape(rows, tok, width)
    vec[4:5, :] = jnp.sum(gf, axis=0, keepdims=True)
    vec[5:6, :] = jnp.sum(back * unit, axis=0, keepdims=True)
    vec[6:7, :] = jnp.sum(back, axis=0, keepdims=True)
    vec[7:8, :] = jnp.sum(low.astype(F32), axis=0, keepdims=True)


def ffn_grad_kernel(sp, hid_m, pre_m, n_m, got, g_m, g_o, d_keep, d_send, u_keep, u_send, gd, gu):
    half = hid_m.shape[1]
    gd[...] = tn(hid_m[...], g_m[...]) + tn(got[:, :half], g_o[...])
    gu[...] = tn(n_m[...], pre_m[...]) + tn(got[:, 2 * half :], got[:, half : 2 * half])
    rd = gd.shape[0] // PIECES
    ru = gu.shape[0] // PIECES
    width = gd.shape[1]
    for slot in range(PIECES):
        d, u = (d_keep, u_keep) if slot < PIECES // 2 else (d_send, u_send)
        at = slot % (PIECES // 2)
        d[at] = gd[pl.ds(pl.multiple_of((sp[2] ^ slot) * rd, rd), rd), :].astype(BF16)
        rows = pl.ds(pl.multiple_of((sp[3] ^ slot) * ru, ru), ru)
        for i in range(half // width):
            u[at, i * ru : (i + 1) * ru, :] = gu[rows, i * width : (i + 1) * width].astype(BF16)


def attend_back_kernel(stations, tok, row, whole, last, *refs):
    refs = list(refs)

    def take(count):
        got = refs[:count]
        del refs[:count]
        return got

    sp, offsets, crop, br_m, br_o, wo, qm, lse, ot, weights = take(10)
    k, v, kt, norm_t = (take(stations) for _ in range(4))
    sums_in = take(5) if row else None
    if last:
        vectors, vec_in = take(2)
    dn_m, dn_o = take(2)
    gq, gk, gv, go, sums = take(5)
    at = row if whole else 0
    heads = HEADS // 2
    _, width, half = weights.shape
    size = half // heads
    chip = 2 * tok
    block = min(4, stations)
    blocks = stations // block

    branch = jnp.concatenate([br_m[at], br_o[at]], axis=0)
    do = nt(branch, wo[half_of(sp[0], half), :])
    dot = do.T
    do = do.astype(BF16)
    lane = lax.broadcasted_iota(jnp.int32, (chip, 2 * size), 1)
    head_at = at * heads
    out_t = jnp.concatenate([ot[head_at + h] for h in range(heads)], axis=0).astype(BF16)
    go_row = nn(out_t, branch)
    query_seg = segments(positions(sp, stations, 0, tok, (1, chip), 1), offsets, crop, row)
    biases = []
    for chunk in range(stations):
        key_seg = segments(positions(sp, stations, chunk, tok, (chip, chip), 0), offsets, crop, row)
        biases.append(jnp.where(key_seg == query_seg, 0.0, MASKED))
    dqt = []
    dks = [[] for _ in range(blocks)]
    dvs = [[] for _ in range(blocks)]
    for pair in range(heads // 2):
        lanes = slice(pair * 2 * size, (pair + 1) * 2 * size)
        dk = [None] * blocks
        dv = [None] * blocks
        for h in (2 * pair, 2 * pair + 1):
            wide = do[:, lanes]
            dm = jnp.where((lane >= size) if h % 2 else (lane < size), wide, jnp.zeros_like(wide))
            delta = jnp.sum(ot[head_at + h] * dot[h * size : (h + 1) * size], axis=0, keepdims=True)
            dq = None
            for b in range(blocks):
                chunks = range(b * block, (b + 1) * block)
                keys = jnp.concatenate([k[c][at, :, lanes] for c in chunks], axis=0)
                values = jnp.concatenate([v[c][at, :, lanes] for c in chunks], axis=0)
                keys_t = jnp.concatenate([kt[c][at, h * size : (h + 1) * size, :] for c in chunks], axis=1)
                bias = jnp.concatenate([biases[c] for c in chunks], axis=0)
                p = jnp.exp(nt(keys, qm[head_at + h]) + bias - lse[head_at + h])
                ds = (p * (nt(values, dm) - delta)).astype(BF16)
                dv_h, dk_h = nn(p.astype(BF16), dm), nn(ds, qm[head_at + h])
                dv[b] = dv_h if dv[b] is None else dv[b] + dv_h
                dk[b] = dk_h if dk[b] is None else dk[b] + dk_h
                more = nn(keys_t, ds)
                dq = more if dq is None else dq + more
            dqt.append(dq)
        for b in range(blocks):
            dks[b].append(dk[b].astype(BF16))
            dvs[b].append(dv[b].astype(BF16))
    dq = (jnp.concatenate(dqt, axis=0) * size**-0.5).T.astype(BF16)
    gq_row = nn(norm_t[0][at], dq)
    gk_row = gv_row = sum_k = sum_v = 0.0
    for b in range(blocks):
        dk = jnp.concatenate(dks[b], axis=1)
        dv = jnp.concatenate(dvs[b], axis=1)
        normed = jnp.concatenate([norm_t[c][at] for c in range(b * block, (b + 1) * block)], axis=1)
        gk_row += nn(normed, dk)
        gv_row += nn(normed, dv)
        sum_k += jnp.sum(dk.astype(F32), axis=0, keepdims=True)
        sum_v += jnp.sum(dv.astype(F32), axis=0, keepdims=True)
        dn = nt(dk, weights[1]) + nt(dv, weights[2])
        for i in range(block):
            part = dn[i * chip : (i + 1) * chip]
            if b + i == 0:
                part += nt(dq, weights[0])
            dn_m[b * block + i] = part[:tok].astype(BF16)
            dn_o[b * block + i] = part[tok:].astype(BF16)
    sum_q = jnp.sum(dq.astype(F32), axis=0, keepdims=True)
    made_here = (gq_row, gk_row, gv_row, go_row, jnp.concatenate([sum_q, sum_v, sum_k, jnp.zeros((5, half), F32)]))
    for i, (ref, value) in enumerate(zip((gq, gk, gv, go, sums), made_here)):
        ref[...] = value if sums_in is None else value + sums_in[i][...]
    if not last:
        return

    ones, twos = take(2), take(2)
    vec = refs[0]
    lane = lax.broadcasted_iota(jnp.int32, (2, width), 1)
    both = sums[0:2, :]
    both = jnp.concatenate([both, both], axis=1)
    vec[0:2, :] = jnp.where((lane >= half) == (sp[0] == 1), both, 0.0)
    vec[2:3, :] = vec_in[7:8, :]
    vec[3:4, :] = vec_in[4:5, :]
    vec[4:8, :] = vec_in[0:4, :]
    vec[10:12, :] = vec_in[5:7, :]
    vec[12:16, :] = jnp.zeros((4, width), F32)
    wide = [weights[i].astype(F32) for i in range(3)]
    shifts = sum(w * sums[i : i + 1, :] for w, i in zip(wide, (0, 2, 1)))
    gains = sum(w * g[...] for w, g in zip(wide, (gq, gk, gv)))

    def across(values):
        folded = sum(values[:, i * 128 : (i + 1) * 128] for i in range(half // 128))
        return jnp.sum(folded.T, axis=0, keepdims=True)

    shift_grad = across(shifts)
    vec[9:10, :] = shift_grad
    vec[8:9, :] = (across(gains) - vectors[1:2, :] * shift_grad) / vectors[0:1, :]
    n = width // PIECES
    low = n // 2
    per = PIECES // 2
    for slot in range(PIECES):
        one, two = ones[slot // per], twos[slot // per]
        base = slot % per * n
        piece = sp[2] ^ slot
        part = pl.ds(pl.multiple_of(piece * n, n), n)
        one[base : base + n, :half] = gq[part, :].astype(BF16)
        one[base : base + n, half:] = gk[part, :].astype(BF16)
        piece = sp[3] ^ slot
        first = pl.ds(pl.multiple_of(piece * n, n), low)
        second = pl.ds(pl.multiple_of(piece * n + low, low), low)
        two[base : base + low, :half] = gv[first, :].astype(BF16)
        two[base : base + low, half:] = gv[second, :].astype(BF16)
        two[base + low : base + n, :] = go[pl.ds(pl.multiple_of(piece * low, low), low), :].astype(BF16)
    for i, two in enumerate(twos):
        lines = [vec[pl.ds(sp[3] ^ (i * per + s), 1), :] for s in range(per)]
        two[per * n :, :] = padded(lines).astype(BF16)


def last_kernel(tokens, gain, mid_grad, *refs):
    out = refs[-1]
    rows, tok, width = tokens.shape
    flat = rows * tok
    unit, scale = normalize(tokens[...].reshape(flat, width).astype(F32))
    arrived = refs[-2][...].astype(F32).reshape(flat, width)
    parts = [refs[2 * r][0].astype(F32) + refs[2 * r + 1][0].astype(F32) for r in range(rows)]
    dn = jnp.concatenate(parts, axis=0) + arrived
    grad = mid_grad[...] + norm_back(dn, unit, scale, gain[0:1, :])
    out[...] = grad.astype(BF16).reshape(rows, tok, width)


def unpack_ffn_kernel(sp, *refs):
    refs = list(refs)
    up, down = refs[-2:]
    d_mine, d_other, u_mine, u_other = refs[0:2], refs[2:4], refs[4:6], refs[6:8]
    half, rd, width = d_mine[0].shape
    ru = up.shape[0] // PIECES
    hidden = down.shape[0]
    for slot in range(PIECES):
        at = slot % half
        for which, d, u in ((0, d_mine, u_mine), (1, d_other, u_other)):
            c = sp[which]
            rows = pl.ds(pl.multiple_of(c * (hidden // 2) + (sp[2] ^ slot) * rd, rd), rd)
            down[rows, :] = d[slot // half][at].astype(F32)
            rows = pl.ds(pl.multiple_of((sp[3] ^ slot) * ru, ru), ru)
            for i in range(rd // ru):
                cols = pl.ds(pl.multiple_of(c * (hidden // 2) + i * width, 128), width)
                up[rows, cols] = u[slot // half][at, i * ru : (i + 1) * ru, :].astype(F32)


def unpack_attend_kernel(sp, *refs):
    gq, gk, gv, go, vec = refs[-5:]
    ones, twos = (refs[0:2], refs[2:4]), (refs[4:6], refs[6:8])
    width = gq.shape[0]
    half = width // 2
    n = width // PIECES
    low = n // 2
    per = PIECES // 2
    for slot in range(PIECES):
        base = slot % per * n
        for which in range(2):
            one, two = ones[which][slot // per], twos[which][slot // per]
            cols = half_of(sp[which], half)
            piece = sp[2] ^ slot
            rows = pl.ds(pl.multiple_of(piece * n, n), n)
            gq[rows, cols] = one[base : base + n, :half].astype(F32)
            gk[rows, cols] = one[base : base + n, half:].astype(F32)
            piece = sp[3] ^ slot
            first = pl.ds(pl.multiple_of(piece * n, n), low)
            second = pl.ds(pl.multiple_of(piece * n + low, low), low)
            gv[first, cols] = two[base : base + low, :half].astype(F32)
            gv[second, cols] = two[base : base + low, half:].astype(F32)
            out_rows = pl.ds(pl.multiple_of(sp[which] * half + piece * low, low), low)
            go[out_rows, :] = two[base + low : base + n, :].astype(F32)
    for side in range(2):
        both = twos[0][side][per * n :, :].astype(F32) + twos[1][side][per * n :, :].astype(F32)
        for s in range(per):
            vec[pl.ds(sp[3] ^ (side * per + s), 1), :] = both[s : s + 1]


def total(*values):
    return sum(v.astype(F32) for v in values).astype(BF16)


def sum_kernel(*refs):
    refs[-1][...] = total(*[r[...] for r in refs[:-1]])


def upper_kernel(*refs):
    count = len(refs) // 3
    for i, out in enumerate(refs[2 * count :]):
        keep, got = refs[2 * i : 2 * i + 2]
        half = keep.shape[0] // 2
        out[...] = total(keep[half:], got[half:])


def quarter_kernel(d_keep, d_got, d_last, u_keep, u_got, u_last, keep, send):
    rd = d_keep.shape[1]
    half = keep.shape[0]
    for i in range(2 * half):
        out = send if i >= half else keep
        out[i % half, :rd] = total(d_keep[i], d_got[i], d_last[i])
        out[i % half, rd:] = total(u_keep[i], u_got[i], u_last[i])


def halve_kernel(keep, got, out_keep, out_send):
    out_keep[...] = total(keep[0], got[0])
    out_send[...] = total(keep[1], got[1])


def pair_kernel(one, two, out):
    out[0] = one[...]
    out[1] = two[...]


def divide_kernel(one, two, d, u):
    rd = d.shape[1]
    for i in range(d.shape[0]):
        part = (one if i < 2 else two)[i % 2]
        d[i] = part[:rd]
        u[i] = part[rd:]


def join_kernel(*refs):
    count = len(refs) // 3
    for i, out in enumerate(refs[2 * count :]):
        one, two = refs[2 * i : 2 * i + 2]
        out[: one.shape[0]] = one[...]
        out[one.shape[0] :] = two[...]


def attend_upper_kernel(one_keep, one_got, two_keep, two_got, one, two):
    n = one.shape[0]
    one[...] = total(one_keep[n:], one_got[n:])
    two[:n] = total(two_keep[n : 2 * n], two_got[n : 2 * n])
    lines = total(two_keep[2 * n :], two_got[2 * n :]).astype(F32)
    two[n:] = fill(lines[4:8])


def fill(lines):
    return jnp.concatenate([lines, jnp.zeros((16 - lines.shape[0], lines.shape[1]), F32)], axis=0).astype(BF16)


def attend_quarter_kernel(one_keep, one_got, one_last, two_keep, two_got, two_last, keep, send):
    count = 2 * keep.shape[0]
    n = one_last.shape[0] // count
    lines = total(two_keep[2 * count * n :], two_got[2 * count * n :], two_last[count * n :]).astype(F32)
    for i in range(count):
        out = (keep, send)[i // 2]
        part = slice(i * n, (i + 1) * n)
        out[i % 2, :n] = total(one_keep[part], one_got[part], one_last[part])
        out[i % 2, n : 2 * n] = total(two_keep[part], two_got[part], two_last[part])
        out[i % 2, 2 * n :] = jnp.broadcast_to(lines[i : i + 1], (16, lines.shape[1])).astype(BF16)


def attend_divide_kernel(first, second, one, two):
    n = one.shape[0] // 4
    lines = []
    for i in range(4):
        part = (first if i < 2 else second)[i % 2]
        one[i * n : (i + 1) * n] = part[:n]
        two[i * n : (i + 1) * n] = part[n : 2 * n]
        lines.append(part[2 * n :].astype(F32)[:1])
    two[4 * n :] = padded(lines).astype(BF16)


def attend_join_kernel(one_a, one_b, two_a, two_b, one, two):
    n = one_a.shape[0]
    one[:n] = one_a[...]
    one[n:] = one_b[...]
    two[:n] = two_a[:n]
    two[n : 2 * n] = two_b[:n]
    lines = jnp.concatenate([two_a[n:].astype(F32)[:4], two_b[n:].astype(F32)[:4]], axis=0)
    two[2 * n :] = fill(lines)


def norm_grad_kernel(chunk, rows, *refs):
    out = refs[-1]
    for r in range(rows):
        values = [refs[2 * r][chunk], refs[2 * r + 1][chunk]]
        if len(refs) > 2 * rows + 1:
            values.append(refs[2 * rows][r])
        out[r] = total(*values)


VMEM = pl.BlockSpec(memory_space=pltpu.VMEM)
SMEM = pl.BlockSpec(memory_space=pltpu.SMEM)
HBM = pl.BlockSpec(memory_space=pltpu.HBM)


def call(kernel, ins, outs, scratch=(), us=1.0, limit=16, name=None, scalars=1, specs=None, grid=()):
    return pl.pallas_call(
        kernel,
        grid=grid,
        in_specs=[SMEM] * scalars + (specs or [VMEM] * (len(ins) - scalars)),
        out_specs=[VMEM] * len(outs),
        out_shape=list(outs),
        scratch_shapes=list(scratch),
        compiler_params=pltpu.CompilerParams(vmem_limit_bytes=limit * MIB),
        cost_estimate=pl.CostEstimate(flops=int(us * 1.1e9), bytes_accessed=0, transcendentals=0),
        name=name,
    )(*ins)


def load(sp, arrays, halved, name, limit=16):
    shapes = [a.shape[:-1] + (a.shape[-1] // (2 if h else 1),) for a, h in zip(arrays, halved)]
    return call(
        functools.partial(load_kernel, halved), [sp] + arrays, [made(s, a.dtype) for s, a in zip(shapes, arrays)],
        scratch=[pltpu.SemaphoreType.DMA] * len(arrays), us=2.0, limit=limit, name=name, specs=[HBM] * len(arrays),
    )


def made(shape, dtype):
    return jax.ShapeDtypeStruct(shape, dtype)


def exchange(array, axis, mask):
    count = lax.axis_size(axis)
    return lax.ppermute(array, axis, [(i, i ^ mask) for i in range(count)])


def merge(kernel, ins, outs, name):
    return call(kernel, list(ins), list(outs), us=0.05, limit=8, name=name, scalars=0)


def tied(*arrays):
    return lax.optimization_barrier(arrays)


class Chain:
    def __init__(self):
        self.token = None

    def __call__(self, function, ins, *args, **kwargs):
        at = next(i for i, a in enumerate(ins) if a.ndim > 1 and a.dtype != jnp.int32)
        ins = list(ins)
        if self.token is not None:
            ins[at], _ = tied(ins[at], self.token)
        outs = list(function(ins, *args, **kwargs))
        self.token = outs[-1]
        return outs


def my_id(bits):
    out = 0
    for axis, mask in bits:
        out = out * 2 + jnp.where((lax.axis_index(axis) & mask) != 0, 1, 0)
    return out


def body(
    tokens, grad_out, crop, offsets, w_query, w_key, w_value, w_out, w_up, w_down, b_query, b_value,
    b_out, b_up, b_down, gain_one, shift_one, gain_two, shift_two,
):
    rows, tok, width = tokens.shape
    seq_count, dp_count = lax.axis_size("seq"), lax.axis_size("dp")
    stations = seq_count // 2
    hidden = w_up.shape[1]
    half = width // 2
    heads = HEADS // 2
    size = half // heads
    chip = 2 * tok
    flat = rows * tok
    small = stations <= 4
    seq = lax.axis_index("seq")
    core, station = seq % 2, seq // 2
    line = lambda v: v.reshape(1, -1)

    order = list(range(0, stations, 2)) + list(range(1, stations, 2))[::-1]
    ring = []
    for i, s in enumerate(order):
        after = order[(i + 1) % stations]
        ring += [(2 * s + c, 2 * after + c) for c in range(2)]

    dp_bits = [("dp", 1 << i) for i in range(dp_count.bit_length() - 1)]
    st_bits = [("seq", 2 << i) for i in range(stations.bit_length() - 1)]
    bit_x, bit_y = dp_bits[:2]
    rest = dp_bits[2:] + st_bits[2:]
    ids = [my_id([bit_x, bit_y] + st_bits[:2]), my_id([bit_y, bit_x] + st_bits[:2])]
    sp = jnp.stack([core, 1 - core, *ids, station]).astype(jnp.int32)

    mine = lambda a: lax.dynamic_slice_in_dim(a, core * half, half, a.ndim - 1)
    weights = jnp.stack([mine(w_query), mine(w_key), mine(w_value)])
    pad = lambda a: jnp.pad(mine(a), (0, half))
    vectors = jnp.stack([gain_one, shift_one, pad(b_query), pad(b_value)] + [jnp.zeros_like(gain_one)] * 4)
    state = []
    kept = [[], [], [], []]
    for j in range(stations):
        if j:
            block = lax.ppermute(block if j > 1 else tokens, "seq", ring)
            block, *state = tied(block, *state)
        else:
            block = tokens
        other = exchange(block, "seq", 1)
        first, last = j == 0, j == stations - 1
        ins = [sp, offsets, crop, block, other, vectors, weights] + ([] if first else state)
        outs = [
            made((rows, chip, half), BF16),
            made((rows, chip, half), BF16),
            made((rows, half, chip), BF16),
            made((rows, width, chip), BF16),
        ]
        if first:
            outs += [made((rows * heads, chip, 2 * size), BF16)]
        stat = made((rows * heads, 1, chip), F32)
        acc = made((rows * heads, size, chip), F32)
        if last:
            outs += [stat, acc, made((rows, tok, half), BF16), made((rows, tok, half), BF16)]
        else:
            outs += [stat, stat, acc]
        got = call(
            functools.partial(chunk_kernel, stations, j, tok, rows), ins, outs,
            us=5.0, limit=LIMITS[0], name=f"attend_chunk_{j}", scalars=3,
        )
        for where, array in zip(kept, got[:4]):
            where.append(array)
        got = got[4:]
        if first:
            query, got = got[0], got[1:]
        if not last:
            state = [query] + list(got)
        if j == min(1, stations - 1):
            sp_b, state[0] = tied(sp, state[0])
            tokens_v, g_v, wo, up, down, bo, bu, bd, gain_b, shift_b = load(
                sp_b,
                [tokens, grad_out, w_out, w_up, w_down, line(b_out), line(b_up), line(b_down), line(gain_two), line(shift_two)],
                [False] * 10, "load_feed_forward",
            )
            state[0], up = tied(state[0], up)
    lse, out_t, att_m, att_o = got
    att_r = exchange(att_o, "seq", 1)
    g_other = exchange(grad_out, "seq", 1).reshape(flat, width)

    wide = made((flat, width), F32)
    vec8 = made((8, width), F32)
    mid, normed_two, send, total, back, vec_a = call(
        ffn_first_kernel, [sp, att_m, att_r, wo, tokens_v, g_v, up, down, bo, bu, gain_b, shift_b],
        [wide, made((flat, width), BF16), made((flat, hidden + width), BF16), wide, wide, vec8],
        us=4.0, limit=LIMITS[1], name="feed_forward_a",
    )
    got = exchange(send, "seq", 1)
    outputs, hid_m, pre_m, mid_grad, branch, vec_ffn = call(
        ffn_second_kernel, [sp, mid, normed_two, g_v, up, down, bu, bd, gain_b, total, back, vec_a],
        [made((rows, tok, width), BF16), made((flat, hidden // 2), BF16), made((flat, hidden // 2), BF16), wide,
         made((rows, tok, width), BF16), vec8],
        us=4.0, limit=LIMITS[1], name="feed_forward_b",
    )
    branch_r = exchange(branch, "seq", 1)
    piece = made((PIECES // 2, hidden // 2 // PIECES, width), BF16)
    d_keep, d_send, u_keep, u_send = call(
        ffn_grad_kernel, [sp, hid_m, pre_m, normed_two, got, g_v.reshape(flat, width), g_other],
        [piece, piece, piece, piece],
        scratch=[pltpu.VMEM((hidden // 2, width), F32), pltpu.VMEM((width, hidden // 2), F32)],
        us=3.0, limit=LIMITS[2], name="feed_forward_grad",
    )
    branch, d_send, u_send = tied(branch, d_send, u_send)

    q = PIECES // GROUP
    d_got, u_got = exchange(d_send, *bit_x), exchange(u_send, *bit_y)

    sums = []
    chain = Chain()
    dn_m, dn_o = [], []
    for r in range(rows):
        last = r == rows - 1
        arrays = [branch, branch_r, wo, query, lse, out_t, weights] + [a for part in kept for a in part]
        specs = [VMEM] * len(arrays)
        if not small:
            for i, a in enumerate(arrays):
                if a.ndim == 3 and a is not weights:
                    block_shape = (a.shape[0] // rows,) + a.shape[1:]
                    specs[i] = pl.BlockSpec(block_shape, functools.partial(lambda r, i: (r, 0, 0), r))
        tail = list(sums)
        if last:
            tail += [vectors, vec_ffn]
        part = made((stations, tok, width), BF16)
        grads = [made((width, half), F32)] * 3 + [made((half, width), F32), made((8, half), F32)]
        outs = [part, part] + grads
        if last:
            outs += [made((width // 2, width), BF16)] * 2 + [made((width // 2 + 16, width), BF16)] * 2
        run = functools.partial(call, functools.partial(attend_back_kernel, stations, tok, r, small, last))
        res = chain(
            run, [sp, offsets, crop] + arrays + tail, outs, scratch=[pltpu.VMEM((16, width), F32)] if last else [],
            us=BACK_US, limit=LIMITS[3] if small else 48, name=f"attend_back_{r}", scalars=3,
            specs=specs + [VMEM] * len(tail), grid=() if small else (1,),
        )
        dn_m.append(res[0])
        dn_o.append(res[1])
        sums = list(res[2:7])
        if r == rows - 2:
            early = [exchange(a, "seq", 1) for a in dn_o[: min(1, r)]]
            sums[0], d_got, u_got, *early = tied(sums[0], d_got, u_got, *early)
            quarters = made((q,) + piece.shape[1:], BF16)
            chain.token = sums[0]
            d_next, u_next = chain(functools.partial(merge, upper_kernel), [d_keep, d_got, u_keep, u_got], [quarters, quarters], "add_quarters")
            d_got2, u_got2 = exchange(d_next, *bit_y), exchange(u_next, *bit_x)
    one_keep, one_send, two_keep, two_send = res[7:]

    rd = hidden // 2 // PIECES
    n = width // PIECES
    ff_part, at_part = made((2 * rd, width), BF16), made((2 * n + 16, width), BF16)
    two_of = lambda a: made((2,) + a.shape, BF16)
    token_block = made((rows, tok, width), BF16)
    bit_z, bit_w = st_bits[:2]

    def step(kernel, ins, outs, name):
        return chain(functools.partial(merge, kernel), ins, outs, name)

    def over_rest(part, name):
        for i, (where, mask) in enumerate(rest):
            part = step(sum_kernel, [part, exchange(part, where, mask)], [made(part.shape, BF16)], f"{name}_{i}")[0]
        return part

    one_got, two_got = exchange(one_send, *bit_x), exchange(two_send, *bit_y)
    dn_r = early + [exchange(a, "seq", 1) for a in dn_o[len(early) :]]
    pairs = [a for both in zip(dn_m, dn_r) for a in both]

    def norm_step(j, arrived):
        kernel = functools.partial(norm_grad_kernel, j, rows)
        part = step(kernel, pairs + arrived, [token_block], f"add_norm_grad_{j}")[0]
        return [lax.ppermute(part, "seq", ring)]

    a_keep, a_send = step(
        quarter_kernel, [d_keep, d_got, d_got2, u_keep, u_got, u_got2], [two_of(ff_part)] * 2, "add_pieces"
    )
    a_got = exchange(a_send, *bit_z)
    arrived = norm_step(1, [])
    one_next, two_next = step(
        attend_upper_kernel, [one_keep, one_got, two_keep, two_got],
        [made((4 * n, width), BF16), made((4 * n + 16, width), BF16)], "add_attend_quarters",
    )
    one_got2, two_got2 = exchange(one_next, *bit_y), exchange(two_next, *bit_x)
    a_keep, a_send = step(halve_kernel, [a_keep, a_got], [ff_part] * 2, "add_halves")
    a_got = exchange(a_send, *bit_w)
    b_keep, b_send = step(
        attend_quarter_kernel, [one_keep, one_got, one_got2, two_keep, two_got, two_got2],
        [two_of(at_part)] * 2, "add_attend_pieces",
    )
    b_got = exchange(b_send, *bit_z)
    a_own = over_rest(step(sum_kernel, [a_keep, a_got], [ff_part], "add_last")[0], "add_rest")
    a_near = exchange(a_own, *bit_w)
    if stations > 2:
        arrived = norm_step(2, arrived)
    b_keep, b_send = step(halve_kernel, [b_keep, b_got], [at_part] * 2, "add_attend_halves")
    b_got = exchange(b_send, *bit_w)
    a_pair = step(pair_kernel, [a_own, a_near], [two_of(ff_part)], "pair")[0]
    a_far = exchange(a_pair, *bit_z)
    b_own = over_rest(step(sum_kernel, [b_keep, b_got], [at_part], "add_attend_last")[0], "add_attend_rest")
    b_near = exchange(b_own, *bit_w)
    d_mine, u_mine = step(divide_kernel, [a_pair, a_far], [quarters, quarters], "divide_pieces")
    d_y, u_x = exchange(d_mine, *bit_y), exchange(u_mine, *bit_x)
    b_pair = step(pair_kernel, [b_own, b_near], [two_of(at_part)], "attend_pair")[0]
    b_far = exchange(b_pair, *bit_z)
    for j in range(3, stations):
        arrived = norm_step(j, arrived)
    d_near, u_near = step(join_kernel, [d_mine, d_y, u_mine, u_x], [piece, piece], "join_pieces")
    d_far, u_far = exchange(d_near, *bit_x), exchange(u_near, *bit_y)
    one_mine, two_mine = step(
        attend_divide_kernel, [b_pair, b_far],
        [made((4 * n, width), BF16), made((4 * n + 16, width), BF16)], "divide_attend_pieces",
    )
    one_y, two_x = exchange(one_mine, *bit_y), exchange(two_mine, *bit_x)
    one_near, two_near = step(
        attend_join_kernel, [one_mine, one_y, two_mine, two_x],
        [made((8 * n, width), BF16), made((8 * n + 16, width), BF16)], "join_attend_pieces",
    )
    one_far, two_far = exchange(one_near, *bit_x), exchange(two_near, *bit_y)
    d_all = [d_near, d_far, exchange(d_near, "seq", 1), exchange(d_far, "seq", 1)]
    u_all = [u_near, u_far, exchange(u_near, "seq", 1), exchange(u_far, "seq", 1)]
    run = functools.partial(call, last_kernel)
    input_grad = chain(
        run, [tokens_v, vectors, mid_grad] + pairs + arrived, [token_block], us=0.1, limit=LIMITS[4], name="input_grad", scalars=0
    )[0]
    run = functools.partial(call, unpack_ffn_kernel)
    grad_up, grad_down = chain(
        run, [sp] + d_all + u_all, [made((width, hidden), F32), made((hidden, width), F32)],
        us=0.1, limit=LIMITS[4], name="unpack_feed_forward",
    )
    one_all = [one_near, one_far, exchange(one_near, "seq", 1), exchange(one_far, "seq", 1)]
    two_all = [two_near, two_far, exchange(two_near, "seq", 1), exchange(two_far, "seq", 1)]
    square = made((width, width), F32)
    run = functools.partial(call, unpack_attend_kernel)
    grad_query, grad_key, grad_value, grad_out_proj, vec = chain(
        run, [sp] + one_all + two_all, [square, square, square, square, made((PIECES, width), F32)],
        us=0.1, limit=LIMITS[4], name="unpack_attend",
    )

    return (
        outputs, input_grad, grad_query, grad_key, grad_value, grad_out_proj, grad_up, grad_down,
        vec[0], vec[1], vec[2], vec[4:8].reshape(-1), vec[3], vec[8], vec[9], vec[10], vec[11],
    )


def solution(mesh):
    split, row, copied = P("dp", "seq", None), P("dp"), P()
    return jax.shard_map(
        body,
        mesh=mesh,
        in_specs=(split, split, row, P("dp", None)) + (copied,) * 15,
        out_specs=(split, split) + (copied,) * 15,
        check_vma=False,
    )
```

```python
import functools

import jax
import jax.numpy as jnp
from jax import lax
from jax.experimental import pallas as pl
from jax.experimental.pallas import tpu as pltpu
from jax.sharding import PartitionSpec as P

HEADS = 8
EPSILON = 1e-06
MASKED = -1e30
MIB = 1024 * 1024
LIMITS = (16, 20, 20, 26, 20)
PIECES = 16
GROUP = 4
BACK_US = 0.05
BF16 = jnp.bfloat16
F32 = jnp.float32
GELU_C = 0.7978845608028654
GELU_A = 0.044715


def nn(a, b):
    return jnp.dot(a, b, preferred_element_type=F32)


def nt(a, b):
    return lax.dot_general(a, b, (((1,), (1,)), ((), ())), preferred_element_type=F32)


def tn(a, b):
    return lax.dot_general(a, b, (((0,), (0,)), ((), ())), preferred_element_type=F32)


def normalize(values):
    center = values - jnp.mean(values, axis=-1, keepdims=True)
    scale = lax.rsqrt(jnp.mean(center * center, axis=-1, keepdims=True) + EPSILON)
    return center * scale, scale


def norm_back(cotangent, unit, scale, gain):
    g = cotangent * gain
    return scale * (
        g
        - jnp.mean(g, axis=-1, keepdims=True)
        - unit * jnp.mean(g * unit, axis=-1, keepdims=True)
    )


def segments(pos, offsets, crop, row):
    count = offsets.shape[1]
    seg = jnp.zeros(pos.shape, jnp.int32)
    for j in range(count):
        seg += (pos >= offsets[row, j]).astype(jnp.int32)
    return seg + count * (pos >= crop[row]).astype(jnp.int32)


def ring_station(place, count):
    return jnp.where(place < count // 2, 2 * place, 2 * (count - 1 - place) + 1)


def ring_place(station, count):
    return jnp.where(station % 2 == 0, station // 2, count - 1 - station // 2)


def positions(sp, chunk, tok, shape, dim):
    start = (sp[4] ^ chunk) * (2 * tok)
    i = lax.broadcasted_iota(jnp.int32, shape, dim)
    return i + jnp.where(i < tok, start + sp[0] * tok, start + sp[1] * tok - tok)


def half_of(which, width):
    return pl.ds(pl.multiple_of(which * width, 128), width)


def padded(lines):
    return jnp.concatenate(lines + [jnp.zeros((16 - len(lines), lines[0].shape[1]), F32)], axis=0)


def load_kernel(halved, sp, *refs):
    count = len(halved)
    sources, targets, sems = refs[:count], refs[count : 2 * count], refs[2 * count :]
    copies = []
    for half, source, target, sem in zip(halved, sources, targets, sems):
        if half:
            source = source.at[:, half_of(sp[0], source.shape[1] // 2)]
        copies.append(pltpu.make_async_copy(source, target, sem))
    for copy in copies:
        copy.start()
    for copy in copies:
        copy.wait()


def chunk_kernel(chunk, last, tok, rows, *refs):
    refs = list(refs)
    first = chunk == 0
    sp, offsets, crop, xm, xo, vectors, weights = refs[:7]
    refs = refs[7:]
    if not first:
        qm_in, m_in, l_in, acc_in = refs[:4]
        refs = refs[4:]
    k_out, v_out, kt_out, nt_out = refs[:4]
    refs = refs[4:]
    if first:
        qm_out = refs.pop(0)
    if last:
        lse_out, ot_out, att_m, att_o = refs[:4]
    else:
        m_out, l_out, acc_out = refs
    half = weights.shape[2]
    heads = HEADS // 2
    size = half // heads
    chip = 2 * tok
    for at, x in ((0, xm), (tok, xo)):
        values = x[...].reshape(rows * tok, -1).astype(F32)
        unit, _ = normalize(values)
        normed = unit * vectors[0:1, :] + vectors[1:2, :]
        low = normed.astype(BF16)
        k = nn(low, weights[1])
        v = (nn(low, weights[2]) + vectors[3:4, half_of(sp[0], half)]).astype(BF16)
        if first:
            q = ((nn(low, weights[0]) + vectors[2:3, half_of(sp[0], half)]).astype(BF16).astype(F32) * size**-0.5).astype(BF16)
            lane = lax.broadcasted_iota(jnp.int32, (tok, 2 * size), 1)
        for r in range(rows):
            part = slice(r * tok, (r + 1) * tok)
            k_out[r, at : at + tok, :] = k[part].astype(BF16)
            v_out[r, at : at + tok, :] = v[part]
            kt_out[r, :, at : at + tok] = k[part].T.astype(BF16)
            nt_out[r, :, at : at + tok] = normed[part].T.astype(BF16)
            if first:
                for h in range(heads):
                    pair = q[part, (h // 2) * 2 * size : (h // 2 + 1) * 2 * size]
                    keep = (lane >= size) if h % 2 else (lane < size)
                    qm_out[r * heads + h, at : at + tok, :] = jnp.where(keep, pair, jnp.zeros_like(pair))
    qm = qm_out if first else qm_in
    for r in range(rows):
        key_seg = segments(positions(sp, chunk, tok, (chip, chip), 0), offsets, crop, r)
        query_seg = segments(positions(sp, 0, tok, (1, chip), 1), offsets, crop, r)
        bias = jnp.where(key_seg == query_seg, 0.0, MASKED)
        outs = []
        spot = [r * heads + h for h in range(heads)]
        pairs = [slice((h // 2) * 2 * size, (h // 2 + 1) * 2 * size) for h in range(heads)]
        s = [nt(k_out[r, :, pairs[h]], qm[spot[h]]) + bias for h in range(heads)]
        tops = [jnp.max(a, axis=0, keepdims=True) for a in s]
        if not first:
            olds = [m_in[at] for at in spot]
            tops = [jnp.maximum(a, b) for a, b in zip(olds, tops)]
        p = [jnp.exp(a - b) for a, b in zip(s, tops)]
        totals = [jnp.sum(a, axis=0, keepdims=True) for a in p]
        addeds = [tn(v_out[r, :, pairs[h]], p[h].astype(BF16)) for h in range(heads)]
        for h, at in enumerate(spot):
            added = addeds[h][(h % 2) * size : (h % 2 + 1) * size]
            total = totals[h]
            if not first:
                keep = jnp.exp(olds[h] - tops[h])
                total += l_in[at] * keep
                added += acc_in[at] * keep
            if last:
                lse_out[at] = tops[h] + jnp.log(total)
                out = added / total
                ot_out[at] = out
                outs.append(out)
            else:
                m_out[at] = tops[h]
                l_out[at] = total
                acc_out[at] = added
        if last:
            att = jnp.concatenate(outs, axis=0).T.astype(BF16)
            att_m[r] = att[:tok]
            att_o[r] = att[tok:]


def feed_forward_half(sp, which, normed, g, up, down, bup, hid, pre, at, vec, total, back):
    half = up.shape[1] // 2
    row = min(512, half)
    block = min(512, row)
    count = half // block
    cols = [pl.ds(pl.multiple_of(sp[which] * half + j * block, 128), block) for j in range(count)]
    for first in range(0, count, 2):
        js = range(first, min(first + 2, count))
        us = [nn(normed, up[:, cols[j]]) + bup[:, cols[j]] for j in js]
        gs = [nt(g, down[cols[j], :]) for j in js]
        outs, pres = [], []
        for j, u, back_in in zip(js, us, gs):
            square = u * u
            plus = 1.0 + jnp.tanh(u * (GELU_C + GELU_C * GELU_A * square))
            low = 0.5 * u
            hidden = (low * plus).astype(BF16)
            slope = plus * (0.5 + low * (2.0 - plus) * (GELU_C + 3 * GELU_C * GELU_A * square))
            grad = (back_in * slope).astype(BF16)
            hid[:, j * block : (j + 1) * block] = hidden
            pre[:, at + j * block : at + (j + 1) * block] = grad
            outs.append(hidden)
            pres.append(grad)
            line = jnp.sum(grad.astype(F32), axis=0, keepdims=True)
            lane = j * block % row
            vec[pl.ds(sp[which] * (half // row) + j * block // row, 1), lane : lane + block] = line
        for j, hidden, grad in zip(js, outs, pres):
            more, less = nn(hidden, down[cols[j], :]), nt(grad, up[:, cols[j]])
            total = more if total is None else total + more
            back = less if back is None else back + less
    return total, back


def ffn_first_kernel(
    sp, att_m, att_o, wo, tokens, cot, up, down, b_out, bup, gain, shift, mid_out, normed_out, send, total_out, back_out, vec
):
    rows, tok, width = tokens.shape
    flat = rows * tok
    quarter = width // 2
    mine = pl.ds(pl.multiple_of(sp[0] * quarter, 128), quarter)
    other = pl.ds(pl.multiple_of(sp[1] * quarter, 128), quarter)
    mid = (
        tokens[...].reshape(flat, width).astype(F32)
        + nn(att_m[...].reshape(flat, -1), wo[mine, :])
        + nn(att_o[...].reshape(flat, -1), wo[other, :])
        + b_out[...]
    )
    mid_out[...] = mid
    unit, _ = normalize(mid)
    normed = (unit * gain[...] + shift[...]).astype(BF16)
    normed_out[...] = normed
    half = up.shape[1] // 2
    send[:, 2 * half :] = normed
    vec[...] = jnp.zeros_like(vec)
    g = cot[...].reshape(flat, width)
    total_out[...], back_out[...] = feed_forward_half(
        sp, 1, normed, g, up, down, bup, send, send, half, vec, None, None
    )


def ffn_second_kernel(
    sp, mid_in, normed_in, cot, up, down, bup, b_down, gain, total_in, back_in, vec_in, out, hid, pre, mid_grad, branch, vec
):
    rows, tok, width = cot.shape
    flat = rows * tok
    g = cot[...].reshape(flat, width)
    vec[...] = vec_in[...]
    total, back = feed_forward_half(
        sp, 0, normed_in[...], g, up, down, bup, hid, pre, 0, vec, total_in[...], back_in[...]
    )
    mid = mid_in[...]
    out[...] = (mid + total + b_down[...]).astype(BF16).reshape(rows, tok, width)
    unit, scale = normalize(mid)
    gf = g.astype(F32)
    grad = gf + norm_back(back, unit, scale, gain[...])
    mid_grad[...] = grad
    low = grad.astype(BF16)
    branch[...] = low.reshape(rows, tok, width)
    vec[4:5, :] = jnp.sum(gf, axis=0, keepdims=True)
    vec[5:6, :] = jnp.sum(back * unit, axis=0, keepdims=True)
    vec[6:7, :] = jnp.sum(back, axis=0, keepdims=True)
    vec[7:8, :] = jnp.sum(low.astype(F32), axis=0, keepdims=True)


def ffn_grad_kernel(sp, hid_m, pre_m, n_m, got, g_m, g_o, d_keep, d_send, u_keep, u_send, gd, gu):
    half = hid_m.shape[1]
    gd[...] = tn(hid_m[...], g_m[...]) + tn(got[:, :half], g_o[...])
    gu[...] = tn(n_m[...], pre_m[...]) + tn(got[:, 2 * half :], got[:, half : 2 * half])
    rd = gd.shape[0] // PIECES
    ru = gu.shape[0] // PIECES
    width = gd.shape[1]
    for slot in range(PIECES):
        d, u = (d_keep, u_keep) if slot < PIECES // 2 else (d_send, u_send)
        at = slot % (PIECES // 2)
        d[at] = gd[pl.ds(pl.multiple_of((sp[2] ^ slot) * rd, rd), rd), :].astype(BF16)
        rows = pl.ds(pl.multiple_of((sp[3] ^ slot) * ru, ru), ru)
        for i in range(half // width):
            u[at, i * ru : (i + 1) * ru, :] = gu[rows, i * width : (i + 1) * width].astype(BF16)


def attend_back_kernel(stations, tok, row, whole, last, *refs):
    refs = list(refs)

    def take(count):
        got = refs[:count]
        del refs[:count]
        return got

    sp, offsets, crop, br_m, br_o, wo, qm, lse, ot, weights = take(10)
    k, v, kt, norm_t = (take(stations) for _ in range(4))
    sums_in = take(5) if row else None
    if last:
        vectors, vec_in = take(2)
    dn_m, dn_o = take(2)
    if last:
        ones, twos = take(2), take(2)
    gq, gk, gv, go, sums = take(5)
    at = row if whole else 0
    heads = HEADS // 2
    _, width, half = weights.shape
    size = half // heads
    chip = 2 * tok
    block = min(4, stations)
    blocks = stations // block

    branch = jnp.concatenate([br_m[at], br_o[at]], axis=0)
    do = nt(branch, wo[half_of(sp[0], half), :])
    dot = do.T
    do = do.astype(BF16)
    lane = lax.broadcasted_iota(jnp.int32, (chip, 2 * size), 1)
    head_at = at * heads
    out_t = jnp.concatenate([ot[head_at + h] for h in range(heads)], axis=0).astype(BF16)
    go_row = nn(out_t, branch)
    query_seg = segments(positions(sp, 0, tok, (1, chip), 1), offsets, crop, row)
    biases = []
    for chunk in range(stations):
        key_seg = segments(positions(sp, chunk, tok, (chip, chip), 0), offsets, crop, row)
        biases.append(jnp.where(key_seg == query_seg, 0.0, MASKED))
    dqt = []
    dks = [[] for _ in range(blocks)]
    dvs = [[] for _ in range(blocks)]
    for pair in range(heads // 2):
        lanes = slice(pair * 2 * size, (pair + 1) * 2 * size)
        dk = [None] * blocks
        dv = [None] * blocks
        for h in (2 * pair, 2 * pair + 1):
            wide = do[:, lanes]
            dm = jnp.where((lane >= size) if h % 2 else (lane < size), wide, jnp.zeros_like(wide))
            delta = jnp.sum(ot[head_at + h] * dot[h * size : (h + 1) * size], axis=0, keepdims=True)
            dq = None
            for b in range(blocks):
                chunks = range(b * block, (b + 1) * block)
                keys = jnp.concatenate([k[c][at, :, lanes] for c in chunks], axis=0)
                values = jnp.concatenate([v[c][at, :, lanes] for c in chunks], axis=0)
                keys_t = jnp.concatenate([kt[c][at, h * size : (h + 1) * size, :] for c in chunks], axis=1)
                bias = jnp.concatenate([biases[c] for c in chunks], axis=0)
                p = jnp.exp(nt(keys, qm[head_at + h]) + bias - lse[head_at + h])
                ds = (p * (nt(values, dm) - delta)).astype(BF16)
                dv_h, dk_h = nn(p.astype(BF16), dm), nn(ds, qm[head_at + h])
                dv[b] = dv_h if dv[b] is None else dv[b] + dv_h
                dk[b] = dk_h if dk[b] is None else dk[b] + dk_h
                more = nn(keys_t, ds)
                dq = more if dq is None else dq + more
            dqt.append(dq)
        for b in range(blocks):
            dks[b].append(dk[b].astype(BF16))
            dvs[b].append(dv[b].astype(BF16))
    dq = (jnp.concatenate(dqt, axis=0) * size**-0.5).T.astype(BF16)
    gq_row = nn(norm_t[0][at], dq)
    gk_row = gv_row = sum_k = sum_v = 0.0
    for b in range(blocks):
        dk = jnp.concatenate(dks[b], axis=1)
        dv = jnp.concatenate(dvs[b], axis=1)
        normed = jnp.concatenate([norm_t[c][at] for c in range(b * block, (b + 1) * block)], axis=1)
        gk_row += nn(normed, dk)
        gv_row += nn(normed, dv)
        sum_k += jnp.sum(dk.astype(F32), axis=0, keepdims=True)
        sum_v += jnp.sum(dv.astype(F32), axis=0, keepdims=True)
        dn = nt(dk, weights[1]) + nt(dv, weights[2])
        for i in range(block):
            part = dn[i * chip : (i + 1) * chip]
            if b + i == 0:
                part += nt(dq, weights[0])
            dn_m[b * block + i] = part[:tok].astype(BF16)
            dn_o[b * block + i] = part[tok:].astype(BF16)
    sum_q = jnp.sum(dq.astype(F32), axis=0, keepdims=True)
    made_here = (gq_row, gk_row, gv_row, go_row, jnp.concatenate([sum_q, sum_v, sum_k, jnp.zeros((5, half), F32)]))
    for i, (ref, value) in enumerate(zip((gq, gk, gv, go, sums), made_here)):
        ref[...] = value if sums_in is None else value + sums_in[i][...]
    if not last:
        return

    vec = refs[0]
    lane = lax.broadcasted_iota(jnp.int32, (2, width), 1)
    both = sums[0:2, :]
    both = jnp.concatenate([both, both], axis=1)
    vec[0:2, :] = jnp.where((lane >= half) == (sp[0] == 1), both, 0.0)
    vec[2:3, :] = vec_in[7:8, :]
    vec[3:4, :] = vec_in[4:5, :]
    vec[4:8, :] = vec_in[0:4, :]
    vec[10:12, :] = vec_in[5:7, :]
    vec[12:16, :] = jnp.zeros((4, width), F32)
    wide = [weights[i].astype(F32) for i in range(3)]
    shifts = sum(w * sums[i : i + 1, :] for w, i in zip(wide, (0, 2, 1)))
    gains = sum(w * g[...] for w, g in zip(wide, (gq, gk, gv)))

    def across(values):
        folded = sum(values[:, i * 128 : (i + 1) * 128] for i in range(half // 128))
        return jnp.sum(folded.T, axis=0, keepdims=True)

    shift_grad = across(shifts)
    vec[9:10, :] = shift_grad
    vec[8:9, :] = (across(gains) - vectors[1:2, :] * shift_grad) / vectors[0:1, :]
    n = width // PIECES
    low = n // 2
    per = PIECES // 2
    for slot in range(PIECES):
        one, two = ones[slot // per], twos[slot // per]
        base = slot % per * n
        piece = sp[2] ^ slot
        part = pl.ds(pl.multiple_of(piece * n, n), n)
        one[base : base + n, :half] = gq[part, :].astype(BF16)
        one[base : base + n, half:] = gk[part, :].astype(BF16)
        piece = sp[3] ^ slot
        first = pl.ds(pl.multiple_of(piece * n, n), low)
        second = pl.ds(pl.multiple_of(piece * n + low, low), low)
        two[base : base + low, :half] = gv[first, :].astype(BF16)
        two[base : base + low, half:] = gv[second, :].astype(BF16)
        two[base + low : base + n, :] = go[pl.ds(pl.multiple_of(piece * low, low), low), :].astype(BF16)
    for i, two in enumerate(twos):
        lines = [vec[pl.ds(sp[3] ^ (i * per + s), 1), :] for s in range(per)]
        two[per * n :, :] = padded(lines).astype(BF16)


def last_kernel(tokens, gain, mid_grad, *refs):
    out = refs[-1]
    rows, tok, width = tokens.shape
    flat = rows * tok
    unit, scale = normalize(tokens[...].reshape(flat, width).astype(F32))
    parts = [refs[2 * r][0].astype(F32) + refs[2 * r + 1][0].astype(F32) + refs[-2][r].astype(F32) for r in range(rows)]
    grad = mid_grad[...] + norm_back(jnp.concatenate(parts, axis=0), unit, scale, gain[0:1, :])
    out[...] = grad.astype(BF16).reshape(rows, tok, width)


def unpack_ffn_kernel(far, sp, *refs):
    refs = list(refs)
    d_both, u_both = refs[0:2], refs[2:4]
    down, up, done, d_wide, u_wide, sems = refs[-6:]
    done[...] = jnp.zeros_like(done)
    _, rd, width = d_both[0].shape
    ru = up.shape[0] // PIECES
    half = down.shape[0] // 2
    count = PIECES // GROUP
    copies = []
    for which in range(2):
        for i in range(GROUP // 2):
            at = which * (GROUP // 2) + i
            group = (GROUP // 2 if far else 0) + i
            for k in range(count):
                slot = i * count + k
                place = (sp[2] ^ k) & (count - 1)
                rows = pl.ds(pl.multiple_of(place * rd, rd), rd)
                d_wide[at, rows, :] = d_both[which][slot].astype(F32)
                place = (sp[3] ^ k) & (count - 1)
                rows = pl.ds(pl.multiple_of(place * ru, ru), ru)
                for n in range(rd // ru):
                    part = u_both[which][slot, n * ru : (n + 1) * ru, :]
                    u_wide[at, rows, n * width : (n + 1) * width] = part.astype(F32)
            size = count * rd
            rows = pl.ds(pl.multiple_of(sp[which] * half + ((sp[2] // count) ^ group) * size, size), size)
            copies.append(pltpu.make_async_copy(d_wide.at[at], down.at[rows, :], sems.at[2 * at]))
            copies[-1].start()
            size = count * ru
            rows = pl.ds(pl.multiple_of(((sp[3] // count) ^ group) * size, size), size)
            copies.append(pltpu.make_async_copy(u_wide.at[at], up.at[rows, half_of(sp[which], half)], sems.at[2 * at + 1]))
            copies[-1].start()
    for copy in copies:
        copy.wait()


def unpack_attend_kernel(sp, *refs):
    gq, gk, gv, go, *lines = refs[8:]
    vec = lines.pop()
    ones, twos = (refs[0:2], refs[2:4]), (refs[4:6], refs[6:8])
    width = gq.shape[0]
    half = width // 2
    n = width // PIECES
    low = n // 2
    per = PIECES // 2
    for slot in range(PIECES):
        base = slot % per * n
        for which in range(2):
            one, two = ones[which][slot // per], twos[which][slot // per]
            cols = half_of(sp[which], half)
            piece = sp[2] ^ slot
            rows = pl.ds(pl.multiple_of(piece * n, n), n)
            gq[rows, cols] = one[base : base + n, :half].astype(F32)
            gk[rows, cols] = one[base : base + n, half:].astype(F32)
            piece = sp[3] ^ slot
            first = pl.ds(pl.multiple_of(piece * n, n), low)
            second = pl.ds(pl.multiple_of(piece * n + low, low), low)
            gv[first, cols] = two[base : base + low, :half].astype(F32)
            gv[second, cols] = two[base : base + low, half:].astype(F32)
            out_rows = pl.ds(pl.multiple_of(sp[which] * half + piece * low, low), low)
            go[out_rows, :] = two[base + low : base + n, :].astype(F32)
    for side in range(2):
        both = twos[0][side][per * n :, :].astype(F32) + twos[1][side][per * n :, :].astype(F32)
        for s in range(per):
            vec[pl.ds(sp[3] ^ (side * per + s), 1), :] = both[s : s + 1]
    for line, row in zip(lines, (0, 1, 2, 4, 3, 8, 9, 10, 11)):
        count = line.shape[1] // width
        for i in range(count):
            line[:, i * width : (i + 1) * width] = vec[row + i : row + i + 1, :]


def total(*values):
    return sum(v.astype(F32) for v in values).astype(BF16)


def sum_kernel(*refs):
    refs[-1][...] = total(*[r[...] for r in refs[:-1]])


def upper_kernel(*refs):
    count = len(refs) // 3
    for i, out in enumerate(refs[2 * count :]):
        keep, got = refs[2 * i : 2 * i + 2]
        half = keep.shape[0] // 2
        out[...] = total(keep[half:], got[half:])


def quarter_kernel(d_keep, d_got, d_last, u_keep, u_got, u_last, keep, send):
    rd = d_keep.shape[1]
    half = keep.shape[0]
    for i in range(2 * half):
        out = send if i >= half else keep
        out[i % half, :rd] = total(d_keep[i], d_got[i], d_last[i])
        out[i % half, rd:] = total(u_keep[i], u_got[i], u_last[i])


def halve_kernel(keep, got, out_keep, out_send):
    out_keep[...] = total(keep[0], got[0])
    out_send[...] = total(keep[1], got[1])


def pair_kernel(one, two, out):
    out[0] = one[...]
    out[1] = two[...]


def divide_kernel(one, two, d, u):
    rd = d.shape[1]
    for i in range(d.shape[0]):
        part = (one if i < 2 else two)[i % 2]
        d[i] = part[:rd]
        u[i] = part[rd:]


def join_kernel(*refs):
    count = len(refs) // 3
    for i, out in enumerate(refs[2 * count :]):
        one, two = refs[2 * i : 2 * i + 2]
        out[: one.shape[0]] = one[...]
        out[one.shape[0] :] = two[...]


def attend_upper_kernel(one_keep, one_got, two_keep, two_got, one, two):
    n = one.shape[0]
    one[...] = total(one_keep[n:], one_got[n:])
    two[:n] = total(two_keep[n : 2 * n], two_got[n : 2 * n])
    lines = total(two_keep[2 * n :], two_got[2 * n :]).astype(F32)
    two[n:] = fill(lines[4:8])


def fill(lines):
    return jnp.concatenate([lines, jnp.zeros((16 - lines.shape[0], lines.shape[1]), F32)], axis=0).astype(BF16)


def attend_quarter_kernel(one_keep, one_got, one_last, two_keep, two_got, two_last, keep, send):
    count = 2 * keep.shape[0]
    n = one_last.shape[0] // count
    lines = total(two_keep[2 * count * n :], two_got[2 * count * n :], two_last[count * n :]).astype(F32)
    for i in range(count):
        out = (keep, send)[i // 2]
        part = slice(i * n, (i + 1) * n)
        out[i % 2, :n] = total(one_keep[part], one_got[part], one_last[part])
        out[i % 2, n : 2 * n] = total(two_keep[part], two_got[part], two_last[part])
        out[i % 2, 2 * n :] = jnp.broadcast_to(lines[i : i + 1], (16, lines.shape[1])).astype(BF16)


def attend_divide_kernel(first, second, one, two):
    n = one.shape[0] // 4
    lines = []
    for i in range(4):
        part = (first if i < 2 else second)[i % 2]
        one[i * n : (i + 1) * n] = part[:n]
        two[i * n : (i + 1) * n] = part[n : 2 * n]
        lines.append(part[2 * n :].astype(F32)[:1])
    two[4 * n :] = padded(lines).astype(BF16)


def attend_join_kernel(one_a, one_b, two_a, two_b, one, two):
    n = one_a.shape[0]
    one[:n] = one_a[...]
    one[n:] = one_b[...]
    two[:n] = two_a[:n]
    two[n : 2 * n] = two_b[:n]
    lines = jnp.concatenate([two_a[n:].astype(F32)[:4], two_b[n:].astype(F32)[:4]], axis=0)
    two[2 * n :] = fill(lines)


def norm_grad_kernel(step, stations, rows, sp, *refs):
    out = refs[-1]
    place = lax.rem(ring_place(sp[4], stations) + stations - step, stations)
    chunk = sp[4] ^ ring_station(place, stations)
    for r in range(rows):
        values = [refs[2 * r][chunk], refs[2 * r + 1][chunk]]
        if step > 1:
            values.append(refs[2 * rows][r])
        out[r] = total(*values)


VMEM = pl.BlockSpec(memory_space=pltpu.VMEM)
SMEM = pl.BlockSpec(memory_space=pltpu.SMEM)
HBM = pl.BlockSpec(memory_space=pltpu.HBM)
ANY = pl.BlockSpec(memory_space=pl.ANY)


def call(kernel, ins, outs, scratch=(), us=1.0, limit=16, name=None, scalars=1, specs=None, grid=(), out_specs=None, aliases=None, extra=()):
    count = len(ins)

    def body_of(*refs):
        kernel(*refs[:count], *refs[count + len(extra) :])

    return pl.pallas_call(
        body_of,
        grid=grid,
        in_specs=[SMEM] * scalars + (specs or [VMEM] * (count - scalars)) + [ANY] * len(extra),
        out_specs=out_specs or [VMEM] * len(outs),
        input_output_aliases=aliases or {},
        out_shape=list(outs),
        scratch_shapes=list(scratch),
        compiler_params=pltpu.CompilerParams(vmem_limit_bytes=limit * MIB),
        cost_estimate=pl.CostEstimate(flops=int(us * 1.1e9), bytes_accessed=0, transcendentals=0),
        name=name,
    )(*ins, *extra)


def load(sp, arrays, halved, name, limit=16):
    shapes = [a.shape[:-1] + (a.shape[-1] // (2 if h else 1),) for a, h in zip(arrays, halved)]
    return call(
        functools.partial(load_kernel, halved), [sp] + arrays, [made(s, a.dtype) for s, a in zip(shapes, arrays)],
        scratch=[pltpu.SemaphoreType.DMA] * len(arrays), us=2.0, limit=limit, name=name, specs=[HBM] * len(arrays),
    )


def made(shape, dtype):
    return jax.ShapeDtypeStruct(shape, dtype)


def exchange(array, axis, mask):
    count = lax.axis_size(axis)
    return lax.ppermute(array, axis, [(i, i ^ mask) for i in range(count)])


def merge(kernel, ins, outs, name, extra=()):
    specs = [SMEM if a.dtype == jnp.int32 else VMEM for a in ins]
    return call(kernel, list(ins), list(outs), us=0.05, limit=8, name=name, scalars=0, specs=specs, extra=extra)


def tied(*arrays):
    return lax.optimization_barrier(arrays)


class Chain:
    def __init__(self, token):
        self.token = token

    def __call__(self, function, *args, **kwargs):
        outs = list(function(*args, extra=[self.token], **kwargs))
        self.token = outs[-1]
        return outs

    def hold(self, *arrays):
        *arrays, self.token = tied(*arrays, self.token)
        return arrays


def my_id(bits):
    out = 0
    for axis, mask in bits:
        out = out * 2 + jnp.where((lax.axis_index(axis) & mask) != 0, 1, 0)
    return out


def body(
    tokens, grad_out, crop, offsets, w_query, w_key, w_value, w_out, w_up, w_down, b_query, b_value,
    b_out, b_up, b_down, gain_one, shift_one, gain_two, shift_two,
):
    rows, tok, width = tokens.shape
    seq_count, dp_count = lax.axis_size("seq"), lax.axis_size("dp")
    stations = seq_count // 2
    hidden = w_up.shape[1]
    half = width // 2
    heads = HEADS // 2
    size = half // heads
    chip = 2 * tok
    flat = rows * tok
    small = stations <= 4
    seq = lax.axis_index("seq")
    core, station = seq % 2, seq // 2
    line = lambda v: v.reshape(1, -1)

    order = list(range(0, stations, 2)) + list(range(1, stations, 2))[::-1]
    ring = []
    for i, s in enumerate(order):
        after = order[(i + 1) % stations]
        ring += [(2 * s + c, 2 * after + c) for c in range(2)]

    dp_bits = [("dp", 1 << i) for i in range(dp_count.bit_length() - 1)]
    st_bits = [("seq", 2 << i) for i in range(stations.bit_length() - 1)]
    bit_x, bit_y = dp_bits[:2]
    rest = dp_bits[2:] + st_bits[2:]
    ids = [my_id([bit_x, bit_y] + st_bits[:2]), my_id([bit_y, bit_x] + st_bits[:2])]
    sp = jnp.stack([core, 1 - core, *ids, station]).astype(jnp.int32)

    mine = lambda a: lax.dynamic_slice_in_dim(a, core * half, half, a.ndim - 1)
    weights = jnp.stack([mine(w_query), mine(w_key), mine(w_value)])
    vectors = jnp.stack([gain_one, shift_one, b_query, b_value] + [jnp.zeros_like(gain_one)] * 4)
    state = []
    kept = [[None] * stations for _ in range(4)]
    blocks = {0: tokens}
    turns = [int(f"{i:0{stations.bit_length() - 1}b}"[::-1], 2) for i in range(stations)]
    for at, j in enumerate(turns):
        if j:
            low = j & -j
            block = blocks[j] = exchange(blocks[j ^ low], "seq", 2 * low)
            if at == 1 or at == stations - 1:
                block, state[-1] = tied(block, state[-1])
                blocks[j] = block
        else:
            block = tokens
        other = exchange(block, "seq", 1)
        first, last = at == 0, at == stations - 1
        ins = [sp, offsets, crop, block, other, vectors, weights] + ([] if first else state)
        outs = [
            made((rows, chip, half), BF16),
            made((rows, chip, half), BF16),
            made((rows, half, chip), BF16),
            made((rows, width, chip), BF16),
        ]
        if first:
            outs += [made((rows * heads, chip, 2 * size), BF16)]
        stat = made((rows * heads, 1, chip), F32)
        acc = made((rows * heads, size, chip), F32)
        if last:
            outs += [stat, acc, made((rows, tok, half), BF16), made((rows, tok, half), BF16)]
        else:
            outs += [stat, stat, acc]
        got = call(
            functools.partial(chunk_kernel, j, last, tok, rows), ins, outs,
            us=0.05, limit=LIMITS[0], name=f"attend_chunk_{j}", scalars=3,
        )
        for where, array in zip(kept, got[:4]):
            where[j] = array
        got = got[4:]
        if first:
            query, got = got[0], got[1:]
        if not last:
            state = [query] + list(got)
        if at == 0:
            sp_b, state[-1] = tied(sp, state[-1])
            tokens_v, g_v, wo, up, down, bo, bu, bd, gain_b, shift_b = load(
                sp_b,
                [tokens, grad_out, w_out, w_up, w_down, line(b_out), line(b_up), line(b_down), line(gain_two), line(shift_two)],
                [False] * 10, "load_feed_forward",
            )
            g_other = exchange(g_v, "seq", 1)
            state[-1], up = tied(state[-1], up)
        if at == 1:
            state[-1], g_other = tied(state[-1], g_other)
            g_other = g_other.reshape(flat, width)
    lse, out_t, att_m, att_o = got
    att_r = exchange(att_o, "seq", 1)

    wide = made((flat, width), F32)
    vec8 = made((8, width), F32)
    mid, normed_two, send, total, back, vec_a = call(
        ffn_first_kernel, [sp, att_m, att_r, wo, tokens_v, g_v, up, down, bo, bu, gain_b, shift_b],
        [wide, made((flat, width), BF16), made((flat, hidden + width), BF16), wide, wide, vec8],
        us=4.0, limit=LIMITS[1], name="feed_forward_a",
    )
    got = exchange(send, "seq", 1)
    outputs, hid_m, pre_m, mid_grad, branch, vec_ffn = call(
        ffn_second_kernel, [sp, mid, normed_two, g_v, up, down, bu, bd, gain_b, total, back, vec_a],
        [made((rows, tok, width), BF16), made((flat, hidden // 2), BF16), made((flat, hidden // 2), BF16), wide,
         made((rows, tok, width), BF16), vec8],
        us=4.0, limit=LIMITS[1], name="feed_forward_b",
    )
    branch_r = exchange(branch, "seq", 1)
    piece = made((PIECES // 2, hidden // 2 // PIECES, width), BF16)
    d_keep, d_send, u_keep, u_send = call(
        ffn_grad_kernel, [sp, hid_m, pre_m, normed_two, got, g_v.reshape(flat, width), g_other],
        [piece, piece, piece, piece],
        scratch=[pltpu.VMEM((hidden // 2, width), F32), pltpu.VMEM((width, hidden // 2), F32)],
        us=3.0, limit=LIMITS[2], name="feed_forward_grad",
    )
    chain = Chain(u_keep)

    q = PIECES // GROUP
    d_got, u_got = exchange(d_send, *bit_x), exchange(u_send, *bit_y)

    sums = []
    dn_m, dn_o, dn_r = [], [], []

    def together(name, *jobs):
        ins = [a for _, arrays, _ in jobs for a in arrays]
        outs = [s for _, _, shapes in jobs for s in shapes]

        def kernel(*refs):
            at, to = 0, len(ins)
            for one, arrays, shapes in jobs:
                one(*refs[at : at + len(arrays)], *refs[to : to + len(shapes)])
                at, to = at + len(arrays), to + len(shapes)

        res = iter(chain(functools.partial(merge, kernel), ins, outs, name))
        return [[next(res) for _ in shapes] for _, _, shapes in jobs]

    def norm_job(chunk, before):
        pairs = [a for both in zip(dn_m, dn_r) for a in both]
        kernel = functools.partial(norm_grad_kernel, chunk, stations, rows)
        return (kernel, [sp] + pairs + before, [made((rows, tok, width), BF16)])

    for r in range(rows):
        last = r == rows - 1
        arrays = [branch, branch_r, wo, query, lse, out_t, weights] + [a for part in kept for a in part]
        specs = [VMEM] * len(arrays)
        if not small:
            for i, a in enumerate(arrays):
                if a.ndim == 3 and a is not weights:
                    block_shape = (a.shape[0] // rows,) + a.shape[1:]
                    specs[i] = pl.BlockSpec(block_shape, functools.partial(lambda r, i: (r, 0, 0), r))
        tail = list(sums)
        if last:
            tail += [vectors, vec_ffn]
        part = made((stations, tok, width), BF16)
        grads = [made((width, half), F32)] * 3 + [made((half, width), F32), made((8, half), F32)]
        outs = [part, part] + grads
        scratch = []
        if last:
            outs = [part, part] + [made((width // 2, width), BF16)] * 2 + [made((width // 2 + 16, width), BF16)] * 2
            scratch = [pltpu.VMEM(g.shape, F32) for g in grads] + [pltpu.VMEM((16, width), F32)]
        run = functools.partial(call, functools.partial(attend_back_kernel, stations, tok, r, small, last))
        res = chain(
            run, [sp, offsets, crop] + arrays + tail, outs, scratch=scratch,
            us=BACK_US, limit=LIMITS[3] if small else 48, name=f"attend_back_{r}", scalars=3,
            specs=specs + [VMEM] * len(tail), grid=() if small else (1,),
        )
        dn_m.append(res[0])
        dn_o.append(res[1])
        sums = list(res[2:7])
        if r == rows - 2:
            quarters = made((q,) + piece.shape[1:], BF16)
            ((d_next, u_next),) = together(
                "add_quarters", (upper_kernel, [d_keep, d_got, u_keep, u_got], [quarters, quarters])
            )
            d_got2, u_got2 = exchange(d_next, *bit_y), exchange(u_next, *bit_x)
            dn_r += [exchange(a, "seq", 1) for a in chain.hold(*dn_o)]
    one_keep, one_send, two_keep, two_send = res[2:]

    rd = hidden // 2 // PIECES
    n = width // PIECES
    ff_part, at_part = made((2 * rd, width), BF16), made((2 * n + 16, width), BF16)
    two_of = lambda a: made((2,) + a.shape, BF16)
    token_block = made((rows, tok, width), BF16)
    bit_z, bit_w = st_bits[:2]

    def over_rest(part):
        for i, (where, mask) in enumerate(rest):
            got = exchange(part, where, mask)
            ((part,),) = together(f"add_rest_{i}", (sum_kernel, [part, got], [made(part.shape, BF16)]))
        return part

    def unpack(far, d, d_other, u, u_other, before):
        ins = [sp, d, d_other, u, u_other] + before
        scratch = [
            pltpu.VMEM((GROUP, q * rd, width), F32), pltpu.VMEM((GROUP, q * width // PIECES, hidden // 2), F32),
            pltpu.SemaphoreType.DMA((2 * GROUP,)),
        ]
        return chain(
            functools.partial(call, functools.partial(unpack_ffn_kernel, far)), ins,
            [made((hidden, width), F32), made((width, hidden), F32), made((8, 128), F32)], scratch=scratch, us=0.1,
            limit=LIMITS[4], name="unpack_feed_forward", specs=[VMEM] * 4 + [HBM] * len(before),
            out_specs=[HBM] * 2 + [VMEM], aliases={5: 0, 6: 1} if before else None,
        )[:2]

    def other_core(*arrays):
        return [exchange(a, "seq", 1) for a in arrays]

    two_a, two_b = two_of(ff_part), two_of(at_part)
    dn_r = chain.hold(*dn_r)
    ((a_keep, a_send),) = together(
        "phase_1", (quarter_kernel, [d_keep, d_got, d_got2, u_keep, u_got, u_got2], [two_a, two_a])
    )
    one_send, two_send, dn_last = chain.hold(one_send, two_send, dn_o[-1])
    a_got = exchange(a_send, *bit_z)
    one_got, two_got = exchange(one_send, *bit_x), exchange(two_send, *bit_y)
    dn_r += chain.hold(*other_core(dn_last))

    one_shape, two_shape = made((4 * n, width), BF16), made((4 * n + 16, width), BF16)
    (a_keep, a_send), (one_next, two_next) = together(
        "phase_2",
        (halve_kernel, [a_keep, a_got], [ff_part] * 2),
        (attend_upper_kernel, [one_keep, one_got, two_keep, two_got], [one_shape, two_shape]),
    )
    a_got = exchange(a_send, *bit_w)
    one_got2, two_got2 = exchange(one_next, *bit_y), exchange(two_next, *bit_x)

    (a_own,), (b_keep, b_send) = together(
        "phase_3",
        (sum_kernel, [a_keep, a_got], [ff_part]),
        (attend_quarter_kernel, [one_keep, one_got, one_got2, two_keep, two_got, two_got2], [two_b, two_b]),
    )
    a_own = over_rest(a_own)
    a_near = exchange(a_own, *bit_w)
    b_got = exchange(b_send, *bit_z)

    (a_pair,), (b_keep, b_send) = together(
        "phase_4",
        (pair_kernel, [a_own, a_near], [two_a]),
        (halve_kernel, [b_keep, b_got], [at_part] * 2),
    )
    a_far = exchange(a_pair, *bit_z)
    b_got = exchange(b_send, *bit_w)

    (d_mine, u_mine), (b_own,) = together(
        "phase_5",
        (divide_kernel, [a_pair, a_far], [quarters, quarters]),
        (sum_kernel, [b_keep, b_got], [at_part]),
    )
    b_own = over_rest(b_own)
    d_y, u_x = exchange(d_mine, *bit_y), exchange(u_mine, *bit_x)
    b_near = exchange(b_own, *bit_w)

    (d_near, u_near), (b_pair,), (moving,) = together(
        "phase_6",
        (join_kernel, [d_mine, d_y, u_mine, u_x], [piece, piece]),
        (pair_kernel, [b_own, b_near], [two_b]),
        norm_job(1, []),
    )
    d_far, u_far = exchange(d_near, *bit_x), exchange(u_near, *bit_y)
    b_far = exchange(b_pair, *bit_z)
    moving = lax.ppermute(moving, "seq", ring)
    for chunk in range(2, stations - 2):
        ((moving,),) = together("norm_step", norm_job(chunk, [moving]))
        moving = lax.ppermute(moving, "seq", ring)
    d_far, u_far = chain.hold(d_far, u_far)

    (one_mine, two_mine), (moving,) = together(
        "phase_7",
        (attend_divide_kernel, [b_pair, b_far], [one_shape, two_shape]),
        norm_job(stations - 2, [moving]),
    )
    one_y, two_x = exchange(one_mine, *bit_y), exchange(two_mine, *bit_x)
    moving = lax.ppermute(moving, "seq", ring)
    d_near, u_near = chain.hold(d_near, u_near)
    d_near_o, u_near_o = chain.hold(*other_core(d_near, u_near))
    grad_down, grad_up = unpack(False, d_near, d_near_o, u_near, u_near_o, [])

    (one_near, two_near), (moving,) = together(
        "phase_8",
        (
            attend_join_kernel, [one_mine, one_y, two_mine, two_x],
            [made((8 * n, width), BF16), made((8 * n + 16, width), BF16)],
        ),
        norm_job(stations - 1, [moving]),
    )
    one_far, two_far = exchange(one_near, *bit_x), exchange(two_near, *bit_y)
    moving = lax.ppermute(moving, "seq", ring)
    d_far, u_far = chain.hold(d_far, u_far)
    d_far_o, u_far_o = chain.hold(*other_core(d_far, u_far))
    grad_down, grad_up = unpack(True, d_far, d_far_o, u_far, u_far_o, [grad_down, grad_up])
    one_near_o, two_near_o = other_core(*chain.hold(one_near, two_near))
    one_far_o, two_far_o = other_core(*chain.hold(one_far, two_far))
    pairs = [a for both in zip(dn_m, dn_r) for a in both]
    input_grad = call(
        last_kernel, [tokens_v, vectors, mid_grad] + pairs + [moving], [token_block],
        us=0.1, limit=LIMITS[4], name="input_grad", scalars=0, extra=[chain.token],
    )[0]
    one_all = [one_near, one_far, one_near_o, one_far_o]
    two_all = [two_near, two_far, two_near_o, two_far_o]
    square = made((width, width), F32)
    run = functools.partial(call, unpack_attend_kernel)
    thin = made((1, width), F32)
    results = chain(
        run, [sp] + one_all + two_all, [square] * 4 + [thin] * 3 + [made((1, hidden), F32)] + [thin] * 5,
        scratch=[pltpu.VMEM((PIECES, width), F32)], us=0.1, limit=LIMITS[4], name="unpack_attend",
    )
    grad_query, grad_key, grad_value, grad_out_proj = results[:4]
    lines = [r.reshape(-1) for r in results[4:]]

    return (outputs, input_grad, grad_query, grad_key, grad_value, grad_out_proj, grad_up, grad_down, *lines)


def solution(mesh):
    split, row, copied = P("dp", "seq", None), P("dp"), P()
    return jax.shard_map(
        body,
        mesh=mesh,
        in_specs=(split, split, row, P("dp", None)) + (copied,) * 15,
        out_specs=(split, split) + (copied,) * 15,
        check_vma=False,
    )
```

```python
import functools

import jax
import jax.numpy as jnp
from jax import lax
from jax.experimental import pallas as pl
from jax.experimental.pallas import tpu as pltpu
from jax.sharding import PartitionSpec as P

HEADS = 8
EPSILON = 1e-06
MASKED = -1e30
MIB = 1024 * 1024
LIMITS = (16, 20, 20, 26, 20)
PIECES = 16
GROUP = 4
BACK_US = 0.05
BF16 = jnp.bfloat16
F32 = jnp.float32
GELU_C = 0.7978845608028654
GELU_A = 0.044715


def nn(a, b):
    return jnp.dot(a, b, preferred_element_type=F32)


def nt(a, b):
    return lax.dot_general(a, b, (((1,), (1,)), ((), ())), preferred_element_type=F32)


def tn(a, b):
    return lax.dot_general(a, b, (((0,), (0,)), ((), ())), preferred_element_type=F32)


def normalize(values):
    center = values - jnp.mean(values, axis=-1, keepdims=True)
    scale = lax.rsqrt(jnp.mean(center * center, axis=-1, keepdims=True) + EPSILON)
    return center * scale, scale


def norm_back(cotangent, unit, scale, gain):
    g = cotangent * gain
    return scale * (
        g
        - jnp.mean(g, axis=-1, keepdims=True)
        - unit * jnp.mean(g * unit, axis=-1, keepdims=True)
    )


def segments(pos, offsets, crop, row):
    count = offsets.shape[1]
    seg = jnp.zeros(pos.shape, jnp.int32)
    for j in range(count):
        seg += (pos >= offsets[row, j]).astype(jnp.int32)
    return seg + count * (pos >= crop[row]).astype(jnp.int32)


def positions(sp, chunk, tok, shape, dim):
    start = (sp[4] ^ chunk) * (2 * tok)
    i = lax.broadcasted_iota(jnp.int32, shape, dim)
    return i + jnp.where(i < tok, start + sp[0] * tok, start + sp[1] * tok - tok)


def half_of(which, width):
    return pl.ds(pl.multiple_of(which * width, 128), width)


def padded(lines):
    return jnp.concatenate(lines + [jnp.zeros((16 - len(lines), lines[0].shape[1]), F32)], axis=0)


def load_kernel(halved, sp, *refs):
    count = len(halved)
    sources, targets, sems = refs[:count], refs[count : 2 * count], refs[2 * count :]
    copies = []
    for half, source, target, sem in zip(halved, sources, targets, sems):
        if half:
            source = source.at[:, half_of(sp[0], source.shape[1] // 2)]
        copies.append(pltpu.make_async_copy(source, target, sem))
    for copy in copies:
        copy.start()
    for copy in copies:
        copy.wait()


def chunk_kernel(chunk, last, tok, rows, *refs):
    refs = list(refs)
    first = chunk == 0
    sp, offsets, crop, xm, xo, vectors, weights = refs[:7]
    refs = refs[7:]
    if not first:
        qm_in, m_in, l_in, acc_in = refs[:4]
        refs = refs[4:]
    k_out, v_out, kt_out, nt_out = refs[:4]
    refs = refs[4:]
    if first:
        qm_out = refs.pop(0)
    if last:
        lse_out, ot_out, att_m, att_o = refs[:4]
    else:
        m_out, l_out, acc_out = refs
    half = weights.shape[2]
    heads = HEADS // 2
    size = half // heads
    chip = 2 * tok
    for at, x in ((0, xm), (tok, xo)):
        values = x[...].reshape(rows * tok, -1).astype(F32)
        unit, _ = normalize(values)
        normed = unit * vectors[0:1, :] + vectors[1:2, :]
        low = normed.astype(BF16)
        k = nn(low, weights[1])
        v = (nn(low, weights[2]) + vectors[3:4, half_of(sp[0], half)]).astype(BF16)
        if first:
            q = ((nn(low, weights[0]) + vectors[2:3, half_of(sp[0], half)]).astype(BF16).astype(F32) * size**-0.5).astype(BF16)
            lane = lax.broadcasted_iota(jnp.int32, (tok, 2 * size), 1)
        for r in range(rows):
            part = slice(r * tok, (r + 1) * tok)
            k_out[r, at : at + tok, :] = k[part].astype(BF16)
            v_out[r, at : at + tok, :] = v[part]
            kt_out[r, :, at : at + tok] = k[part].T.astype(BF16)
            nt_out[r, :, at : at + tok] = normed[part].T.astype(BF16)
            if first:
                for h in range(heads):
                    pair = q[part, (h // 2) * 2 * size : (h // 2 + 1) * 2 * size]
                    keep = (lane >= size) if h % 2 else (lane < size)
                    qm_out[r * heads + h, at : at + tok, :] = jnp.where(keep, pair, jnp.zeros_like(pair))
    qm = qm_out if first else qm_in
    for r in range(rows):
        key_seg = segments(positions(sp, chunk, tok, (chip, chip), 0), offsets, crop, r)
        query_seg = segments(positions(sp, 0, tok, (1, chip), 1), offsets, crop, r)
        bias = jnp.where(key_seg == query_seg, 0.0, MASKED)
        outs = []
        spot = [r * heads + h for h in range(heads)]
        pairs = [slice((h // 2) * 2 * size, (h // 2 + 1) * 2 * size) for h in range(heads)]
        s = [nt(k_out[r, :, pairs[h]], qm[spot[h]]) + bias for h in range(heads)]
        tops = [jnp.max(a, axis=0, keepdims=True) for a in s]
        if not first:
            olds = [m_in[at] for at in spot]
            tops = [jnp.maximum(a, b) for a, b in zip(olds, tops)]
        p = [jnp.exp(a - b) for a, b in zip(s, tops)]
        totals = [jnp.sum(a, axis=0, keepdims=True) for a in p]
        addeds = [tn(v_out[r, :, pairs[h]], p[h].astype(BF16)) for h in range(heads)]
        for h, at in enumerate(spot):
            added = addeds[h][(h % 2) * size : (h % 2 + 1) * size]
            total = totals[h]
            if not first:
                keep = jnp.exp(olds[h] - tops[h])
                total += l_in[at] * keep
                added += acc_in[at] * keep
            if last:
                lse_out[at] = tops[h] + jnp.log(total)
                out = added / total
                ot_out[at] = out
                outs.append(out)
            else:
                m_out[at] = tops[h]
                l_out[at] = total
                acc_out[at] = added
        if last:
            att = jnp.concatenate(outs, axis=0).T.astype(BF16)
            att_m[r] = att[:tok]
            att_o[r] = att[tok:]


def feed_forward_half(sp, which, normed, g, up, down, bup, hid, pre, at, vec, total, back):
    half = up.shape[1] // 2
    row = min(512, half)
    block = min(512, row)
    count = half // block
    cols = [pl.ds(pl.multiple_of(sp[which] * half + j * block, 128), block) for j in range(count)]
    for first in range(0, count, 2):
        js = range(first, min(first + 2, count))
        us = [nn(normed, up[:, cols[j]]) + bup[:, cols[j]] for j in js]
        gs = [nt(g, down[cols[j], :]) for j in js]
        outs, pres = [], []
        for j, u, back_in in zip(js, us, gs):
            square = u * u
            plus = 1.0 + jnp.tanh(u * (GELU_C + GELU_C * GELU_A * square))
            low = 0.5 * u
            hidden = (low * plus).astype(BF16)
            slope = plus * (0.5 + low * (2.0 - plus) * (GELU_C + 3 * GELU_C * GELU_A * square))
            grad = (back_in * slope).astype(BF16)
            hid[:, j * block : (j + 1) * block] = hidden
            pre[:, at + j * block : at + (j + 1) * block] = grad
            outs.append(hidden)
            pres.append(grad)
            line = jnp.sum(grad.astype(F32), axis=0, keepdims=True)
            lane = j * block % row
            vec[pl.ds(sp[which] * (half // row) + j * block // row, 1), lane : lane + block] = line
        for j, hidden, grad in zip(js, outs, pres):
            more, less = nn(hidden, down[cols[j], :]), nt(grad, up[:, cols[j]])
            total = more if total is None else total + more
            back = less if back is None else back + less
    return total, back


def ffn_first_kernel(
    sp, att_m, att_o, wo, tokens, cot, up, down, b_out, bup, gain, shift, mid_out, normed_out, send, total_out, back_out, vec
):
    rows, tok, width = tokens.shape
    flat = rows * tok
    quarter = width // 2
    mine = pl.ds(pl.multiple_of(sp[0] * quarter, 128), quarter)
    other = pl.ds(pl.multiple_of(sp[1] * quarter, 128), quarter)
    mid = (
        tokens[...].reshape(flat, width).astype(F32)
        + nn(att_m[...].reshape(flat, -1), wo[mine, :])
        + nn(att_o[...].reshape(flat, -1), wo[other, :])
        + b_out[...]
    )
    mid_out[...] = mid
    unit, _ = normalize(mid)
    normed = (unit * gain[...] + shift[...]).astype(BF16)
    normed_out[...] = normed
    half = up.shape[1] // 2
    send[:, 2 * half :] = normed
    vec[...] = jnp.zeros_like(vec)
    g = cot[...].reshape(flat, width)
    total_out[...], back_out[...] = feed_forward_half(
        sp, 1, normed, g, up, down, bup, send, send, half, vec, None, None
    )


def ffn_second_kernel(
    sp, mid_in, normed_in, cot, up, down, bup, b_down, gain, total_in, back_in, vec_in, out, hid, pre, mid_grad, branch, vec
):
    rows, tok, width = cot.shape
    flat = rows * tok
    g = cot[...].reshape(flat, width)
    vec[...] = vec_in[...]
    total, back = feed_forward_half(
        sp, 0, normed_in[...], g, up, down, bup, hid, pre, 0, vec, total_in[...], back_in[...]
    )
    mid = mid_in[...]
    out[...] = (mid + total + b_down[...]).astype(BF16).reshape(rows, tok, width)
    unit, scale = normalize(mid)
    gf = g.astype(F32)
    grad = gf + norm_back(back, unit, scale, gain[...])
    mid_grad[...] = grad
    low = grad.astype(BF16)
    branch[...] = low.reshape(rows, tok, width)
    vec[4:5, :] = jnp.sum(gf, axis=0, keepdims=True)
    vec[5:6, :] = jnp.sum(back * unit, axis=0, keepdims=True)
    vec[6:7, :] = jnp.sum(back, axis=0, keepdims=True)
    vec[7:8, :] = jnp.sum(low.astype(F32), axis=0, keepdims=True)


def ffn_grad_kernel(sp, hid_m, pre_m, n_m, got, g_m, g_o, d_keep, d_send, u_keep, u_send):
    half = hid_m.shape[1]
    width = g_m.shape[1]
    per = PIECES // 2
    rd, ru = half // PIECES, width // PIECES
    for send, d, u in ((1, d_send, u_send), (0, d_keep, u_keep)):
        part = (sp[2] // per) ^ send
        cols = half_of(part, half // 2)
        gd = tn(hid_m[:, cols], g_m[...]) + tn(got[:, cols], g_o[...])
        part = (sp[3] // per) ^ send
        own = half_of(part, width // 2)
        others = pl.ds(pl.multiple_of(2 * half + part * (width // 2), 128), width // 2)
        gu = tn(n_m[:, own], pre_m[...]) + tn(got[:, others], got[:, half : 2 * half])
        for p in range(per):
            d[(sp[2] & (per - 1)) ^ p] = gd[p * rd : (p + 1) * rd].astype(BF16)
            at = (sp[3] & (per - 1)) ^ p
            for i in range(half // width):
                u[at, i * ru : (i + 1) * ru, :] = gu[p * ru : (p + 1) * ru, i * width : (i + 1) * width].astype(BF16)


def attend_back_kernel(stations, tok, row, whole, last, *refs):
    refs = list(refs)

    def take(count):
        got = refs[:count]
        del refs[:count]
        return got

    sp, offsets, crop, br_m, br_o, wo, qm, lse, ot, weights = take(10)
    k, v, kt, norm_t = (take(stations) for _ in range(4))
    sums_in = take(5) if row else None
    if last:
        vectors, vec_in = take(2)
        before = take(row)
    dn_m, dn_o = take(2)
    base = row * stations if last else 0
    if last:
        ones, twos = take(2), take(2)
    gq, gk, gv, go, sums = take(5)
    at = row if whole else 0
    heads = HEADS // 2
    _, width, half = weights.shape
    size = half // heads
    chip = 2 * tok
    block = min(4, stations)
    blocks = stations // block

    branch = jnp.concatenate([br_m[at], br_o[at]], axis=0)
    do = nt(branch, wo[half_of(sp[0], half), :])
    dot = do.T
    do = do.astype(BF16)
    lane = lax.broadcasted_iota(jnp.int32, (chip, 2 * size), 1)
    head_at = at * heads
    out_t = jnp.concatenate([ot[head_at + h] for h in range(heads)], axis=0).astype(BF16)
    go_row = nn(out_t, branch)
    query_seg = segments(positions(sp, 0, tok, (1, chip), 1), offsets, crop, row)
    biases = []
    for chunk in range(stations):
        key_seg = segments(positions(sp, chunk, tok, (chip, chip), 0), offsets, crop, row)
        biases.append(jnp.where(key_seg == query_seg, 0.0, MASKED))
    dqt = []
    dks = [[] for _ in range(blocks)]
    dvs = [[] for _ in range(blocks)]
    for pair in range(heads // 2):
        lanes = slice(pair * 2 * size, (pair + 1) * 2 * size)
        dk = [None] * blocks
        dv = [None] * blocks
        for h in (2 * pair, 2 * pair + 1):
            wide = do[:, lanes]
            dm = jnp.where((lane >= size) if h % 2 else (lane < size), wide, jnp.zeros_like(wide))
            delta = jnp.sum(ot[head_at + h] * dot[h * size : (h + 1) * size], axis=0, keepdims=True)
            dq = None
            for b in range(blocks):
                chunks = range(b * block, (b + 1) * block)
                keys = jnp.concatenate([k[c][at, :, lanes] for c in chunks], axis=0)
                values = jnp.concatenate([v[c][at, :, lanes] for c in chunks], axis=0)
                keys_t = jnp.concatenate([kt[c][at, h * size : (h + 1) * size, :] for c in chunks], axis=1)
                bias = jnp.concatenate([biases[c] for c in chunks], axis=0)
                p = jnp.exp(nt(keys, qm[head_at + h]) + bias - lse[head_at + h])
                ds = (p * (nt(values, dm) - delta)).astype(BF16)
                dv_h, dk_h = nn(p.astype(BF16), dm), nn(ds, qm[head_at + h])
                dv[b] = dv_h if dv[b] is None else dv[b] + dv_h
                dk[b] = dk_h if dk[b] is None else dk[b] + dk_h
                more = nn(keys_t, ds)
                dq = more if dq is None else dq + more
            dqt.append(dq)
        for b in range(blocks):
            dks[b].append(dk[b].astype(BF16))
            dvs[b].append(dv[b].astype(BF16))
    dq = (jnp.concatenate(dqt, axis=0) * size**-0.5).T.astype(BF16)
    gq_row = nn(norm_t[0][at], dq)
    gk_row = gv_row = sum_k = sum_v = 0.0
    for b in range(blocks):
        dk = jnp.concatenate(dks[b], axis=1)
        dv = jnp.concatenate(dvs[b], axis=1)
        normed = jnp.concatenate([norm_t[c][at] for c in range(b * block, (b + 1) * block)], axis=1)
        gk_row += nn(normed, dk)
        gv_row += nn(normed, dv)
        sum_k += jnp.sum(dk.astype(F32), axis=0, keepdims=True)
        sum_v += jnp.sum(dv.astype(F32), axis=0, keepdims=True)
        dn = nt(dk, weights[1]) + nt(dv, weights[2])
        for i in range(block):
            part = dn[i * chip : (i + 1) * chip]
            if b + i == 0:
                part += nt(dq, weights[0])
            dn_m[b * block + i] = part[:tok].astype(BF16)
            dn_o[base + b * block + i] = part[tok:].astype(BF16)
    sum_q = jnp.sum(dq.astype(F32), axis=0, keepdims=True)
    made_here = (gq_row, gk_row, gv_row, go_row, jnp.concatenate([sum_q, sum_v, sum_k, jnp.zeros((5, half), F32)]))
    for i, (ref, value) in enumerate(zip((gq, gk, gv, go, sums), made_here)):
        ref[...] = value if sums_in is None else value + sums_in[i][...]
    if not last:
        return

    for r, part in enumerate(before):
        dn_o[r * stations : (r + 1) * stations] = part[...]
    vec = refs[0]
    lane = lax.broadcasted_iota(jnp.int32, (2, width), 1)
    both = sums[0:2, :]
    both = jnp.concatenate([both, both], axis=1)
    vec[0:2, :] = jnp.where((lane >= half) == (sp[0] == 1), both, 0.0)
    vec[2:3, :] = vec_in[7:8, :]
    vec[3:4, :] = vec_in[4:5, :]
    vec[4:8, :] = vec_in[0:4, :]
    vec[10:12, :] = vec_in[5:7, :]
    vec[12:16, :] = jnp.zeros((4, width), F32)
    wide = [weights[i].astype(F32) for i in range(3)]
    shifts = sum(w * sums[i : i + 1, :] for w, i in zip(wide, (0, 2, 1)))
    gains = sum(w * g[...] for w, g in zip(wide, (gq, gk, gv)))

    def across(values):
        folded = sum(values[:, i * 128 : (i + 1) * 128] for i in range(half // 128))
        return jnp.sum(folded.T, axis=0, keepdims=True)

    shift_grad = across(shifts)
    vec[9:10, :] = shift_grad
    vec[8:9, :] = (across(gains) - vectors[1:2, :] * shift_grad) / vectors[0:1, :]
    n = width // PIECES
    low = n // 2
    per = PIECES // 2
    for slot in range(PIECES):
        one, two = ones[slot // per], twos[slot // per]
        base = slot % per * n
        piece = sp[2] ^ slot
        part = pl.ds(pl.multiple_of(piece * n, n), n)
        one[base : base + n, :half] = gq[part, :].astype(BF16)
        one[base : base + n, half:] = gk[part, :].astype(BF16)
        piece = sp[3] ^ slot
        first = pl.ds(pl.multiple_of(piece * n, n), low)
        second = pl.ds(pl.multiple_of(piece * n + low, low), low)
        two[base : base + low, :half] = gv[first, :].astype(BF16)
        two[base : base + low, half:] = gv[second, :].astype(BF16)
        two[base + low : base + n, :] = go[pl.ds(pl.multiple_of(piece * low, low), low), :].astype(BF16)
    for i, two in enumerate(twos):
        lines = [vec[pl.ds(sp[3] ^ (i * per + s), 1), :] for s in range(per)]
        two[per * n :, :] = padded(lines).astype(BF16)


def last_kernel(tokens, gain, mid_grad, *refs):
    out = refs[-1]
    rows, tok, width = tokens.shape
    flat = rows * tok
    unit, scale = normalize(tokens[...].reshape(flat, width).astype(F32))
    parts = []
    for r in range(rows):
        part = refs[r][0].astype(F32) + refs[rows][r * refs[0].shape[0]].astype(F32)
        for arrived in refs[rows + 1 : -1]:
            part += arrived[r].astype(F32)
        parts.append(part)
    grad = mid_grad[...] + norm_back(jnp.concatenate(parts, axis=0), unit, scale, gain[0:1, :])
    out[...] = grad.astype(BF16).reshape(rows, tok, width)


def unpack_ffn_kernel(far, sp, *refs):
    refs = list(refs)
    d_both, u_both = refs[0:2], refs[2:4]
    down, up, done, d_wide, u_wide, sems = refs[-6:]
    done[...] = jnp.zeros_like(done)
    _, rd, width = d_both[0].shape
    ru = up.shape[0] // PIECES
    half = down.shape[0] // 2
    count = PIECES // GROUP
    copies = []
    for which in range(2):
        for i in range(GROUP // 2):
            at = which * (GROUP // 2) + i
            group = (GROUP // 2 if far else 0) + i
            for k in range(count):
                slot = i * count + k
                place = (sp[2] ^ k) & (count - 1)
                rows = pl.ds(pl.multiple_of(place * rd, rd), rd)
                d_wide[at, rows, :] = d_both[which][slot].astype(F32)
                place = (sp[3] ^ k) & (count - 1)
                rows = pl.ds(pl.multiple_of(place * ru, ru), ru)
                for n in range(rd // ru):
                    part = u_both[which][slot, n * ru : (n + 1) * ru, :]
                    u_wide[at, rows, n * width : (n + 1) * width] = part.astype(F32)
            size = count * rd
            rows = pl.ds(pl.multiple_of(sp[which] * half + ((sp[2] // count) ^ group) * size, size), size)
            copies.append(pltpu.make_async_copy(d_wide.at[at], down.at[rows, :], sems.at[2 * at]))
            copies[-1].start()
            size = count * ru
            rows = pl.ds(pl.multiple_of(((sp[3] // count) ^ group) * size, size), size)
            copies.append(pltpu.make_async_copy(u_wide.at[at], up.at[rows, half_of(sp[which], half)], sems.at[2 * at + 1]))
            copies[-1].start()
    for copy in copies:
        copy.wait()


def unpack_attend_kernel(sp, *refs):
    gq, gk, gv, go, *lines = refs[8:]
    vec = lines.pop()
    ones, twos = (refs[0:2], refs[2:4]), (refs[4:6], refs[6:8])
    width = gq.shape[0]
    half = width // 2
    n = width // PIECES
    low = n // 2
    per = PIECES // 2
    for slot in range(PIECES):
        base = slot % per * n
        for which in range(2):
            one, two = ones[which][slot // per], twos[which][slot // per]
            cols = half_of(sp[which], half)
            piece = sp[2] ^ slot
            rows = pl.ds(pl.multiple_of(piece * n, n), n)
            gq[rows, cols] = one[base : base + n, :half].astype(F32)
            gk[rows, cols] = one[base : base + n, half:].astype(F32)
            piece = sp[3] ^ slot
            first = pl.ds(pl.multiple_of(piece * n, n), low)
            second = pl.ds(pl.multiple_of(piece * n + low, low), low)
            gv[first, cols] = two[base : base + low, :half].astype(F32)
            gv[second, cols] = two[base : base + low, half:].astype(F32)
            out_rows = pl.ds(pl.multiple_of(sp[which] * half + piece * low, low), low)
            go[out_rows, :] = two[base + low : base + n, :].astype(F32)
    for side in range(2):
        both = twos[0][side][per * n :, :].astype(F32) + twos[1][side][per * n :, :].astype(F32)
        for s in range(per):
            vec[pl.ds(sp[3] ^ (side * per + s), 1), :] = both[s : s + 1]
    for line, row in zip(lines, (0, 1, 2, 4, 3, 8, 9, 10, 11)):
        count = line.shape[1] // width
        for i in range(count):
            line[:, i * width : (i + 1) * width] = vec[row + i : row + i + 1, :]


def total(*values):
    return sum(v.astype(F32) for v in values).astype(BF16)


def sum_kernel(*refs):
    refs[-1][...] = total(*[r[...] for r in refs[:-1]])


def upper_kernel(*refs):
    count = len(refs) // 3
    for i, out in enumerate(refs[2 * count :]):
        keep, got = refs[2 * i : 2 * i + 2]
        half = keep.shape[0] // 2
        out[...] = total(keep[half:], got[half:])


def quarter_kernel(d_keep, d_got, d_last, u_keep, u_got, u_last, keep, send):
    rd = d_keep.shape[1]
    half = keep.shape[0]
    for i in range(2 * half):
        out = send if i >= half else keep
        out[i % half, :rd] = total(d_keep[i], d_got[i], d_last[i])
        out[i % half, rd:] = total(u_keep[i], u_got[i], u_last[i])


def halve_kernel(keep, got, out_keep, out_send):
    out_keep[...] = total(keep[0], got[0])
    out_send[...] = total(keep[1], got[1])


def pair_kernel(one, two, out):
    out[0] = one[...]
    out[1] = two[...]


def divide_kernel(one, two, d, u):
    rd = d.shape[1]
    for i in range(d.shape[0]):
        part = (one if i < 2 else two)[i % 2]
        d[i] = part[:rd]
        u[i] = part[rd:]


def join_kernel(*refs):
    count = len(refs) // 3
    for i, out in enumerate(refs[2 * count :]):
        one, two = refs[2 * i : 2 * i + 2]
        out[: one.shape[0]] = one[...]
        out[one.shape[0] :] = two[...]


def attend_upper_kernel(one_keep, one_got, two_keep, two_got, one, two):
    n = one.shape[0]
    one[...] = total(one_keep[n:], one_got[n:])
    two[:n] = total(two_keep[n : 2 * n], two_got[n : 2 * n])
    lines = total(two_keep[2 * n :], two_got[2 * n :]).astype(F32)
    two[n:] = fill(lines[4:8])


def fill(lines):
    return jnp.concatenate([lines, jnp.zeros((16 - lines.shape[0], lines.shape[1]), F32)], axis=0).astype(BF16)


def attend_quarter_kernel(one_keep, one_got, one_last, two_keep, two_got, two_last, keep, send):
    count = 2 * keep.shape[0]
    n = one_last.shape[0] // count
    lines = total(two_keep[2 * count * n :], two_got[2 * count * n :], two_last[count * n :]).astype(F32)
    for i in range(count):
        out = (keep, send)[i // 2]
        part = slice(i * n, (i + 1) * n)
        out[i % 2, :n] = total(one_keep[part], one_got[part], one_last[part])
        out[i % 2, n : 2 * n] = total(two_keep[part], two_got[part], two_last[part])
        out[i % 2, 2 * n :] = jnp.broadcast_to(lines[i : i + 1], (16, lines.shape[1])).astype(BF16)


def attend_divide_kernel(first, second, one, two):
    n = one.shape[0] // 4
    lines = []
    for i in range(4):
        part = (first if i < 2 else second)[i % 2]
        one[i * n : (i + 1) * n] = part[:n]
        two[i * n : (i + 1) * n] = part[n : 2 * n]
        lines.append(part[2 * n :].astype(F32)[:1])
    two[4 * n :] = padded(lines).astype(BF16)


def attend_join_kernel(one_a, one_b, two_a, two_b, one, two):
    n = one_a.shape[0]
    one[:n] = one_a[...]
    one[n:] = one_b[...]
    two[:n] = two_a[:n]
    two[n : 2 * n] = two_b[:n]
    lines = jnp.concatenate([two_a[n:].astype(F32)[:4], two_b[n:].astype(F32)[:4]], axis=0)
    two[2 * n :] = fill(lines)


def norm_grad_kernel(chunk, rows, *refs):
    out = refs[-1]
    stations = refs[0].shape[0]
    for r in range(rows):
        out[r] = total(refs[r][chunk], refs[rows][r * stations + chunk], *[a[r] for a in refs[rows + 1 : -1]])


VMEM = pl.BlockSpec(memory_space=pltpu.VMEM)
SMEM = pl.BlockSpec(memory_space=pltpu.SMEM)
HBM = pl.BlockSpec(memory_space=pltpu.HBM)
ANY = pl.BlockSpec(memory_space=pl.ANY)


def call(kernel, ins, outs, scratch=(), us=1.0, limit=16, name=None, scalars=1, specs=None, grid=(), out_specs=None, aliases=None, extra=()):
    count = len(ins)

    def body_of(*refs):
        kernel(*refs[:count], *refs[count + len(extra) :])

    return pl.pallas_call(
        body_of,
        grid=grid,
        in_specs=[SMEM] * scalars + (specs or [VMEM] * (count - scalars)) + [ANY] * len(extra),
        out_specs=out_specs or [VMEM] * len(outs),
        input_output_aliases=aliases or {},
        out_shape=list(outs),
        scratch_shapes=list(scratch),
        compiler_params=pltpu.CompilerParams(vmem_limit_bytes=limit * MIB),
        cost_estimate=pl.CostEstimate(flops=int(us * 1.1e9), bytes_accessed=0, transcendentals=0),
        name=name,
    )(*ins, *extra)


def load(sp, arrays, halved, name, limit=16):
    shapes = [a.shape[:-1] + (a.shape[-1] // (2 if h else 1),) for a, h in zip(arrays, halved)]
    return call(
        functools.partial(load_kernel, halved), [sp] + arrays, [made(s, a.dtype) for s, a in zip(shapes, arrays)],
        scratch=[pltpu.SemaphoreType.DMA] * len(arrays), us=2.0, limit=limit, name=name, specs=[HBM] * len(arrays),
    )


def made(shape, dtype):
    return jax.ShapeDtypeStruct(shape, dtype)


def exchange(array, axis, mask):
    count = lax.axis_size(axis)
    return lax.ppermute(array, axis, [(i, i ^ mask) for i in range(count)])


def merge(kernel, ins, outs, name, extra=()):
    specs = [SMEM if a.dtype == jnp.int32 else VMEM for a in ins]
    return call(kernel, list(ins), list(outs), us=0.05, limit=8, name=name, scalars=0, specs=specs, extra=extra)


def tied(*arrays):
    return lax.optimization_barrier(arrays)


class Chain:
    def __init__(self, token):
        self.token = token

    def __call__(self, function, *args, **kwargs):
        outs = list(function(*args, extra=[self.token], **kwargs))
        self.token = outs[-1]
        return outs

    def hold(self, *arrays):
        *arrays, self.token = tied(*arrays, self.token)
        return arrays


def my_id(bits):
    out = 0
    for axis, mask in bits:
        out = out * 2 + jnp.where((lax.axis_index(axis) & mask) != 0, 1, 0)
    return out


def body(
    tokens, grad_out, crop, offsets, w_query, w_key, w_value, w_out, w_up, w_down, b_query, b_value,
    b_out, b_up, b_down, gain_one, shift_one, gain_two, shift_two,
):
    rows, tok, width = tokens.shape
    seq_count, dp_count = lax.axis_size("seq"), lax.axis_size("dp")
    stations = seq_count // 2
    hidden = w_up.shape[1]
    half = width // 2
    heads = HEADS // 2
    size = half // heads
    chip = 2 * tok
    flat = rows * tok
    small = stations <= 4
    seq = lax.axis_index("seq")
    core, station = seq % 2, seq // 2
    line = lambda v: v.reshape(1, -1)

    dp_bits = [("dp", 1 << i) for i in range(dp_count.bit_length() - 1)]
    st_bits = [("seq", 2 << i) for i in range(stations.bit_length() - 1)]
    bit_x, bit_y = dp_bits[:2]
    rest = dp_bits[2:] + st_bits[2:]
    ids = [my_id([bit_x, bit_y] + st_bits[:2]), my_id([bit_y, bit_x] + st_bits[:2])]
    sp = jnp.stack([core, 1 - core, *ids, station]).astype(jnp.int32)

    mine = lambda a: lax.dynamic_slice_in_dim(a, core * half, half, a.ndim - 1)
    weights = jnp.stack([mine(w_query), mine(w_key), mine(w_value)])
    vectors = jnp.stack([gain_one, shift_one, b_query, b_value] + [jnp.zeros_like(gain_one)] * 4)
    state = []
    kept = [[None] * stations for _ in range(4)]
    blocks = {0: tokens}
    turns = [int(f"{i:0{stations.bit_length() - 1}b}"[::-1], 2) for i in range(stations)]
    for at, j in enumerate(turns):
        if j:
            low = j & -j
            block = blocks[j] = exchange(blocks[j ^ low], "seq", 2 * low)
            if at == 1 or at == stations - 1:
                block, state[-1] = tied(block, state[-1])
                blocks[j] = block
        else:
            block = tokens
        other = exchange(block, "seq", 1)
        first, last = at == 0, at == stations - 1
        ins = [sp, offsets, crop, block, other, vectors, weights] + ([] if first else state)
        outs = [
            made((rows, chip, half), BF16),
            made((rows, chip, half), BF16),
            made((rows, half, chip), BF16),
            made((rows, width, chip), BF16),
        ]
        if first:
            outs += [made((rows * heads, chip, 2 * size), BF16)]
        stat = made((rows * heads, 1, chip), F32)
        acc = made((rows * heads, size, chip), F32)
        if last:
            outs += [stat, acc, made((rows, tok, half), BF16), made((rows, tok, half), BF16)]
        else:
            outs += [stat, stat, acc]
        got = call(
            functools.partial(chunk_kernel, j, last, tok, rows), ins, outs,
            us=0.05, limit=LIMITS[0], name=f"attend_chunk_{j}", scalars=3,
        )
        for where, array in zip(kept, got[:4]):
            where[j] = array
        got = got[4:]
        if first:
            query, got = got[0], got[1:]
        if not last:
            state = [query] + list(got)
        if at == 0:
            sp_b, state[-1] = tied(sp, state[-1])
            tokens_v, g_v, wo, up, down, bo, bu, bd, gain_b, shift_b = load(
                sp_b,
                [tokens, grad_out, w_out, w_up, w_down, line(b_out), line(b_up), line(b_down), line(gain_two), line(shift_two)],
                [False] * 10, "load_feed_forward",
            )
            g_other = exchange(g_v, "seq", 1)
            state[-1], up = tied(state[-1], up)
        if at == 1:
            state[-1], g_other = tied(state[-1], g_other)
            g_other = g_other.reshape(flat, width)
    lse, out_t, att_m, att_o = got
    att_r = exchange(att_o, "seq", 1)

    wide = made((flat, width), F32)
    vec8 = made((8, width), F32)
    mid, normed_two, send, total, back, vec_a = call(
        ffn_first_kernel, [sp, att_m, att_r, wo, tokens_v, g_v, up, down, bo, bu, gain_b, shift_b],
        [wide, made((flat, width), BF16), made((flat, hidden + width), BF16), wide, wide, vec8],
        us=4.0, limit=LIMITS[1], name="feed_forward_a",
    )
    got = exchange(send, "seq", 1)
    outputs, hid_m, pre_m, mid_grad, branch, vec_ffn = call(
        ffn_second_kernel, [sp, mid, normed_two, g_v, up, down, bu, bd, gain_b, total, back, vec_a],
        [made((rows, tok, width), BF16), made((flat, hidden // 2), BF16), made((flat, hidden // 2), BF16), wide,
         made((rows, tok, width), BF16), vec8],
        us=4.0, limit=LIMITS[1], name="feed_forward_b",
    )
    branch_r = exchange(branch, "seq", 1)
    piece = made((PIECES // 2, hidden // 2 // PIECES, width), BF16)
    d_keep, d_send, u_keep, u_send = call(
        ffn_grad_kernel, [sp, hid_m, pre_m, normed_two, got, g_v.reshape(flat, width), g_other],
        [piece, piece, piece, piece],
        us=3.0, limit=LIMITS[2], name="feed_forward_grad",
    )
    d_send, u_send, branch_r = tied(d_send, u_send, branch_r)
    chain = Chain(u_keep)

    q = PIECES // GROUP
    d_got, u_got = exchange(d_send, *bit_x), exchange(u_send, *bit_y)

    sums = []
    dn_m, dn_o, dn_r = [], [], []

    def together(name, *jobs):
        ins = [a for _, arrays, _ in jobs for a in arrays]
        outs = [s for _, _, shapes in jobs for s in shapes]

        def kernel(*refs):
            at, to = 0, len(ins)
            for one, arrays, shapes in jobs:
                one(*refs[at : at + len(arrays)], *refs[to : to + len(shapes)])
                at, to = at + len(arrays), to + len(shapes)

        res = iter(chain(functools.partial(merge, kernel), ins, outs, name))
        return [[next(res) for _ in shapes] for _, _, shapes in jobs]

    def norm_job(chunk, arrived):
        ins = [*dn_m, dn_r, *arrived]
        return (functools.partial(norm_grad_kernel, chunk, rows), ins, [made((rows, tok, width), BF16)])

    for r in range(rows):
        last = r == rows - 1
        arrays = [branch, branch_r, wo, query, lse, out_t, weights] + [a for part in kept for a in part]
        specs = [VMEM] * len(arrays)
        if not small:
            for i, a in enumerate(arrays):
                if a.ndim == 3 and a is not weights:
                    block_shape = (a.shape[0] // rows,) + a.shape[1:]
                    specs[i] = pl.BlockSpec(block_shape, functools.partial(lambda r, i: (r, 0, 0), r))
        tail = list(sums)
        if last:
            tail += [vectors, vec_ffn, *dn_o]
        part = made((stations, tok, width), BF16)
        grads = [made((width, half), F32)] * 3 + [made((half, width), F32), made((8, half), F32)]
        outs = [part, part] + grads
        scratch = []
        if last:
            outs = [part, made((rows * stations, tok, width), BF16)] + [made((width // 2, width), BF16)] * 2 + [made((width // 2 + 16, width), BF16)] * 2
            scratch = [pltpu.VMEM(g.shape, F32) for g in grads] + [pltpu.VMEM((16, width), F32)]
        run = functools.partial(call, functools.partial(attend_back_kernel, stations, tok, r, small, last))
        res = chain(
            run, [sp, offsets, crop] + arrays + tail, outs, scratch=scratch,
            us=BACK_US, limit=LIMITS[3] if small else 48, name=f"attend_back_{r}", scalars=3,
            specs=specs + [VMEM] * len(tail), grid=() if small else (1,),
        )
        dn_m.append(res[0])
        dn_o.append(res[1])
        sums = list(res[2:7])
        if r == rows - 2:
            quarters = made((q,) + piece.shape[1:], BF16)
            ((d_next, u_next),) = together(
                "add_quarters", (upper_kernel, [d_keep, d_got, u_keep, u_got], [quarters, quarters])
            )
            d_got2, u_got2 = exchange(d_next, *bit_y), exchange(u_next, *bit_x)
    one_keep, one_send, two_keep, two_send = res[2:]

    rd = hidden // 2 // PIECES
    n = width // PIECES
    ff_part, at_part = made((2 * rd, width), BF16), made((2 * n + 16, width), BF16)
    two_of = lambda a: made((2,) + a.shape, BF16)
    token_block = made((rows, tok, width), BF16)
    bit_z, bit_w = st_bits[:2]

    def over_rest(part):
        for i, (where, mask) in enumerate(rest):
            got = exchange(part, where, mask)
            ((part,),) = together(f"add_rest_{i}", (sum_kernel, [part, got], [made(part.shape, BF16)]))
        return part

    def unpack(far, d, d_other, u, u_other, before):
        ins = [sp, d, d_other, u, u_other] + before
        scratch = [
            pltpu.VMEM((GROUP, q * rd, width), F32), pltpu.VMEM((GROUP, q * width // PIECES, hidden // 2), F32),
            pltpu.SemaphoreType.DMA((2 * GROUP,)),
        ]
        return chain(
            functools.partial(call, functools.partial(unpack_ffn_kernel, far)), ins,
            [made((hidden, width), F32), made((width, hidden), F32), made((8, 128), F32)], scratch=scratch, us=0.1,
            limit=LIMITS[4], name="unpack_feed_forward", specs=[VMEM] * 4 + [HBM] * len(before),
            out_specs=[HBM] * 2 + [VMEM], aliases={5: 0, 6: 1} if before else None,
        )[:2]

    def other_core(*arrays):
        return [exchange(a, "seq", 1) for a in arrays]

    two_a, two_b = two_of(ff_part), two_of(at_part)
    ((a_keep, a_send),) = together(
        "phase_1", (quarter_kernel, [d_keep, d_got, d_got2, u_keep, u_got, u_got2], [two_a, two_a])
    )
    one_send, two_send, dn_o = chain.hold(one_send, two_send, dn_o[-1])
    a_got = exchange(a_send, *bit_z)
    one_got, two_got = exchange(one_send, *bit_x), exchange(two_send, *bit_y)
    (dn_r,) = chain.hold(*other_core(dn_o))

    one_shape, two_shape = made((4 * n, width), BF16), made((4 * n + 16, width), BF16)
    (a_keep, a_send), (one_next, two_next) = together(
        "phase_2",
        (halve_kernel, [a_keep, a_got], [ff_part] * 2),
        (attend_upper_kernel, [one_keep, one_got, two_keep, two_got], [one_shape, two_shape]),
    )
    a_got = exchange(a_send, *bit_w)
    one_got2, two_got2 = exchange(one_next, *bit_y), exchange(two_next, *bit_x)

    (a_own,), (b_keep, b_send) = together(
        "phase_3",
        (sum_kernel, [a_keep, a_got], [ff_part]),
        (attend_quarter_kernel, [one_keep, one_got, one_got2, two_keep, two_got, two_got2], [two_b, two_b]),
    )
    a_own = over_rest(a_own)
    a_near = exchange(a_own, *bit_w)
    b_got = exchange(b_send, *bit_z)

    (a_pair,), (b_keep, b_send) = together(
        "phase_4",
        (pair_kernel, [a_own, a_near], [two_a]),
        (halve_kernel, [b_keep, b_got], [at_part] * 2),
    )
    a_far = exchange(a_pair, *bit_z)
    b_got = exchange(b_send, *bit_w)

    arrived = {c: [] for c in range(stations)}
    top = stations // 2
    inner = [c for c in reversed(turns) if c not in (0, 1, top)]
    for c in inner[:-1]:
        ((moving,),) = together("norm_step", norm_job(c, arrived[c]))
        arrived[c & (c - 1)].append(exchange(moving, "seq", 2 * (c & -c)))
    c = inner[-1]
    (d_mine, u_mine), (b_own,), (moving,) = together(
        "phase_5",
        (divide_kernel, [a_pair, a_far], [quarters, quarters]),
        (sum_kernel, [b_keep, b_got], [at_part]),
        norm_job(c, arrived[c]),
    )
    b_own = over_rest(b_own)
    d_y, u_x = exchange(d_mine, *bit_y), exchange(u_mine, *bit_x)
    b_near = exchange(b_own, *bit_w)
    (moving,) = chain.hold(exchange(moving, "seq", 2 * (c & -c)))
    arrived[c & (c - 1)].append(moving)

    (d_near, u_near), (b_pair,), (moving,) = together(
        "phase_6",
        (join_kernel, [d_mine, d_y, u_mine, u_x], [piece, piece]),
        (pair_kernel, [b_own, b_near], [two_b]),
        norm_job(top, arrived[top]),
    )
    d_far, u_far = exchange(d_near, *bit_x), exchange(u_near, *bit_y)
    b_far = exchange(b_pair, *bit_z)
    moving = exchange(moving, "seq", 2 * top)
    d_far, u_far = chain.hold(d_far, u_far)

    (one_mine, two_mine), (nearest,) = together(
        "phase_7", (attend_divide_kernel, [b_pair, b_far], [one_shape, two_shape]), norm_job(1, [])
    )
    one_y, two_x = exchange(one_mine, *bit_y), exchange(two_mine, *bit_x)
    nearest = exchange(chain.hold(nearest)[0], "seq", 2)
    (moving,) = chain.hold(moving)
    ((one_near, two_near),) = together(
        "phase_8",
        (
            attend_join_kernel, [one_mine, one_y, two_mine, two_x],
            [made((8 * n, width), BF16), made((8 * n + 16, width), BF16)],
        ),
    )
    one_far, two_far = exchange(one_near, *bit_x), exchange(two_near, *bit_y)
    d_near, u_near = chain.hold(d_near, u_near)
    d_near_o, u_near_o = chain.hold(*other_core(d_near, u_near))
    grad_down, grad_up = unpack(False, d_near, d_near_o, u_near, u_near_o, [])
    d_far_o, u_far_o = chain.hold(*other_core(d_far, u_far))
    grad_down, grad_up = unpack(True, d_far, d_far_o, u_far, u_far_o, [grad_down, grad_up])
    far_held = chain.hold(one_far, two_far, nearest)
    nearest = far_held[2]
    one_near_o, two_near_o = other_core(*chain.hold(one_near, two_near))
    one_far_o, two_far_o = other_core(*far_held[:2])
    input_grad = call(
        last_kernel, [tokens_v, vectors, mid_grad, *dn_m, dn_r, *arrived[0], moving, nearest], [token_block],
        us=0.1, limit=LIMITS[4], name="input_grad", scalars=0, extra=[chain.token],
    )[0]
    one_all = [one_near, one_far, one_near_o, one_far_o]
    two_all = [two_near, two_far, two_near_o, two_far_o]
    square = made((width, width), F32)
    run = functools.partial(call, unpack_attend_kernel)
    thin = made((1, width), F32)
    results = chain(
        run, [sp] + one_all + two_all, [square] * 4 + [thin] * 3 + [made((1, hidden), F32)] + [thin] * 5,
        scratch=[pltpu.VMEM((PIECES, width), F32)], us=0.1, limit=LIMITS[4], name="unpack_attend",
    )
    grad_query, grad_key, grad_value, grad_out_proj = results[:4]
    lines = [r.reshape(-1) for r in results[4:]]

    return (outputs, input_grad, grad_query, grad_key, grad_value, grad_out_proj, grad_up, grad_down, *lines)


def solution(mesh):
    split, row, copied = P("dp", "seq", None), P("dp"), P()
    return jax.shard_map(
        body,
        mesh=mesh,
        in_specs=(split, split, row, P("dp", None)) + (copied,) * 15,
        out_specs=(split, split) + (copied,) * 15,
        check_vma=False,
    )
```

```python
import functools

import jax
import jax.numpy as jnp
from jax import lax
from jax.experimental import pallas as pl
from jax.experimental.pallas import tpu as pltpu
from jax.sharding import PartitionSpec as P

HEADS = 8
EPSILON = 1e-06
MASKED = -1e30
MIB = 1024 * 1024
LIMITS = (16, 20, 20, 26, 20)
PIECES = 16
GROUP = 4
BACK_US = 0.05
BF16 = jnp.bfloat16
F32 = jnp.float32
GELU_C = 0.7978845608028654
GELU_A = 0.044715


def nn(a, b):
    return jnp.dot(a, b, preferred_element_type=F32)


def nt(a, b):
    return lax.dot_general(a, b, (((1,), (1,)), ((), ())), preferred_element_type=F32)


def tn(a, b):
    return lax.dot_general(a, b, (((0,), (0,)), ((), ())), preferred_element_type=F32)


def normalize(values):
    center = values - jnp.mean(values, axis=-1, keepdims=True)
    scale = lax.rsqrt(jnp.mean(center * center, axis=-1, keepdims=True) + EPSILON)
    return center * scale, scale


def norm_back(cotangent, unit, scale, gain):
    g = cotangent * gain
    return scale * (
        g
        - jnp.mean(g, axis=-1, keepdims=True)
        - unit * jnp.mean(g * unit, axis=-1, keepdims=True)
    )


def segments(pos, offsets, crop, row):
    count = offsets.shape[1]
    seg = jnp.zeros(pos.shape, jnp.int32)
    for j in range(count):
        seg += (pos >= offsets[row, j]).astype(jnp.int32)
    return seg + count * (pos >= crop[row]).astype(jnp.int32)


def positions(sp, chunk, tok, shape, dim):
    start = (sp[4] ^ chunk) * (2 * tok)
    i = lax.broadcasted_iota(jnp.int32, shape, dim)
    return i + jnp.where(i < tok, start + sp[0] * tok, start + sp[1] * tok - tok)


def half_of(which, width):
    return pl.ds(pl.multiple_of(which * width, 128), width)


def padded(lines):
    return jnp.concatenate(lines + [jnp.zeros((16 - len(lines), lines[0].shape[1]), F32)], axis=0)


def load_kernel(halved, sp, *refs):
    count = len(halved)
    sources, targets, sems = refs[:count], refs[count : 2 * count], refs[2 * count :]
    copies = []
    for half, source, target, sem in zip(halved, sources, targets, sems):
        if half:
            source = source.at[:, half_of(sp[0], source.shape[1] // 2)]
        copies.append(pltpu.make_async_copy(source, target, sem))
    for copy in copies:
        copy.start()
    for copy in copies:
        copy.wait()


def chunk_kernel(chunk, last, tok, rows, *refs):
    refs = list(refs)
    first = chunk == 0
    sp, offsets, crop, xm, xo, vectors, weights = refs[:7]
    refs = refs[7:]
    if not first:
        qm_in, m_in, l_in, acc_in = refs[:4]
        refs = refs[4:]
    k_out, v_out, kt_out, nt_out = refs[:4]
    refs = refs[4:]
    if first:
        qm_out = refs.pop(0)
    if last:
        lse_out, ot_out, att_m, att_o = refs[:4]
    else:
        m_out, l_out, acc_out = refs
    half = weights.shape[2]
    heads = HEADS // 2
    size = half // heads
    chip = 2 * tok
    for at, x in ((0, xm), (tok, xo)):
        values = x[...].reshape(rows * tok, -1).astype(F32)
        unit, _ = normalize(values)
        normed = unit * vectors[0:1, :] + vectors[1:2, :]
        low = normed.astype(BF16)
        k = nn(low, weights[1])
        v = (nn(low, weights[2]) + vectors[3:4, half_of(sp[0], half)]).astype(BF16)
        if first:
            q = ((nn(low, weights[0]) + vectors[2:3, half_of(sp[0], half)]).astype(BF16).astype(F32) * size**-0.5).astype(BF16)
            lane = lax.broadcasted_iota(jnp.int32, (tok, 2 * size), 1)
        for r in range(rows):
            part = slice(r * tok, (r + 1) * tok)
            k_out[r, at : at + tok, :] = k[part].astype(BF16)
            v_out[r, at : at + tok, :] = v[part]
            kt_out[r, :, at : at + tok] = k[part].T.astype(BF16)
            nt_out[r, :, at : at + tok] = normed[part].T.astype(BF16)
            if first:
                for h in range(heads):
                    pair = q[part, (h // 2) * 2 * size : (h // 2 + 1) * 2 * size]
                    keep = (lane >= size) if h % 2 else (lane < size)
                    qm_out[r * heads + h, at : at + tok, :] = jnp.where(keep, pair, jnp.zeros_like(pair))
    qm = qm_out if first else qm_in
    for r in range(rows):
        key_seg = segments(positions(sp, chunk, tok, (chip, chip), 0), offsets, crop, r)
        query_seg = segments(positions(sp, 0, tok, (1, chip), 1), offsets, crop, r)
        bias = jnp.where(key_seg == query_seg, 0.0, MASKED)
        outs = []
        spot = [r * heads + h for h in range(heads)]
        pairs = [slice((h // 2) * 2 * size, (h // 2 + 1) * 2 * size) for h in range(heads)]
        s = [nt(k_out[r, :, pairs[h]], qm[spot[h]]) + bias for h in range(heads)]
        tops = [jnp.max(a, axis=0, keepdims=True) for a in s]
        if not first:
            olds = [m_in[at] for at in spot]
            tops = [jnp.maximum(a, b) for a, b in zip(olds, tops)]
        p = [jnp.exp(a - b) for a, b in zip(s, tops)]
        totals = [jnp.sum(a, axis=0, keepdims=True) for a in p]
        addeds = [tn(v_out[r, :, pairs[h]], p[h].astype(BF16)) for h in range(heads)]
        for h, at in enumerate(spot):
            added = addeds[h][(h % 2) * size : (h % 2 + 1) * size]
            total = totals[h]
            if not first:
                keep = jnp.exp(olds[h] - tops[h])
                total += l_in[at] * keep
                added += acc_in[at] * keep
            if last:
                lse_out[at] = tops[h] + jnp.log(total)
                out = added / total
                ot_out[at] = out
                outs.append(out)
            else:
                m_out[at] = tops[h]
                l_out[at] = total
                acc_out[at] = added
        if last:
            att = jnp.concatenate(outs, axis=0).T.astype(BF16)
            att_m[r] = att[:tok]
            att_o[r] = att[tok:]


def feed_forward_half(sp, which, normed, g, up, down, bup, hid, pre, at, vec, total, back):
    half = up.shape[1] // 2
    row = min(512, half)
    block = min(512, row)
    count = half // block
    cols = [pl.ds(pl.multiple_of(sp[which] * half + j * block, 128), block) for j in range(count)]
    for first in range(0, count, 2):
        js = range(first, min(first + 2, count))
        us = [nn(normed, up[:, cols[j]]) + bup[:, cols[j]] for j in js]
        gs = [nt(g, down[cols[j], :]) for j in js]
        outs, pres = [], []
        for j, u, back_in in zip(js, us, gs):
            square = u * u
            plus = 1.0 + jnp.tanh(u * (GELU_C + GELU_C * GELU_A * square))
            low = 0.5 * u
            hidden = (low * plus).astype(BF16)
            slope = plus * (0.5 + low * (2.0 - plus) * (GELU_C + 3 * GELU_C * GELU_A * square))
            grad = (back_in * slope).astype(BF16)
            hid[:, j * block : (j + 1) * block] = hidden
            pre[:, at + j * block : at + (j + 1) * block] = grad
            outs.append(hidden)
            pres.append(grad)
            line = jnp.sum(grad.astype(F32), axis=0, keepdims=True)
            lane = j * block % row
            vec[pl.ds(sp[which] * (half // row) + j * block // row, 1), lane : lane + block] = line
        for j, hidden, grad in zip(js, outs, pres):
            more, less = nn(hidden, down[cols[j], :]), nt(grad, up[:, cols[j]])
            total = more if total is None else total + more
            back = less if back is None else back + less
    return total, back


def ffn_first_kernel(
    sp, att_m, att_o, wo, tokens, cot, up, down, b_out, bup, gain, shift, mid_out, normed_out, send, total_out, back_out, vec
):
    rows, tok, width = tokens.shape
    flat = rows * tok
    quarter = width // 2
    mine = pl.ds(pl.multiple_of(sp[0] * quarter, 128), quarter)
    other = pl.ds(pl.multiple_of(sp[1] * quarter, 128), quarter)
    mid = (
        tokens[...].reshape(flat, width).astype(F32)
        + nn(att_m[...].reshape(flat, -1), wo[mine, :])
        + nn(att_o[...].reshape(flat, -1), wo[other, :])
        + b_out[...]
    )
    mid_out[...] = mid
    unit, _ = normalize(mid)
    normed = (unit * gain[...] + shift[...]).astype(BF16)
    normed_out[...] = normed
    half = up.shape[1] // 2
    send[:, 2 * half :] = normed
    vec[...] = jnp.zeros_like(vec)
    g = cot[...].reshape(flat, width)
    total_out[...], back_out[...] = feed_forward_half(
        sp, 1, normed, g, up, down, bup, send, send, half, vec, None, None
    )


def ffn_second_kernel(
    sp, mid_in, normed_in, cot, up, down, bup, b_down, gain, total_in, back_in, vec_in, out, hid, pre, mid_grad, branch, vec
):
    rows, tok, width = cot.shape
    flat = rows * tok
    g = cot[...].reshape(flat, width)
    vec[...] = vec_in[...]
    total, back = feed_forward_half(
        sp, 0, normed_in[...], g, up, down, bup, hid, pre, 0, vec, total_in[...], back_in[...]
    )
    mid = mid_in[...]
    out[...] = (mid + total + b_down[...]).astype(BF16).reshape(rows, tok, width)
    unit, scale = normalize(mid)
    gf = g.astype(F32)
    grad = gf + norm_back(back, unit, scale, gain[...])
    mid_grad[...] = grad
    low = grad.astype(BF16)
    branch[...] = low.reshape(rows, tok, width)
    vec[4:5, :] = jnp.sum(gf, axis=0, keepdims=True)
    vec[5:6, :] = jnp.sum(back * unit, axis=0, keepdims=True)
    vec[6:7, :] = jnp.sum(back, axis=0, keepdims=True)
    vec[7:8, :] = jnp.sum(low.astype(F32), axis=0, keepdims=True)


def ffn_grad_kernel(send, sp, hid_m, pre_m, n_m, got, g_m, g_o, d, u):
    half = hid_m.shape[1]
    width = g_m.shape[1]
    per = PIECES // 2
    rd, ru = half // PIECES, width // PIECES
    part = (sp[2] // per) ^ send
    cols = half_of(part, half // 2)
    gd = tn(hid_m[:, cols], g_m[...]) + tn(got[:, cols], g_o[...])
    part = (sp[3] // per) ^ send
    own = half_of(part, width // 2)
    others = pl.ds(pl.multiple_of(2 * half + part * (width // 2), 128), width // 2)
    gu = tn(n_m[:, own], pre_m[...]) + tn(got[:, others], got[:, half : 2 * half])
    for p in range(per):
        d[(sp[2] & (per - 1)) ^ p] = gd[p * rd : (p + 1) * rd].astype(BF16)
        at = (sp[3] & (per - 1)) ^ p
        for i in range(half // width):
            u[at, i * ru : (i + 1) * ru, :] = gu[p * ru : (p + 1) * ru, i * width : (i + 1) * width].astype(BF16)


def attend_back_kernel(stations, tok, rows_here, whole, last, *refs):
    refs = list(refs)

    def take(count):
        got = refs[:count]
        del refs[:count]
        return got

    sp, offsets, crop, br_m, br_o, wo, qm, lse, ot, weights = take(10)
    k, v, kt, norm_t = (take(stations) for _ in range(4))
    sums_in = take(5) if rows_here[0] else None
    if last:
        vectors, vec_in = take(2)
        before = take(rows_here[0])
    dn_m = take(len(rows_here))
    dn_o = take(1 if last else len(rows_here))
    if last:
        ones, twos = take(2), take(2)
    gq, gk, gv, go, sums = take(5)
    heads = HEADS // 2
    _, width, half = weights.shape
    size = half // heads
    chip = 2 * tok
    block = min(4, stations)
    blocks = stations // block

    made_here = [0.0] * 5
    for place, row in enumerate(rows_here):
        at = row if whole else 0
        branch = jnp.concatenate([br_m[at], br_o[at]], axis=0)
        do = nt(branch, wo[half_of(sp[0], half), :])
        dot = do.T
        do = do.astype(BF16)
        lane = lax.broadcasted_iota(jnp.int32, (chip, 2 * size), 1)
        head_at = at * heads
        out_t = jnp.concatenate([ot[head_at + h] for h in range(heads)], axis=0).astype(BF16)
        go_row = nn(out_t, branch)
        query_seg = segments(positions(sp, 0, tok, (1, chip), 1), offsets, crop, row)
        biases = []
        for chunk in range(stations):
            key_seg = segments(positions(sp, chunk, tok, (chip, chip), 0), offsets, crop, row)
            biases.append(jnp.where(key_seg == query_seg, 0.0, MASKED))
        dqt = []
        dks = [[] for _ in range(blocks)]
        dvs = [[] for _ in range(blocks)]
        for pair in range(heads // 2):
            lanes = slice(pair * 2 * size, (pair + 1) * 2 * size)
            dk = [None] * blocks
            dv = [None] * blocks
            for h in (2 * pair, 2 * pair + 1):
                wide = do[:, lanes]
                dm = jnp.where((lane >= size) if h % 2 else (lane < size), wide, jnp.zeros_like(wide))
                delta = jnp.sum(ot[head_at + h] * dot[h * size : (h + 1) * size], axis=0, keepdims=True)
                dq = None
                for b in range(blocks):
                    chunks = range(b * block, (b + 1) * block)
                    keys = jnp.concatenate([k[c][at, :, lanes] for c in chunks], axis=0)
                    values = jnp.concatenate([v[c][at, :, lanes] for c in chunks], axis=0)
                    keys_t = jnp.concatenate([kt[c][at, h * size : (h + 1) * size, :] for c in chunks], axis=1)
                    bias = jnp.concatenate([biases[c] for c in chunks], axis=0)
                    p = jnp.exp(nt(keys, qm[head_at + h]) + bias - lse[head_at + h])
                    ds = (p * (nt(values, dm) - delta)).astype(BF16)
                    dv_h, dk_h = nn(p.astype(BF16), dm), nn(ds, qm[head_at + h])
                    dv[b] = dv_h if dv[b] is None else dv[b] + dv_h
                    dk[b] = dk_h if dk[b] is None else dk[b] + dk_h
                    more = nn(keys_t, ds)
                    dq = more if dq is None else dq + more
                dqt.append(dq)
            for b in range(blocks):
                dks[b].append(dk[b].astype(BF16))
                dvs[b].append(dv[b].astype(BF16))
        dq = (jnp.concatenate(dqt, axis=0) * size**-0.5).T.astype(BF16)
        gq_row = nn(norm_t[0][at], dq)
        gk_row = gv_row = sum_k = sum_v = 0.0
        for b in range(blocks):
            dk = jnp.concatenate(dks[b], axis=1)
            dv = jnp.concatenate(dvs[b], axis=1)
            normed = jnp.concatenate([norm_t[c][at] for c in range(b * block, (b + 1) * block)], axis=1)
            gk_row += nn(normed, dk)
            gv_row += nn(normed, dv)
            sum_k += jnp.sum(dk.astype(F32), axis=0, keepdims=True)
            sum_v += jnp.sum(dv.astype(F32), axis=0, keepdims=True)
            dn = nt(dk, weights[1]) + nt(dv, weights[2])
            for i in range(block):
                part = dn[i * chip : (i + 1) * chip]
                if b + i == 0:
                    part += nt(dq, weights[0])
                dn_m[place][b * block + i] = part[:tok].astype(BF16)
                dn_o[0 if last else place][(row * stations if last else 0) + b * block + i] = part[tok:].astype(BF16)
        sum_q = jnp.sum(dq.astype(F32), axis=0, keepdims=True)
        rest = jnp.zeros((5, half), F32)
        values = (gq_row, gk_row, gv_row, go_row, jnp.concatenate([sum_q, sum_v, sum_k, rest]))
        made_here = [a + b for a, b in zip(made_here, values)]
    for i, (ref, value) in enumerate(zip((gq, gk, gv, go, sums), made_here)):
        ref[...] = value if sums_in is None else value + sums_in[i][...]
    if not last:
        return

    for r, part in enumerate(before):
        dn_o[0][r * stations : (r + 1) * stations] = part[...]
    vec = refs[0]
    lane = lax.broadcasted_iota(jnp.int32, (2, width), 1)
    both = sums[0:2, :]
    both = jnp.concatenate([both, both], axis=1)
    vec[0:2, :] = jnp.where((lane >= half) == (sp[0] == 1), both, 0.0)
    vec[2:3, :] = vec_in[7:8, :]
    vec[3:4, :] = vec_in[4:5, :]
    vec[4:8, :] = vec_in[0:4, :]
    vec[10:12, :] = vec_in[5:7, :]
    vec[12:16, :] = jnp.zeros((4, width), F32)
    wide = [weights[i].astype(F32) for i in range(3)]
    shifts = sum(w * sums[i : i + 1, :] for w, i in zip(wide, (0, 2, 1)))
    gains = sum(w * g[...] for w, g in zip(wide, (gq, gk, gv)))

    def across(values):
        folded = sum(values[:, i * 128 : (i + 1) * 128] for i in range(half // 128))
        return jnp.sum(folded.T, axis=0, keepdims=True)

    shift_grad = across(shifts)
    vec[9:10, :] = shift_grad
    vec[8:9, :] = (across(gains) - vectors[1:2, :] * shift_grad) / vectors[0:1, :]
    n = width // PIECES
    low = n // 2
    per = PIECES // 2
    for slot in range(PIECES):
        one, two = ones[slot // per], twos[slot // per]
        base = slot % per * n
        piece = sp[2] ^ slot
        part = pl.ds(pl.multiple_of(piece * n, n), n)
        one[base : base + n, :half] = gq[part, :].astype(BF16)
        one[base : base + n, half:] = gk[part, :].astype(BF16)
        piece = sp[3] ^ slot
        first = pl.ds(pl.multiple_of(piece * n, n), low)
        second = pl.ds(pl.multiple_of(piece * n + low, low), low)
        two[base : base + low, :half] = gv[first, :].astype(BF16)
        two[base : base + low, half:] = gv[second, :].astype(BF16)
        two[base + low : base + n, :] = go[pl.ds(pl.multiple_of(piece * low, low), low), :].astype(BF16)
    for i, two in enumerate(twos):
        lines = [vec[pl.ds(sp[3] ^ (i * per + s), 1), :] for s in range(per)]
        two[per * n :, :] = padded(lines).astype(BF16)


def last_kernel(tokens, gain, mid_grad, *refs):
    out = refs[-1]
    rows, tok, width = tokens.shape
    flat = rows * tok
    unit, scale = normalize(tokens[...].reshape(flat, width).astype(F32))
    parts = []
    for r in range(rows):
        part = refs[r][0].astype(F32) + refs[rows][r * refs[0].shape[0]].astype(F32)
        for arrived in refs[rows + 1 : -1]:
            part += arrived[r].astype(F32)
        parts.append(part)
    grad = mid_grad[...] + norm_back(jnp.concatenate(parts, axis=0), unit, scale, gain[0:1, :])
    out[...] = grad.astype(BF16).reshape(rows, tok, width)


def unpack_ffn_kernel(far, sp, *refs):
    refs = list(refs)
    d_both, u_both = refs[0:2], refs[2:4]
    down, up, done, d_wide, u_wide, sems = refs[-6:]
    done[...] = jnp.zeros_like(done)
    _, rd, width = d_both[0].shape
    ru = up.shape[0] // PIECES
    half = down.shape[0] // 2
    count = PIECES // GROUP
    copies = []
    for which in range(2):
        for i in range(GROUP // 2):
            at = which * (GROUP // 2) + i
            group = (GROUP // 2 if far else 0) + i
            for k in range(count):
                slot = i * count + k
                place = (sp[2] ^ k) & (count - 1)
                rows = pl.ds(pl.multiple_of(place * rd, rd), rd)
                d_wide[at, rows, :] = d_both[which][slot].astype(F32)
                place = (sp[3] ^ k) & (count - 1)
                rows = pl.ds(pl.multiple_of(place * ru, ru), ru)
                for n in range(rd // ru):
                    part = u_both[which][slot, n * ru : (n + 1) * ru, :]
                    u_wide[at, rows, n * width : (n + 1) * width] = part.astype(F32)
            size = count * rd
            rows = pl.ds(pl.multiple_of(sp[which] * half + ((sp[2] // count) ^ group) * size, size), size)
            copies.append(pltpu.make_async_copy(d_wide.at[at], down.at[rows, :], sems.at[2 * at]))
            copies[-1].start()
            size = count * ru
            rows = pl.ds(pl.multiple_of(((sp[3] // count) ^ group) * size, size), size)
            copies.append(pltpu.make_async_copy(u_wide.at[at], up.at[rows, half_of(sp[which], half)], sems.at[2 * at + 1]))
            copies[-1].start()
    for copy in copies:
        copy.wait()


def unpack_attend_kernel(sp, *refs):
    gq, gk, gv, go, *lines = refs[8:]
    vec = lines.pop()
    ones, twos = (refs[0:2], refs[2:4]), (refs[4:6], refs[6:8])
    width = gq.shape[0]
    half = width // 2
    n = width // PIECES
    low = n // 2
    per = PIECES // 2
    for slot in range(PIECES):
        base = slot % per * n
        for which in range(2):
            one, two = ones[which][slot // per], twos[which][slot // per]
            cols = half_of(sp[which], half)
            piece = sp[2] ^ slot
            rows = pl.ds(pl.multiple_of(piece * n, n), n)
            gq[rows, cols] = one[base : base + n, :half].astype(F32)
            gk[rows, cols] = one[base : base + n, half:].astype(F32)
            piece = sp[3] ^ slot
            first = pl.ds(pl.multiple_of(piece * n, n), low)
            second = pl.ds(pl.multiple_of(piece * n + low, low), low)
            gv[first, cols] = two[base : base + low, :half].astype(F32)
            gv[second, cols] = two[base : base + low, half:].astype(F32)
            out_rows = pl.ds(pl.multiple_of(sp[which] * half + piece * low, low), low)
            go[out_rows, :] = two[base + low : base + n, :].astype(F32)
    for side in range(2):
        both = twos[0][side][per * n :, :].astype(F32) + twos[1][side][per * n :, :].astype(F32)
        for s in range(per):
            vec[pl.ds(sp[3] ^ (side * per + s), 1), :] = both[s : s + 1]
    for line, row in zip(lines, (0, 1, 2, 4, 3, 8, 9, 10, 11)):
        count = line.shape[1] // width
        for i in range(count):
            line[:, i * width : (i + 1) * width] = vec[row + i : row + i + 1, :]


def total(*values):
    return sum(v.astype(F32) for v in values).astype(BF16)


def sum_kernel(*refs):
    refs[-1][...] = total(*[r[...] for r in refs[:-1]])


def upper_kernel(*refs):
    count = len(refs) // 3
    for i, out in enumerate(refs[2 * count :]):
        keep, got = refs[2 * i : 2 * i + 2]
        half = keep.shape[0] // 2
        out[...] = total(keep[half:], got[half:])


def quarter_kernel(d_keep, d_got, d_last, u_keep, u_got, u_last, keep, send):
    rd = d_keep.shape[1]
    half = keep.shape[0]
    for i in range(2 * half):
        out = send if i >= half else keep
        out[i % half, :rd] = total(d_keep[i], d_got[i], d_last[i])
        out[i % half, rd:] = total(u_keep[i], u_got[i], u_last[i])


def halve_kernel(keep, got, out_keep, out_send):
    out_keep[...] = total(keep[0], got[0])
    out_send[...] = total(keep[1], got[1])


def pair_kernel(one, two, out):
    out[0] = one[...]
    out[1] = two[...]


def divide_kernel(one, two, d, u):
    rd = d.shape[1]
    for i in range(d.shape[0]):
        part = (one if i < 2 else two)[i % 2]
        d[i] = part[:rd]
        u[i] = part[rd:]


def join_kernel(*refs):
    count = len(refs) // 3
    for i, out in enumerate(refs[2 * count :]):
        one, two = refs[2 * i : 2 * i + 2]
        out[: one.shape[0]] = one[...]
        out[one.shape[0] :] = two[...]


def attend_upper_kernel(one_keep, one_got, two_keep, two_got, one, two):
    n = one.shape[0]
    one[...] = total(one_keep[n:], one_got[n:])
    two[:n] = total(two_keep[n : 2 * n], two_got[n : 2 * n])
    lines = total(two_keep[2 * n :], two_got[2 * n :]).astype(F32)
    two[n:] = fill(lines[4:8])


def fill(lines):
    return jnp.concatenate([lines, jnp.zeros((16 - lines.shape[0], lines.shape[1]), F32)], axis=0).astype(BF16)


def attend_quarter_kernel(one_keep, one_got, one_last, two_keep, two_got, two_last, keep, send):
    count = 2 * keep.shape[0]
    n = one_last.shape[0] // count
    lines = total(two_keep[2 * count * n :], two_got[2 * count * n :], two_last[count * n :]).astype(F32)
    for i in range(count):
        out = (keep, send)[i // 2]
        part = slice(i * n, (i + 1) * n)
        out[i % 2, :n] = total(one_keep[part], one_got[part], one_last[part])
        out[i % 2, n : 2 * n] = total(two_keep[part], two_got[part], two_last[part])
        out[i % 2, 2 * n :] = jnp.broadcast_to(lines[i : i + 1], (16, lines.shape[1])).astype(BF16)


def attend_divide_kernel(first, second, one, two):
    n = one.shape[0] // 4
    lines = []
    for i in range(4):
        part = (first if i < 2 else second)[i % 2]
        one[i * n : (i + 1) * n] = part[:n]
        two[i * n : (i + 1) * n] = part[n : 2 * n]
        lines.append(part[2 * n :].astype(F32)[:1])
    two[4 * n :] = padded(lines).astype(BF16)


def attend_join_kernel(one_a, one_b, two_a, two_b, one, two):
    n = one_a.shape[0]
    one[:n] = one_a[...]
    one[n:] = one_b[...]
    two[:n] = two_a[:n]
    two[n : 2 * n] = two_b[:n]
    lines = jnp.concatenate([two_a[n:].astype(F32)[:4], two_b[n:].astype(F32)[:4]], axis=0)
    two[2 * n :] = fill(lines)


def norm_grad_kernel(chunk, rows, *refs):
    out = refs[-1]
    stations = refs[0].shape[0]
    for r in range(rows):
        out[r] = total(refs[r][chunk], refs[rows][r * stations + chunk], *[a[r] for a in refs[rows + 1 : -1]])


VMEM = pl.BlockSpec(memory_space=pltpu.VMEM)
SMEM = pl.BlockSpec(memory_space=pltpu.SMEM)
HBM = pl.BlockSpec(memory_space=pltpu.HBM)
ANY = pl.BlockSpec(memory_space=pl.ANY)


def call(kernel, ins, outs, scratch=(), us=1.0, limit=16, name=None, scalars=1, specs=None, grid=(), out_specs=None, aliases=None, extra=()):
    count = len(ins)

    def body_of(*refs):
        kernel(*refs[:count], *refs[count + len(extra) :])

    return pl.pallas_call(
        body_of,
        grid=grid,
        in_specs=[SMEM] * scalars + (specs or [VMEM] * (count - scalars)) + [ANY] * len(extra),
        out_specs=out_specs or [VMEM] * len(outs),
        input_output_aliases=aliases or {},
        out_shape=list(outs),
        scratch_shapes=list(scratch),
        compiler_params=pltpu.CompilerParams(vmem_limit_bytes=limit * MIB),
        cost_estimate=pl.CostEstimate(flops=int(us * 1.1e9), bytes_accessed=0, transcendentals=0),
        name=name,
    )(*ins, *extra)


def load(sp, arrays, halved, name, limit=16):
    shapes = [a.shape[:-1] + (a.shape[-1] // (2 if h else 1),) for a, h in zip(arrays, halved)]
    return call(
        functools.partial(load_kernel, halved), [sp] + arrays, [made(s, a.dtype) for s, a in zip(shapes, arrays)],
        scratch=[pltpu.SemaphoreType.DMA] * len(arrays), us=2.0, limit=limit, name=name, specs=[HBM] * len(arrays),
    )


def made(shape, dtype):
    return jax.ShapeDtypeStruct(shape, dtype)


def exchange(array, axis, mask):
    count = lax.axis_size(axis)
    return lax.ppermute(array, axis, [(i, i ^ mask) for i in range(count)])


def merge(kernel, ins, outs, name, extra=()):
    specs = [SMEM if a.dtype == jnp.int32 else VMEM for a in ins]
    return call(kernel, list(ins), list(outs), us=0.05, limit=8, name=name, scalars=0, specs=specs, extra=extra)


def tied(*arrays):
    return lax.optimization_barrier(arrays)


class Chain:
    def __init__(self, token):
        self.token = token

    def __call__(self, function, *args, **kwargs):
        outs = list(function(*args, extra=[self.token], **kwargs))
        self.token = outs[-1]
        return outs

    def hold(self, *arrays):
        *arrays, self.token = tied(*arrays, self.token)
        return arrays


def my_id(bits):
    out = 0
    for axis, mask in bits:
        out = out * 2 + jnp.where((lax.axis_index(axis) & mask) != 0, 1, 0)
    return out


def body(
    tokens, grad_out, crop, offsets, w_query, w_key, w_value, w_out, w_up, w_down, b_query, b_value,
    b_out, b_up, b_down, gain_one, shift_one, gain_two, shift_two,
):
    rows, tok, width = tokens.shape
    seq_count, dp_count = lax.axis_size("seq"), lax.axis_size("dp")
    stations = seq_count // 2
    hidden = w_up.shape[1]
    half = width // 2
    heads = HEADS // 2
    size = half // heads
    chip = 2 * tok
    flat = rows * tok
    small = stations <= 4
    seq = lax.axis_index("seq")
    core, station = seq % 2, seq // 2
    line = lambda v: v.reshape(1, -1)

    dp_bits = [("dp", 1 << i) for i in range(dp_count.bit_length() - 1)]
    st_bits = [("seq", 2 << i) for i in range(stations.bit_length() - 1)]
    bit_x, bit_y = dp_bits[:2]
    rest = dp_bits[2:] + st_bits[2:]
    ids = [my_id([bit_x, bit_y] + st_bits[:2]), my_id([bit_y, bit_x] + st_bits[:2])]
    sp = jnp.stack([core, 1 - core, *ids, station]).astype(jnp.int32)

    mine = lambda a: lax.dynamic_slice_in_dim(a, core * half, half, a.ndim - 1)
    weights = jnp.stack([mine(w_query), mine(w_key), mine(w_value)])
    vectors = jnp.stack([gain_one, shift_one, b_query, b_value] + [jnp.zeros_like(gain_one)] * 4)
    state = []
    kept = [[None] * stations for _ in range(4)]
    blocks = {0: tokens}
    turns = [int(f"{i:0{stations.bit_length() - 1}b}"[::-1], 2) for i in range(stations)]
    for at, j in enumerate(turns):
        if j:
            low = j & -j
            block = blocks[j] = exchange(blocks[j ^ low], "seq", 2 * low)
            if at == 1 or at == stations - 1:
                block, state[-1] = tied(block, state[-1])
                blocks[j] = block
        else:
            block = tokens
        other = exchange(block, "seq", 1)
        first, last = at == 0, at == stations - 1
        ins = [sp, offsets, crop, block, other, vectors, weights] + ([] if first else state)
        outs = [
            made((rows, chip, half), BF16),
            made((rows, chip, half), BF16),
            made((rows, half, chip), BF16),
            made((rows, width, chip), BF16),
        ]
        if first:
            outs += [made((rows * heads, chip, 2 * size), BF16)]
        stat = made((rows * heads, 1, chip), F32)
        acc = made((rows * heads, size, chip), F32)
        if last:
            outs += [stat, acc, made((rows, tok, half), BF16), made((rows, tok, half), BF16)]
        else:
            outs += [stat, stat, acc]
        got = call(
            functools.partial(chunk_kernel, j, last, tok, rows), ins, outs,
            us=0.05, limit=LIMITS[0], name=f"attend_chunk_{j}", scalars=3,
        )
        for where, array in zip(kept, got[:4]):
            where[j] = array
        got = got[4:]
        if first:
            query, got = got[0], got[1:]
        if not last:
            state = [query] + list(got)
        if at == 0:
            sp_b, state[-1] = tied(sp, state[-1])
            tokens_v, g_v, wo, up, down, bo, bu, bd, gain_b, shift_b = load(
                sp_b,
                [tokens, grad_out, w_out, w_up, w_down, line(b_out), line(b_up), line(b_down), line(gain_two), line(shift_two)],
                [False] * 10, "load_feed_forward",
            )
            g_other = exchange(g_v, "seq", 1)
            state[-1], up = tied(state[-1], up)
        if at == 1:
            state[-1], g_other = tied(state[-1], g_other)
            g_other = g_other.reshape(flat, width)
    lse, out_t, att_m, att_o = got
    att_r = exchange(att_o, "seq", 1)

    wide = made((flat, width), F32)
    vec8 = made((8, width), F32)
    mid, normed_two, send, total, back, vec_a = call(
        ffn_first_kernel, [sp, att_m, att_r, wo, tokens_v, g_v, up, down, bo, bu, gain_b, shift_b],
        [wide, made((flat, width), BF16), made((flat, hidden + width), BF16), wide, wide, vec8],
        us=4.0, limit=LIMITS[1], name="feed_forward_a",
    )
    got = exchange(send, "seq", 1)
    outputs, hid_m, pre_m, mid_grad, branch, vec_ffn = call(
        ffn_second_kernel, [sp, mid, normed_two, g_v, up, down, bu, bd, gain_b, total, back, vec_a],
        [made((rows, tok, width), BF16), made((flat, hidden // 2), BF16), made((flat, hidden // 2), BF16), wide,
         made((rows, tok, width), BF16), vec8],
        us=4.0, limit=LIMITS[1], name="feed_forward_b",
    )
    branch_r = exchange(branch, "seq", 1)
    piece = made((PIECES // 2, hidden // 2 // PIECES, width), BF16)
    ins = [sp, hid_m, pre_m, normed_two, got, g_v.reshape(flat, width), g_other]
    d_send, u_send = call(
        functools.partial(ffn_grad_kernel, 1), ins, [piece, piece], us=3.0, limit=LIMITS[2], name="feed_forward_grad_sent"
    )
    d_send, u_send, branch_r = tied(d_send, u_send, branch_r)
    chain = Chain(d_send)
    d_keep, u_keep = chain(
        functools.partial(call, functools.partial(ffn_grad_kernel, 0)), ins, [piece, piece], us=0.05, limit=LIMITS[2],
        name="feed_forward_grad_kept",
    )

    q = PIECES // GROUP
    d_got, u_got = exchange(d_send, *bit_x), exchange(u_send, *bit_y)

    sums = []
    dn_m, dn_o, dn_r = [], [], []

    def together(name, *jobs):
        ins = [a for _, arrays, _ in jobs for a in arrays]
        outs = [s for _, _, shapes in jobs for s in shapes]

        def kernel(*refs):
            at, to = 0, len(ins)
            for one, arrays, shapes in jobs:
                one(*refs[at : at + len(arrays)], *refs[to : to + len(shapes)])
                at, to = at + len(arrays), to + len(shapes)

        res = iter(chain(functools.partial(merge, kernel), ins, outs, name))
        return [[next(res) for _ in shapes] for _, _, shapes in jobs]

    def norm_job(chunk, arrived):
        ins = [*dn_m, dn_r, *arrived]
        return (functools.partial(norm_grad_kernel, chunk, rows), ins, [made((rows, tok, width), BF16)])

    groups = [tuple(range(rows - 1)), (rows - 1,)] if small else [(r,) for r in range(rows)]
    for group in groups:
        r, last = group[-1], group[-1] == rows - 1
        arrays = [branch, branch_r, wo, query, lse, out_t, weights] + [a for part in kept for a in part]
        specs = [VMEM] * len(arrays)
        if not small:
            for i, a in enumerate(arrays):
                if a.ndim == 3 and a is not weights:
                    block_shape = (a.shape[0] // rows,) + a.shape[1:]
                    specs[i] = pl.BlockSpec(block_shape, functools.partial(lambda r, i: (r, 0, 0), r))
        tail = list(sums)
        if last:
            tail += [vectors, vec_ffn, *dn_o]
        part = made((stations, tok, width), BF16)
        grads = [made((width, half), F32)] * 3 + [made((half, width), F32), made((8, half), F32)]
        outs = [part] * (2 * len(group)) + grads
        scratch = []
        if last:
            outs = [part, made((rows * stations, tok, width), BF16)] + [made((width // 2, width), BF16)] * 2 + [made((width // 2 + 16, width), BF16)] * 2
            scratch = [pltpu.VMEM(g.shape, F32) for g in grads] + [pltpu.VMEM((16, width), F32)]
        run = functools.partial(call, functools.partial(attend_back_kernel, stations, tok, group, small, last))
        res = chain(
            run, [sp, offsets, crop] + arrays + tail, outs, scratch=scratch,
            us=BACK_US, limit=LIMITS[3] if small else 48, name=f"attend_back_{r}", scalars=3,
            specs=specs + [VMEM] * len(tail), grid=() if small else (1,),
        )
        if last:
            dn_m.append(res[0])
            dn_o.append(res[1])
        else:
            dn_m += res[: len(group)]
            dn_o += res[len(group) : 2 * len(group)]
            sums = list(res[2 * len(group) :])
        if r == rows - 2:
            quarters = made((q,) + piece.shape[1:], BF16)
            ((d_next, u_next),) = together(
                "add_quarters", (upper_kernel, [d_keep, d_got, u_keep, u_got], [quarters, quarters])
            )
            d_got2, u_got2 = exchange(d_next, *bit_y), exchange(u_next, *bit_x)
    one_keep, one_send, two_keep, two_send = res[2:]

    rd = hidden // 2 // PIECES
    n = width // PIECES
    ff_part, at_part = made((2 * rd, width), BF16), made((2 * n + 16, width), BF16)
    two_of = lambda a: made((2,) + a.shape, BF16)
    token_block = made((rows, tok, width), BF16)
    bit_z, bit_w = st_bits[:2]

    def over_rest(part):
        for i, (where, mask) in enumerate(rest):
            got = exchange(part, where, mask)
            ((part,),) = together(f"add_rest_{i}", (sum_kernel, [part, got], [made(part.shape, BF16)]))
        return part

    def unpack(far, d, d_other, u, u_other, before):
        ins = [sp, d, d_other, u, u_other] + before
        scratch = [
            pltpu.VMEM((GROUP, q * rd, width), F32), pltpu.VMEM((GROUP, q * width // PIECES, hidden // 2), F32),
            pltpu.SemaphoreType.DMA((2 * GROUP,)),
        ]
        return chain(
            functools.partial(call, functools.partial(unpack_ffn_kernel, far)), ins,
            [made((hidden, width), F32), made((width, hidden), F32), made((8, 128), F32)], scratch=scratch, us=0.1,
            limit=LIMITS[4], name="unpack_feed_forward", specs=[VMEM] * 4 + [HBM] * len(before),
            out_specs=[HBM] * 2 + [VMEM], aliases={5: 0, 6: 1} if before else None,
        )[:2]

    def other_core(*arrays):
        return [exchange(a, "seq", 1) for a in arrays]

    two_a, two_b = two_of(ff_part), two_of(at_part)
    ((a_keep, a_send),) = together(
        "phase_1", (quarter_kernel, [d_keep, d_got, d_got2, u_keep, u_got, u_got2], [two_a, two_a])
    )
    one_send, two_send, dn_o = chain.hold(one_send, two_send, dn_o[-1])
    a_got = exchange(a_send, *bit_z)
    one_got, two_got = exchange(one_send, *bit_x), exchange(two_send, *bit_y)
    (dn_r,) = chain.hold(*other_core(dn_o))

    one_shape, two_shape = made((4 * n, width), BF16), made((4 * n + 16, width), BF16)
    (a_keep, a_send), (one_next, two_next) = together(
        "phase_2",
        (halve_kernel, [a_keep, a_got], [ff_part] * 2),
        (attend_upper_kernel, [one_keep, one_got, two_keep, two_got], [one_shape, two_shape]),
    )
    a_got = exchange(a_send, *bit_w)
    one_got2, two_got2 = exchange(one_next, *bit_y), exchange(two_next, *bit_x)

    (a_own,), (b_keep, b_send) = together(
        "phase_3",
        (sum_kernel, [a_keep, a_got], [ff_part]),
        (attend_quarter_kernel, [one_keep, one_got, one_got2, two_keep, two_got, two_got2], [two_b, two_b]),
    )
    a_own = over_rest(a_own)
    a_near = exchange(a_own, *bit_w)
    b_got = exchange(b_send, *bit_z)

    (a_pair,), (b_keep, b_send) = together(
        "phase_4",
        (pair_kernel, [a_own, a_near], [two_a]),
        (halve_kernel, [b_keep, b_got], [at_part] * 2),
    )
    a_far = exchange(a_pair, *bit_z)
    b_got = exchange(b_send, *bit_w)

    arrived = {c: [] for c in range(stations)}
    top = stations // 2
    inner = [c for c in reversed(turns) if c not in (0, 1, top)]
    for c in inner[:-1]:
        ((moving,),) = together("norm_step", norm_job(c, arrived[c]))
        arrived[c & (c - 1)].append(exchange(moving, "seq", 2 * (c & -c)))
    c = inner[-1]
    (d_mine, u_mine), (b_own,), (moving,) = together(
        "phase_5",
        (divide_kernel, [a_pair, a_far], [quarters, quarters]),
        (sum_kernel, [b_keep, b_got], [at_part]),
        norm_job(c, arrived[c]),
    )
    b_own = over_rest(b_own)
    d_y, u_x = exchange(d_mine, *bit_y), exchange(u_mine, *bit_x)
    b_near = exchange(b_own, *bit_w)
    (moving,) = chain.hold(exchange(moving, "seq", 2 * (c & -c)))
    arrived[c & (c - 1)].append(moving)

    (d_near, u_near), (b_pair,), (moving,) = together(
        "phase_6",
        (join_kernel, [d_mine, d_y, u_mine, u_x], [piece, piece]),
        (pair_kernel, [b_own, b_near], [two_b]),
        norm_job(top, arrived[top]),
    )
    d_far, u_far = exchange(d_near, *bit_x), exchange(u_near, *bit_y)
    b_far = exchange(b_pair, *bit_z)
    moving = exchange(moving, "seq", 2 * top)
    d_far, u_far = chain.hold(d_far, u_far)

    (one_mine, two_mine), (nearest,) = together(
        "phase_7", (attend_divide_kernel, [b_pair, b_far], [one_shape, two_shape]), norm_job(1, [])
    )
    one_y, two_x = exchange(one_mine, *bit_y), exchange(two_mine, *bit_x)
    nearest = exchange(chain.hold(nearest)[0], "seq", 2)
    (moving,) = chain.hold(moving)
    ((one_near, two_near),) = together(
        "phase_8",
        (
            attend_join_kernel, [one_mine, one_y, two_mine, two_x],
            [made((8 * n, width), BF16), made((8 * n + 16, width), BF16)],
        ),
    )
    one_far, two_far = exchange(one_near, *bit_x), exchange(two_near, *bit_y)
    d_near, u_near = chain.hold(d_near, u_near)
    d_near_o, u_near_o = chain.hold(*other_core(d_near, u_near))
    grad_down, grad_up = unpack(False, d_near, d_near_o, u_near, u_near_o, [])
    d_far_o, u_far_o = chain.hold(*other_core(d_far, u_far))
    grad_down, grad_up = unpack(True, d_far, d_far_o, u_far, u_far_o, [grad_down, grad_up])
    far_held = chain.hold(one_far, two_far, nearest)
    nearest = far_held[2]
    one_near_o, two_near_o = other_core(*chain.hold(one_near, two_near))
    one_far_o, two_far_o = other_core(*far_held[:2])
    input_grad = call(
        last_kernel, [tokens_v, vectors, mid_grad, *dn_m, dn_r, *arrived[0], moving, nearest], [token_block],
        us=0.1, limit=LIMITS[4], name="input_grad", scalars=0, extra=[chain.token],
    )[0]
    one_all = [one_near, one_far, one_near_o, one_far_o]
    two_all = [two_near, two_far, two_near_o, two_far_o]
    square = made((width, width), F32)
    run = functools.partial(call, unpack_attend_kernel)
    thin = made((1, width), F32)
    results = chain(
        run, [sp] + one_all + two_all, [square] * 4 + [thin] * 3 + [made((1, hidden), F32)] + [thin] * 5,
        scratch=[pltpu.VMEM((PIECES, width), F32)], us=0.1, limit=LIMITS[4], name="unpack_attend",
    )
    grad_query, grad_key, grad_value, grad_out_proj = results[:4]
    lines = [r.reshape(-1) for r in results[4:]]

    return (outputs, input_grad, grad_query, grad_key, grad_value, grad_out_proj, grad_up, grad_down, *lines)


def solution(mesh):
    split, row, copied = P("dp", "seq", None), P("dp"), P()
    return jax.shard_map(
        body,
        mesh=mesh,
        in_specs=(split, split, row, P("dp", None)) + (copied,) * 15,
        out_specs=(split, split) + (copied,) * 15,
        check_vma=False,
    )
```

```python
import functools

import jax
import jax.numpy as jnp
from jax import lax
from jax.experimental import pallas as pl
from jax.experimental.pallas import tpu as pltpu
from jax.sharding import PartitionSpec as P

HEADS = 8
EPSILON = 1e-06
MASKED = -1e30
MIB = 1024 * 1024
LIMITS = (16, 20, 20, 26, 20)
PIECES = 16
GROUP = 4
BACK_US = 0.05
BF16 = jnp.bfloat16
F32 = jnp.float32
GELU_C = 0.7978845608028654
GELU_A = 0.044715


def nn(a, b):
    return jnp.dot(a, b, preferred_element_type=F32)


def nt(a, b):
    return lax.dot_general(a, b, (((1,), (1,)), ((), ())), preferred_element_type=F32)


def tn(a, b):
    return lax.dot_general(a, b, (((0,), (0,)), ((), ())), preferred_element_type=F32)


def normalize(values):
    center = values - jnp.mean(values, axis=-1, keepdims=True)
    scale = lax.rsqrt(jnp.mean(center * center, axis=-1, keepdims=True) + EPSILON)
    return center * scale, scale


def norm_back(cotangent, unit, scale, gain):
    g = cotangent * gain
    return scale * (
        g
        - jnp.mean(g, axis=-1, keepdims=True)
        - unit * jnp.mean(g * unit, axis=-1, keepdims=True)
    )


def segments(pos, offsets, crop, row):
    count = offsets.shape[1]
    seg = jnp.zeros(pos.shape, jnp.int32)
    for j in range(count):
        seg += (pos >= offsets[row, j]).astype(jnp.int32)
    return seg + count * (pos >= crop[row]).astype(jnp.int32)


def positions(sp, chunk, tok, shape, dim):
    start = (sp[4] ^ chunk) * (2 * tok)
    i = lax.broadcasted_iota(jnp.int32, shape, dim)
    return i + jnp.where(i < tok, start + sp[0] * tok, start + sp[1] * tok - tok)


def half_of(which, width):
    return pl.ds(pl.multiple_of(which * width, 128), width)


def padded(lines):
    return jnp.concatenate(lines + [jnp.zeros((16 - len(lines), lines[0].shape[1]), F32)], axis=0)


def load_kernel(halved, sp, *refs):
    count = len(halved)
    sources, targets, sems = refs[:count], refs[count : 2 * count], refs[2 * count :]
    copies = []
    for half, source, target, sem in zip(halved, sources, targets, sems):
        if half:
            source = source.at[:, half_of(sp[0], source.shape[1] // 2)]
        copies.append(pltpu.make_async_copy(source, target, sem))
    for copy in copies:
        copy.start()
    for copy in copies:
        copy.wait()


def chunk_kernel(chunk, last, tok, rows, *refs):
    refs = list(refs)
    first = chunk == 0
    sp, offsets, crop, xm, xo, vectors, weights = refs[:7]
    refs = refs[7:]
    if not first:
        qm_in, m_in, l_in, acc_in = refs[:4]
        refs = refs[4:]
    k_out, v_out, kt_out, nt_out = refs[:4]
    refs = refs[4:]
    if first:
        qm_out = refs.pop(0)
    if last:
        lse_out, ot_out, att_m, att_o = refs[:4]
    else:
        m_out, l_out, acc_out = refs
    half = weights.shape[2]
    heads = HEADS // 2
    size = half // heads
    chip = 2 * tok
    for at, x in ((0, xm), (tok, xo)):
        values = x[...].reshape(rows * tok, -1).astype(F32)
        unit, _ = normalize(values)
        normed = unit * vectors[0:1, :] + vectors[1:2, :]
        low = normed.astype(BF16)
        k = nn(low, weights[1])
        v = (nn(low, weights[2]) + vectors[3:4, half_of(sp[0], half)]).astype(BF16)
        if first:
            q = ((nn(low, weights[0]) + vectors[2:3, half_of(sp[0], half)]).astype(BF16).astype(F32) * size**-0.5).astype(BF16)
            lane = lax.broadcasted_iota(jnp.int32, (tok, 2 * size), 1)
        for r in range(rows):
            part = slice(r * tok, (r + 1) * tok)
            k_out[r, at : at + tok, :] = k[part].astype(BF16)
            v_out[r, at : at + tok, :] = v[part]
            kt_out[r, :, at : at + tok] = k[part].T.astype(BF16)
            nt_out[r, :, at : at + tok] = normed[part].T.astype(BF16)
            if first:
                for h in range(heads):
                    pair = q[part, (h // 2) * 2 * size : (h // 2 + 1) * 2 * size]
                    keep = (lane >= size) if h % 2 else (lane < size)
                    qm_out[r * heads + h, at : at + tok, :] = jnp.where(keep, pair, jnp.zeros_like(pair))
    qm = qm_out if first else qm_in
    for r in range(rows):
        key_seg = segments(positions(sp, chunk, tok, (chip, chip), 0), offsets, crop, r)
        query_seg = segments(positions(sp, 0, tok, (1, chip), 1), offsets, crop, r)
        bias = jnp.where(key_seg == query_seg, 0.0, MASKED)
        outs = []
        spot = [r * heads + h for h in range(heads)]
        pairs = [slice((h // 2) * 2 * size, (h // 2 + 1) * 2 * size) for h in range(heads)]
        s = [nt(k_out[r, :, pairs[h]], qm[spot[h]]) + bias for h in range(heads)]
        tops = [jnp.max(a, axis=0, keepdims=True) for a in s]
        if not first:
            olds = [m_in[at] for at in spot]
            tops = [jnp.maximum(a, b) for a, b in zip(olds, tops)]
        p = [jnp.exp(a - b) for a, b in zip(s, tops)]
        totals = [jnp.sum(a, axis=0, keepdims=True) for a in p]
        addeds = [tn(v_out[r, :, pairs[h]], p[h].astype(BF16)) for h in range(heads)]
        for h, at in enumerate(spot):
            added = addeds[h][(h % 2) * size : (h % 2 + 1) * size]
            total = totals[h]
            if not first:
                keep = jnp.exp(olds[h] - tops[h])
                total += l_in[at] * keep
                added += acc_in[at] * keep
            if last:
                lse_out[at] = tops[h] + jnp.log(total)
                out = added / total
                ot_out[at] = out
                outs.append(out)
            else:
                m_out[at] = tops[h]
                l_out[at] = total
                acc_out[at] = added
        if last:
            att = jnp.concatenate(outs, axis=0).T.astype(BF16)
            att_m[r] = att[:tok]
            att_o[r] = att[tok:]


def feed_forward_half(sp, which, normed, g, up, down, bup, hid, pre, at, vec, total, back):
    half = up.shape[1] // 2
    row = min(512, half)
    block = min(512, row)
    count = half // block
    cols = [pl.ds(pl.multiple_of(sp[which] * half + j * block, 128), block) for j in range(count)]
    for first in range(0, count, 2):
        js = range(first, min(first + 2, count))
        us = [nn(normed, up[:, cols[j]]) + bup[:, cols[j]] for j in js]
        gs = [nt(g, down[cols[j], :]) for j in js]
        outs, pres = [], []
        for j, u, back_in in zip(js, us, gs):
            square = u * u
            plus = 1.0 + jnp.tanh(u * (GELU_C + GELU_C * GELU_A * square))
            low = 0.5 * u
            hidden = (low * plus).astype(BF16)
            slope = plus * (0.5 + low * (2.0 - plus) * (GELU_C + 3 * GELU_C * GELU_A * square))
            grad = (back_in * slope).astype(BF16)
            hid[:, j * block : (j + 1) * block] = hidden
            pre[:, at + j * block : at + (j + 1) * block] = grad
            outs.append(hidden)
            pres.append(grad)
            line = jnp.sum(grad.astype(F32), axis=0, keepdims=True)
            lane = j * block % row
            vec[pl.ds(sp[which] * (half // row) + j * block // row, 1), lane : lane + block] = line
        for j, hidden, grad in zip(js, outs, pres):
            more, less = nn(hidden, down[cols[j], :]), nt(grad, up[:, cols[j]])
            total = more if total is None else total + more
            back = less if back is None else back + less
    return total, back


def ffn_first_kernel(
    sp, att_m, att_o, wo, tokens, cot, up, down, b_out, bup, gain, shift, mid_out, normed_out, send, total_out, back_out, vec
):
    rows, tok, width = tokens.shape
    flat = rows * tok
    quarter = width // 2
    mine = pl.ds(pl.multiple_of(sp[0] * quarter, 128), quarter)
    other = pl.ds(pl.multiple_of(sp[1] * quarter, 128), quarter)
    mid = (
        tokens[...].reshape(flat, width).astype(F32)
        + nn(att_m[...].reshape(flat, -1), wo[mine, :])
        + nn(att_o[...].reshape(flat, -1), wo[other, :])
        + b_out[...]
    )
    mid_out[...] = mid
    unit, _ = normalize(mid)
    normed = (unit * gain[...] + shift[...]).astype(BF16)
    normed_out[...] = normed
    half = up.shape[1] // 2
    send[:, 2 * half :] = normed
    vec[...] = jnp.zeros_like(vec)
    g = cot[...].reshape(flat, width)
    total_out[...], back_out[...] = feed_forward_half(
        sp, 1, normed, g, up, down, bup, send, send, half, vec, None, None
    )


def ffn_second_kernel(
    sp, mid_in, normed_in, cot, up, down, bup, b_down, gain, total_in, back_in, vec_in, out, hid, pre, mid_grad, branch, vec
):
    rows, tok, width = cot.shape
    flat = rows * tok
    g = cot[...].reshape(flat, width)
    vec[...] = vec_in[...]
    total, back = feed_forward_half(
        sp, 0, normed_in[...], g, up, down, bup, hid, pre, 0, vec, total_in[...], back_in[...]
    )
    mid = mid_in[...]
    out[...] = (mid + total + b_down[...]).astype(BF16).reshape(rows, tok, width)
    unit, scale = normalize(mid)
    gf = g.astype(F32)
    grad = gf + norm_back(back, unit, scale, gain[...])
    mid_grad[...] = grad
    low = grad.astype(BF16)
    branch[...] = low.reshape(rows, tok, width)
    vec[4:5, :] = jnp.sum(gf, axis=0, keepdims=True)
    vec[5:6, :] = jnp.sum(back * unit, axis=0, keepdims=True)
    vec[6:7, :] = jnp.sum(back, axis=0, keepdims=True)
    vec[7:8, :] = jnp.sum(low.astype(F32), axis=0, keepdims=True)


def ffn_grad_kernel(send, sp, hid_m, pre_m, n_m, got, g_m, g_o, d, u):
    half = hid_m.shape[1]
    width = g_m.shape[1]
    per = PIECES // 2
    rd, ru = half // PIECES, width // PIECES
    part = (sp[2] // per) ^ send
    cols = half_of(part, half // 2)
    gd = tn(hid_m[:, cols], g_m[...]) + tn(got[:, cols], g_o[...])
    part = (sp[3] // per) ^ send
    own = half_of(part, width // 2)
    others = pl.ds(pl.multiple_of(2 * half + part * (width // 2), 128), width // 2)
    gu = tn(n_m[:, own], pre_m[...]) + tn(got[:, others], got[:, half : 2 * half])
    for p in range(per):
        d[(sp[2] & (per - 1)) ^ p] = gd[p * rd : (p + 1) * rd].astype(BF16)
        at = (sp[3] & (per - 1)) ^ p
        for i in range(half // width):
            u[at, i * ru : (i + 1) * ru, :] = gu[p * ru : (p + 1) * ru, i * width : (i + 1) * width].astype(BF16)


def attend_back_kernel(stations, tok, rows_here, whole, last, *refs):
    refs = list(refs)

    def take(count):
        got = refs[:count]
        del refs[:count]
        return got

    sp, offsets, crop, br_m, br_o, wo, qm, lse, ot, weights = take(10)
    k, v, kt, norm_t = (take(stations) for _ in range(4))
    sums_in = take(5) if rows_here[0] else None
    if last:
        vectors, vec_in = take(2)
        before = take(rows_here[0])
    dn_m = take(len(rows_here))
    dn_o = take(1 if last else len(rows_here))
    if last:
        ones, twos = take(2), take(2)
    gq, gk, gv, go, sums = take(5)
    heads = HEADS // 2
    _, width, half = weights.shape
    size = half // heads
    chip = 2 * tok
    block = min(4, stations)
    blocks = stations // block

    made_here = [0.0] * 5
    for place, row in enumerate(rows_here):
        at = row if whole else 0
        branch = jnp.concatenate([br_m[at], br_o[at]], axis=0)
        do = nt(branch, wo[half_of(sp[0], half), :])
        dot = do.T
        do = do.astype(BF16)
        lane = lax.broadcasted_iota(jnp.int32, (chip, 2 * size), 1)
        head_at = at * heads
        out_t = jnp.concatenate([ot[head_at + h] for h in range(heads)], axis=0).astype(BF16)
        go_row = nn(out_t, branch)
        query_seg = segments(positions(sp, 0, tok, (1, chip), 1), offsets, crop, row)
        biases = []
        for chunk in range(stations):
            key_seg = segments(positions(sp, chunk, tok, (chip, chip), 0), offsets, crop, row)
            biases.append(jnp.where(key_seg == query_seg, 0.0, MASKED))
        dqt = []
        dks = [[] for _ in range(blocks)]
        dvs = [[] for _ in range(blocks)]
        for pair in range(heads // 2):
            lanes = slice(pair * 2 * size, (pair + 1) * 2 * size)
            dk = [None] * blocks
            dv = [None] * blocks
            for h in (2 * pair, 2 * pair + 1):
                wide = do[:, lanes]
                dm = jnp.where((lane >= size) if h % 2 else (lane < size), wide, jnp.zeros_like(wide))
                delta = jnp.sum(ot[head_at + h] * dot[h * size : (h + 1) * size], axis=0, keepdims=True)
                dq = None
                for b in range(blocks):
                    chunks = range(b * block, (b + 1) * block)
                    keys = jnp.concatenate([k[c][at, :, lanes] for c in chunks], axis=0)
                    values = jnp.concatenate([v[c][at, :, lanes] for c in chunks], axis=0)
                    keys_t = jnp.concatenate([kt[c][at, h * size : (h + 1) * size, :] for c in chunks], axis=1)
                    bias = jnp.concatenate([biases[c] for c in chunks], axis=0)
                    p = jnp.exp(nt(keys, qm[head_at + h]) + bias - lse[head_at + h])
                    ds = (p * (nt(values, dm) - delta)).astype(BF16)
                    dv_h, dk_h = nn(p.astype(BF16), dm), nn(ds, qm[head_at + h])
                    dv[b] = dv_h if dv[b] is None else dv[b] + dv_h
                    dk[b] = dk_h if dk[b] is None else dk[b] + dk_h
                    more = nn(keys_t, ds)
                    dq = more if dq is None else dq + more
                dqt.append(dq)
            for b in range(blocks):
                dks[b].append(dk[b].astype(BF16))
                dvs[b].append(dv[b].astype(BF16))
        dq = (jnp.concatenate(dqt, axis=0) * size**-0.5).T.astype(BF16)
        gq_row = nn(norm_t[0][at], dq)
        gk_row = gv_row = sum_k = sum_v = 0.0
        for b in range(blocks):
            dk = jnp.concatenate(dks[b], axis=1)
            dv = jnp.concatenate(dvs[b], axis=1)
            normed = jnp.concatenate([norm_t[c][at] for c in range(b * block, (b + 1) * block)], axis=1)
            gk_row += nn(normed, dk)
            gv_row += nn(normed, dv)
            sum_k += jnp.sum(dk.astype(F32), axis=0, keepdims=True)
            sum_v += jnp.sum(dv.astype(F32), axis=0, keepdims=True)
            dn = nt(dk, weights[1]) + nt(dv, weights[2])
            for i in range(block):
                part = dn[i * chip : (i + 1) * chip]
                if b + i == 0:
                    part += nt(dq, weights[0])
                dn_m[place][b * block + i] = part[:tok].astype(BF16)
                dn_o[0 if last else place][(row * stations if last else 0) + b * block + i] = part[tok:].astype(BF16)
        sum_q = jnp.sum(dq.astype(F32), axis=0, keepdims=True)
        rest = jnp.zeros((5, half), F32)
        values = (gq_row, gk_row, gv_row, go_row, jnp.concatenate([sum_q, sum_v, sum_k, rest]))
        made_here = [a + b for a, b in zip(made_here, values)]
    for i, (ref, value) in enumerate(zip((gq, gk, gv, go, sums), made_here)):
        ref[...] = value if sums_in is None else value + sums_in[i][...]
    if not last:
        return

    for r, part in enumerate(before):
        dn_o[0][r * stations : (r + 1) * stations] = part[...]
    vec = refs[0]
    lane = lax.broadcasted_iota(jnp.int32, (2, width), 1)
    both = sums[0:2, :]
    both = jnp.concatenate([both, both], axis=1)
    vec[0:2, :] = jnp.where((lane >= half) == (sp[0] == 1), both, 0.0)
    vec[2:3, :] = vec_in[7:8, :]
    vec[3:4, :] = vec_in[4:5, :]
    vec[4:8, :] = vec_in[0:4, :]
    vec[10:12, :] = vec_in[5:7, :]
    vec[12:16, :] = jnp.zeros((4, width), F32)
    wide = [weights[i].astype(F32) for i in range(3)]
    shifts = sum(w * sums[i : i + 1, :] for w, i in zip(wide, (0, 2, 1)))
    gains = sum(w * g[...] for w, g in zip(wide, (gq, gk, gv)))

    def across(values):
        folded = sum(values[:, i * 128 : (i + 1) * 128] for i in range(half // 128))
        return jnp.sum(folded.T, axis=0, keepdims=True)

    shift_grad = across(shifts)
    vec[9:10, :] = shift_grad
    vec[8:9, :] = (across(gains) - vectors[1:2, :] * shift_grad) / vectors[0:1, :]
    n = width // PIECES
    low = n // 2
    per = PIECES // 2
    for slot in range(PIECES):
        one, two = ones[slot // per], twos[slot // per]
        base = slot % per * n
        piece = sp[2] ^ slot
        part = pl.ds(pl.multiple_of(piece * n, n), n)
        one[base : base + n, :half] = gq[part, :].astype(BF16)
        one[base : base + n, half:] = gk[part, :].astype(BF16)
        piece = sp[3] ^ slot
        first = pl.ds(pl.multiple_of(piece * n, n), low)
        second = pl.ds(pl.multiple_of(piece * n + low, low), low)
        two[base : base + low, :half] = gv[first, :].astype(BF16)
        two[base : base + low, half:] = gv[second, :].astype(BF16)
        two[base + low : base + n, :] = go[pl.ds(pl.multiple_of(piece * low, low), low), :].astype(BF16)
    for i, two in enumerate(twos):
        lines = [vec[pl.ds(sp[3] ^ (i * per + s), 1), :] for s in range(per)]
        two[per * n :, :] = padded(lines).astype(BF16)


def last_kernel(tokens, gain, mid_grad, *refs):
    out = refs[-1]
    rows, tok, width = tokens.shape
    flat = rows * tok
    unit, scale = normalize(tokens[...].reshape(flat, width).astype(F32))
    parts = []
    for r in range(rows):
        part = refs[r][0].astype(F32) + refs[rows][r * refs[0].shape[0]].astype(F32)
        for arrived in refs[rows + 1 : -1]:
            part += arrived[r].astype(F32)
        parts.append(part)
    grad = mid_grad[...] + norm_back(jnp.concatenate(parts, axis=0), unit, scale, gain[0:1, :])
    out[...] = grad.astype(BF16).reshape(rows, tok, width)


def unpack_ffn_kernel(far, sp, *refs):
    refs = list(refs)
    d_both, u_both = refs[0:2], refs[2:4]
    down, up, done, d_wide, u_wide, sems = refs[-6:]
    done[...] = jnp.zeros_like(done)
    _, rd, width = d_both[0].shape
    ru = up.shape[0] // PIECES
    half = down.shape[0] // 2
    count = PIECES // GROUP
    copies = []
    for which in range(2):
        for i in range(GROUP // 2):
            at = which * (GROUP // 2) + i
            group = (GROUP // 2 if far else 0) + i
            for k in range(count):
                slot = i * count + k
                place = (sp[2] ^ k) & (count - 1)
                rows = pl.ds(pl.multiple_of(place * rd, rd), rd)
                d_wide[at, rows, :] = d_both[which][slot].astype(F32)
                place = (sp[3] ^ k) & (count - 1)
                rows = pl.ds(pl.multiple_of(place * ru, ru), ru)
                for n in range(rd // ru):
                    part = u_both[which][slot, n * ru : (n + 1) * ru, :]
                    u_wide[at, rows, n * width : (n + 1) * width] = part.astype(F32)
            size = count * rd
            rows = pl.ds(pl.multiple_of(sp[which] * half + ((sp[2] // count) ^ group) * size, size), size)
            copies.append(pltpu.make_async_copy(d_wide.at[at], down.at[rows, :], sems.at[2 * at]))
            copies[-1].start()
            size = count * ru
            rows = pl.ds(pl.multiple_of(((sp[3] // count) ^ group) * size, size), size)
            copies.append(pltpu.make_async_copy(u_wide.at[at], up.at[rows, half_of(sp[which], half)], sems.at[2 * at + 1]))
            copies[-1].start()
    for copy in copies:
        copy.wait()


def unpack_attend_kernel(sp, *refs):
    gq, gk, gv, go, *lines = refs[8:]
    vec = lines.pop()
    ones, twos = (refs[0:2], refs[2:4]), (refs[4:6], refs[6:8])
    width = gq.shape[0]
    half = width // 2
    n = width // PIECES
    low = n // 2
    per = PIECES // 2
    for slot in range(PIECES):
        base = slot % per * n
        for which in range(2):
            one, two = ones[which][slot // per], twos[which][slot // per]
            cols = half_of(sp[which], half)
            piece = sp[2] ^ slot
            rows = pl.ds(pl.multiple_of(piece * n, n), n)
            gq[rows, cols] = one[base : base + n, :half].astype(F32)
            gk[rows, cols] = one[base : base + n, half:].astype(F32)
            piece = sp[3] ^ slot
            first = pl.ds(pl.multiple_of(piece * n, n), low)
            second = pl.ds(pl.multiple_of(piece * n + low, low), low)
            gv[first, cols] = two[base : base + low, :half].astype(F32)
            gv[second, cols] = two[base : base + low, half:].astype(F32)
            out_rows = pl.ds(pl.multiple_of(sp[which] * half + piece * low, low), low)
            go[out_rows, :] = two[base + low : base + n, :].astype(F32)
    for side in range(2):
        both = twos[0][side][per * n :, :].astype(F32) + twos[1][side][per * n :, :].astype(F32)
        for s in range(per):
            vec[pl.ds(sp[3] ^ (side * per + s), 1), :] = both[s : s + 1]
    for line, row in zip(lines, (0, 1, 2, 4, 3, 8, 9, 10, 11)):
        count = line.shape[1] // width
        for i in range(count):
            line[:, i * width : (i + 1) * width] = vec[row + i : row + i + 1, :]


def total(*values):
    return sum(v.astype(F32) for v in values).astype(BF16)


def sum_kernel(*refs):
    refs[-1][...] = total(*[r[...] for r in refs[:-1]])


def upper_kernel(*refs):
    count = len(refs) // 3
    for i, out in enumerate(refs[2 * count :]):
        keep, got = refs[2 * i : 2 * i + 2]
        half = keep.shape[0] // 2
        out[...] = total(keep[half:], got[half:])


def quarter_kernel(d_keep, d_got, d_last, u_keep, u_got, u_last, keep, send):
    rd = d_keep.shape[1]
    half = keep.shape[0]
    for i in range(2 * half):
        out = send if i >= half else keep
        out[i % half, :rd] = total(d_keep[i], d_got[i], d_last[i])
        out[i % half, rd:] = total(u_keep[i], u_got[i], u_last[i])


def halve_kernel(keep, got, out_keep, out_send):
    out_keep[...] = total(keep[0], got[0])
    out_send[...] = total(keep[1], got[1])


def pair_kernel(one, two, out):
    out[0] = one[...]
    out[1] = two[...]


def divide_kernel(one, two, d, u):
    rd = d.shape[1]
    for i in range(d.shape[0]):
        part = (one if i < 2 else two)[i % 2]
        d[i] = part[:rd]
        u[i] = part[rd:]


def join_kernel(*refs):
    count = len(refs) // 3
    for i, out in enumerate(refs[2 * count :]):
        one, two = refs[2 * i : 2 * i + 2]
        out[: one.shape[0]] = one[...]
        out[one.shape[0] :] = two[...]


def attend_upper_kernel(one_keep, one_got, two_keep, two_got, one, two):
    n = one.shape[0]
    one[...] = total(one_keep[n:], one_got[n:])
    two[:n] = total(two_keep[n : 2 * n], two_got[n : 2 * n])
    lines = total(two_keep[2 * n :], two_got[2 * n :]).astype(F32)
    two[n:] = fill(lines[4:8])


def fill(lines):
    return jnp.concatenate([lines, jnp.zeros((16 - lines.shape[0], lines.shape[1]), F32)], axis=0).astype(BF16)


def attend_quarter_kernel(one_keep, one_got, one_last, two_keep, two_got, two_last, keep, send):
    count = 2 * keep.shape[0]
    n = one_last.shape[0] // count
    lines = total(two_keep[2 * count * n :], two_got[2 * count * n :], two_last[count * n :]).astype(F32)
    for i in range(count):
        out = (keep, send)[i // 2]
        part = slice(i * n, (i + 1) * n)
        out[i % 2, :n] = total(one_keep[part], one_got[part], one_last[part])
        out[i % 2, n : 2 * n] = total(two_keep[part], two_got[part], two_last[part])
        out[i % 2, 2 * n :] = jnp.broadcast_to(lines[i : i + 1], (16, lines.shape[1])).astype(BF16)


def attend_divide_kernel(first, second, one, two):
    n = one.shape[0] // 4
    lines = []
    for i in range(4):
        part = (first if i < 2 else second)[i % 2]
        one[i * n : (i + 1) * n] = part[:n]
        two[i * n : (i + 1) * n] = part[n : 2 * n]
        lines.append(part[2 * n :].astype(F32)[:1])
    two[4 * n :] = padded(lines).astype(BF16)


def attend_join_kernel(one_a, one_b, two_a, two_b, one, two):
    n = one_a.shape[0]
    one[:n] = one_a[...]
    one[n:] = one_b[...]
    two[:n] = two_a[:n]
    two[n : 2 * n] = two_b[:n]
    lines = jnp.concatenate([two_a[n:].astype(F32)[:4], two_b[n:].astype(F32)[:4]], axis=0)
    two[2 * n :] = fill(lines)


def norm_grad_kernel(chunk, rows, *refs):
    out = refs[-1]
    stations = refs[0].shape[0]
    for r in range(rows):
        out[r] = total(refs[r][chunk], refs[rows][r * stations + chunk], *[a[r] for a in refs[rows + 1 : -1]])


VMEM = pl.BlockSpec(memory_space=pltpu.VMEM)
SMEM = pl.BlockSpec(memory_space=pltpu.SMEM)
HBM = pl.BlockSpec(memory_space=pltpu.HBM)
ANY = pl.BlockSpec(memory_space=pl.ANY)


def call(kernel, ins, outs, scratch=(), us=1.0, limit=16, name=None, scalars=1, specs=None, grid=(), out_specs=None, aliases=None, extra=()):
    count = len(ins)

    def body_of(*refs):
        kernel(*refs[:count], *refs[count + len(extra) :])

    return pl.pallas_call(
        body_of,
        grid=grid,
        in_specs=[SMEM] * scalars + (specs or [VMEM] * (count - scalars)) + [ANY] * len(extra),
        out_specs=out_specs or [VMEM] * len(outs),
        input_output_aliases=aliases or {},
        out_shape=list(outs),
        scratch_shapes=list(scratch),
        compiler_params=pltpu.CompilerParams(vmem_limit_bytes=limit * MIB),
        cost_estimate=pl.CostEstimate(flops=int(us * 1.1e9), bytes_accessed=0, transcendentals=0),
        name=name,
    )(*ins, *extra)


def load(sp, arrays, halved, name, limit=16):
    shapes = [a.shape[:-1] + (a.shape[-1] // (2 if h else 1),) for a, h in zip(arrays, halved)]
    return call(
        functools.partial(load_kernel, halved), [sp] + arrays, [made(s, a.dtype) for s, a in zip(shapes, arrays)],
        scratch=[pltpu.SemaphoreType.DMA] * len(arrays), us=2.0, limit=limit, name=name, specs=[HBM] * len(arrays),
    )


def made(shape, dtype):
    return jax.ShapeDtypeStruct(shape, dtype)


def exchange(array, axis, mask):
    count = lax.axis_size(axis)
    return lax.ppermute(array, axis, [(i, i ^ mask) for i in range(count)])


def merge(kernel, ins, outs, name, extra=()):
    specs = [SMEM if a.dtype == jnp.int32 else VMEM for a in ins]
    return call(kernel, list(ins), list(outs), us=0.05, limit=8, name=name, scalars=0, specs=specs, extra=extra)


def tied(*arrays):
    return lax.optimization_barrier(arrays)


class Chain:
    def __init__(self, token):
        self.token = token

    def __call__(self, function, *args, **kwargs):
        outs = list(function(*args, extra=[self.token], **kwargs))
        self.token = outs[-1]
        return outs

    def hold(self, *arrays):
        *arrays, self.token = tied(*arrays, self.token)
        return arrays


def my_id(bits):
    out = 0
    for axis, mask in bits:
        out = out * 2 + jnp.where((lax.axis_index(axis) & mask) != 0, 1, 0)
    return out


def body(
    tokens, grad_out, crop, offsets, w_query, w_key, w_value, w_out, w_up, w_down, b_query, b_value,
    b_out, b_up, b_down, gain_one, shift_one, gain_two, shift_two,
):
    rows, tok, width = tokens.shape
    seq_count, dp_count = lax.axis_size("seq"), lax.axis_size("dp")
    stations = seq_count // 2
    hidden = w_up.shape[1]
    half = width // 2
    heads = HEADS // 2
    size = half // heads
    chip = 2 * tok
    flat = rows * tok
    small = stations <= 4
    seq = lax.axis_index("seq")
    core, station = seq % 2, seq // 2
    line = lambda v: v.reshape(1, -1)

    dp_bits = [("dp", 1 << i) for i in range(dp_count.bit_length() - 1)]
    st_bits = [("seq", 2 << i) for i in range(stations.bit_length() - 1)]
    bit_x, bit_y = dp_bits[:2]
    rest = dp_bits[2:] + st_bits[2:]
    ids = [my_id([bit_x, bit_y] + st_bits[:2]), my_id([bit_y, bit_x] + st_bits[:2])]
    sp = jnp.stack([core, 1 - core, *ids, station]).astype(jnp.int32)

    mine = lambda a: lax.dynamic_slice_in_dim(a, core * half, half, a.ndim - 1)
    weights = jnp.stack([mine(w_query), mine(w_key), mine(w_value)])
    vectors = jnp.stack([gain_one, shift_one, b_query, b_value] + [jnp.zeros_like(gain_one)] * 4)
    state = []
    kept = [[None] * stations for _ in range(4)]
    blocks = {0: tokens}
    turns = [int(f"{i:0{stations.bit_length() - 1}b}"[::-1], 2) for i in range(stations)]
    for at, j in enumerate(turns):
        if j:
            low = j & -j
            block = blocks[j] = exchange(blocks[j ^ low], "seq", 2 * low)
            if at == 1 or at == stations - 1:
                block, state[-1] = tied(block, state[-1])
                blocks[j] = block
        else:
            block = tokens
        other = exchange(block, "seq", 1)
        first, last = at == 0, at == stations - 1
        ins = [sp, offsets, crop, block, other, vectors, weights] + ([] if first else state)
        outs = [
            made((rows, chip, half), BF16),
            made((rows, chip, half), BF16),
            made((rows, half, chip), BF16),
            made((rows, width, chip), BF16),
        ]
        if first:
            outs += [made((rows * heads, chip, 2 * size), BF16)]
        stat = made((rows * heads, 1, chip), F32)
        acc = made((rows * heads, size, chip), F32)
        if last:
            outs += [stat, acc, made((rows, tok, half), BF16), made((rows, tok, half), BF16)]
        else:
            outs += [stat, stat, acc]
        got = call(
            functools.partial(chunk_kernel, j, last, tok, rows), ins, outs,
            us=0.05, limit=LIMITS[0], name=f"attend_chunk_{j}", scalars=3,
        )
        for where, array in zip(kept, got[:4]):
            where[j] = array
        got = got[4:]
        if first:
            query, got = got[0], got[1:]
        if not last:
            state = [query] + list(got)
        if at == 0:
            sp_b, state[-1] = tied(sp, state[-1])
            tokens_v, g_v, wo, up, down, bo, bu, bd, gain_b, shift_b = load(
                sp_b,
                [tokens, grad_out, w_out, w_up, w_down, line(b_out), line(b_up), line(b_down), line(gain_two), line(shift_two)],
                [False] * 10, "load_feed_forward",
            )
            g_other = exchange(g_v, "seq", 1)
            state[-1], up = tied(state[-1], up)
        if at == 1:
            state[-1], g_other = tied(state[-1], g_other)
            g_other = g_other.reshape(flat, width)
    lse, out_t, att_m, att_o = got
    att_r = exchange(att_o, "seq", 1)

    wide = made((flat, width), F32)
    vec8 = made((8, width), F32)
    mid, normed_two, send, total, back, vec_a = call(
        ffn_first_kernel, [sp, att_m, att_r, wo, tokens_v, g_v, up, down, bo, bu, gain_b, shift_b],
        [wide, made((flat, width), BF16), made((flat, hidden + width), BF16), wide, wide, vec8],
        us=4.0, limit=LIMITS[1], name="feed_forward_a",
    )
    got = exchange(send, "seq", 1)
    outputs, hid_m, pre_m, mid_grad, branch, vec_ffn = call(
        ffn_second_kernel, [sp, mid, normed_two, g_v, up, down, bu, bd, gain_b, total, back, vec_a],
        [made((rows, tok, width), BF16), made((flat, hidden // 2), BF16), made((flat, hidden // 2), BF16), wide,
         made((rows, tok, width), BF16), vec8],
        us=4.0, limit=LIMITS[1], name="feed_forward_b",
    )
    branch_r = exchange(branch, "seq", 1)
    piece = made((PIECES // 2, hidden // 2 // PIECES, width), BF16)
    ins = [sp, hid_m, pre_m, normed_two, got, g_v.reshape(flat, width), g_other]
    d_send, u_send = call(
        functools.partial(ffn_grad_kernel, 1), ins, [piece, piece], us=3.0, limit=LIMITS[2], name="feed_forward_grad_sent"
    )
    d_send, u_send, branch_r = tied(d_send, u_send, branch_r)
    chain = Chain(d_send)
    d_keep, u_keep = chain(
        functools.partial(call, functools.partial(ffn_grad_kernel, 0)), ins, [piece, piece], us=0.05, limit=LIMITS[2],
        name="feed_forward_grad_kept",
    )

    q = PIECES // GROUP
    d_got, u_got = exchange(d_send, *bit_x), exchange(u_send, *bit_y)

    sums = []
    dn_m, dn_o, dn_r = [], [], []

    def together(name, *jobs):
        ins = [a for _, arrays, _ in jobs for a in arrays]
        outs = [s for _, _, shapes in jobs for s in shapes]

        def kernel(*refs):
            at, to = 0, len(ins)
            for one, arrays, shapes in jobs:
                one(*refs[at : at + len(arrays)], *refs[to : to + len(shapes)])
                at, to = at + len(arrays), to + len(shapes)

        res = iter(chain(functools.partial(merge, kernel), ins, outs, name))
        return [[next(res) for _ in shapes] for _, _, shapes in jobs]

    def norm_job(chunk, arrived):
        ins = [*dn_m, dn_r, *arrived]
        return (functools.partial(norm_grad_kernel, chunk, rows), ins, [made((rows, tok, width), BF16)])

    groups = [tuple(range(rows - 1)), (rows - 1,)] if small else [(r,) for r in range(rows)]
    for group in groups:
        r, last = group[-1], group[-1] == rows - 1
        arrays = [branch, branch_r, wo, query, lse, out_t, weights] + [a for part in kept for a in part]
        specs = [VMEM] * len(arrays)
        if not small:
            for i, a in enumerate(arrays):
                if a.ndim == 3 and a is not weights:
                    block_shape = (a.shape[0] // rows,) + a.shape[1:]
                    specs[i] = pl.BlockSpec(block_shape, functools.partial(lambda r, i: (r, 0, 0), r))
        tail = list(sums)
        if last:
            tail += [vectors, vec_ffn, *dn_o]
        part = made((stations, tok, width), BF16)
        grads = [made((width, half), F32)] * 3 + [made((half, width), F32), made((8, half), F32)]
        outs = [part] * (2 * len(group)) + grads
        scratch = []
        if last:
            outs = [part, made((rows * stations, tok, width), BF16)] + [made((width // 2, width), BF16)] * 2 + [made((width // 2 + 16, width), BF16)] * 2
            scratch = [pltpu.VMEM(g.shape, F32) for g in grads] + [pltpu.VMEM((16, width), F32)]
        run = functools.partial(call, functools.partial(attend_back_kernel, stations, tok, group, small, last))
        res = chain(
            run, [sp, offsets, crop] + arrays + tail, outs, scratch=scratch,
            us=BACK_US, limit=LIMITS[3] if small else 48, name=f"attend_back_{r}", scalars=3,
            specs=specs + [VMEM] * len(tail), grid=() if small else (1,),
        )
        if last:
            dn_m.append(res[0])
            dn_o.append(res[1])
        else:
            dn_m += res[: len(group)]
            dn_o += res[len(group) : 2 * len(group)]
            sums = list(res[2 * len(group) :])
        if r == rows - 2:
            quarters = made((q,) + piece.shape[1:], BF16)
            ((d_next, u_next),) = together(
                "add_quarters", (upper_kernel, [d_keep, d_got, u_keep, u_got], [quarters, quarters])
            )
            d_got2, u_got2 = exchange(d_next, *bit_y), exchange(u_next, *bit_x)
    one_keep, one_send, two_keep, two_send = res[2:]

    rd = hidden // 2 // PIECES
    n = width // PIECES
    ff_part, at_part = made((2 * rd, width), BF16), made((2 * n + 16, width), BF16)
    two_of = lambda a: made((2,) + a.shape, BF16)
    token_block = made((rows, tok, width), BF16)
    bit_z, bit_w = st_bits[:2]

    def over_rest(part):
        for i, (where, mask) in enumerate(rest):
            got = exchange(part, where, mask)
            ((part,),) = together(f"add_rest_{i}", (sum_kernel, [part, got], [made(part.shape, BF16)]))
        return part

    def unpack(far, d, d_other, u, u_other, before):
        ins = [sp, d, d_other, u, u_other] + before
        scratch = [
            pltpu.VMEM((GROUP, q * rd, width), F32), pltpu.VMEM((GROUP, q * width // PIECES, hidden // 2), F32),
            pltpu.SemaphoreType.DMA((2 * GROUP,)),
        ]
        return chain(
            functools.partial(call, functools.partial(unpack_ffn_kernel, far)), ins,
            [made((hidden, width), F32), made((width, hidden), F32), made((8, 128), F32)], scratch=scratch, us=0.1,
            limit=LIMITS[4], name="unpack_feed_forward", specs=[VMEM] * 4 + [HBM] * len(before),
            out_specs=[HBM] * 2 + [VMEM], aliases={5: 0, 6: 1} if before else None,
        )[:2]

    def other_core(*arrays):
        return [exchange(a, "seq", 1) for a in arrays]

    two_a, two_b = two_of(ff_part), two_of(at_part)
    ((a_keep, a_send),) = together(
        "phase_1", (quarter_kernel, [d_keep, d_got, d_got2, u_keep, u_got, u_got2], [two_a, two_a])
    )
    one_send, two_send, dn_o = chain.hold(one_send, two_send, dn_o[-1])
    a_got = exchange(a_send, *bit_z)
    one_got, two_got = exchange(one_send, *bit_x), exchange(two_send, *bit_y)
    (dn_r,) = chain.hold(*other_core(dn_o))

    one_shape, two_shape = made((4 * n, width), BF16), made((4 * n + 16, width), BF16)
    (a_keep, a_send), (one_next, two_next) = together(
        "phase_2",
        (halve_kernel, [a_keep, a_got], [ff_part] * 2),
        (attend_upper_kernel, [one_keep, one_got, two_keep, two_got], [one_shape, two_shape]),
    )
    a_got = exchange(a_send, *bit_w)
    one_got2, two_got2 = exchange(one_next, *bit_y), exchange(two_next, *bit_x)

    (a_own,), (b_keep, b_send) = together(
        "phase_3",
        (sum_kernel, [a_keep, a_got], [ff_part]),
        (attend_quarter_kernel, [one_keep, one_got, one_got2, two_keep, two_got, two_got2], [two_b, two_b]),
    )
    a_own = over_rest(a_own)
    a_near = exchange(a_own, *bit_w)
    b_got = exchange(b_send, *bit_z)

    (a_pair,), (b_keep, b_send) = together(
        "phase_4",
        (pair_kernel, [a_own, a_near], [two_a]),
        (halve_kernel, [b_keep, b_got], [at_part] * 2),
    )
    a_far = exchange(a_pair, *bit_z)
    b_got = exchange(b_send, *bit_w)

    arrived = {c: [] for c in range(stations)}
    top = stations // 2
    inner = [c for c in reversed(turns) if c not in (0, 1, top)]
    for c in inner[:-1]:
        ((moving,),) = together("norm_step", norm_job(c, arrived[c]))
        arrived[c & (c - 1)].append(exchange(moving, "seq", 2 * (c & -c)))
    c = inner[-1]
    (d_mine, u_mine), (b_own,), (moving,) = together(
        "phase_5",
        (divide_kernel, [a_pair, a_far], [quarters, quarters]),
        (sum_kernel, [b_keep, b_got], [at_part]),
        norm_job(c, arrived[c]),
    )
    b_own = over_rest(b_own)
    d_y, u_x = exchange(d_mine, *bit_y), exchange(u_mine, *bit_x)
    b_near = exchange(b_own, *bit_w)
    (moving,) = chain.hold(exchange(moving, "seq", 2 * (c & -c)))
    arrived[c & (c - 1)].append(moving)

    (d_near, u_near), (b_pair,), (moving,) = together(
        "phase_6",
        (join_kernel, [d_mine, d_y, u_mine, u_x], [piece, piece]),
        (pair_kernel, [b_own, b_near], [two_b]),
        norm_job(top, arrived[top]),
    )
    d_far, u_far = exchange(d_near, *bit_x), exchange(u_near, *bit_y)
    b_far = exchange(b_pair, *bit_z)
    moving = exchange(moving, "seq", 2 * top)
    d_far, u_far = chain.hold(d_far, u_far)

    (one_mine, two_mine), (nearest,) = together(
        "phase_7", (attend_divide_kernel, [b_pair, b_far], [one_shape, two_shape]), norm_job(1, [])
    )
    one_y, two_x = exchange(one_mine, *bit_y), exchange(two_mine, *bit_x)
    nearest = exchange(chain.hold(nearest)[0], "seq", 2)
    (moving,) = chain.hold(moving)
    ((one_near, two_near),) = together(
        "phase_8",
        (
            attend_join_kernel, [one_mine, one_y, two_mine, two_x],
            [made((8 * n, width), BF16), made((8 * n + 16, width), BF16)],
        ),
    )
    one_far, two_far = exchange(one_near, *bit_x), exchange(two_near, *bit_y)
    d_near_o, u_near_o = chain.hold(*other_core(d_near, u_near))
    grad_down, grad_up = unpack(False, d_near, d_near_o, u_near, u_near_o, [])
    d_far_o, u_far_o = chain.hold(*other_core(d_far, u_far))
    grad_down, grad_up = unpack(True, d_far, d_far_o, u_far, u_far_o, [grad_down, grad_up])
    far_held = chain.hold(one_far, two_far, nearest)
    nearest = far_held[2]
    one_near_o, two_near_o = other_core(*chain.hold(one_near, two_near))
    one_far_o, two_far_o = other_core(*far_held[:2])
    input_grad = call(
        last_kernel, [tokens_v, vectors, mid_grad, *dn_m, dn_r, *arrived[0], moving, nearest], [token_block],
        us=0.1, limit=LIMITS[4], name="input_grad", scalars=0, extra=[chain.token],
    )[0]
    one_all = [one_near, one_far, one_near_o, one_far_o]
    two_all = [two_near, two_far, two_near_o, two_far_o]
    square = made((width, width), F32)
    run = functools.partial(call, unpack_attend_kernel)
    thin = made((1, width), F32)
    results = chain(
        run, [sp] + one_all + two_all, [square] * 4 + [thin] * 3 + [made((1, hidden), F32)] + [thin] * 5,
        scratch=[pltpu.VMEM((PIECES, width), F32)], us=0.1, limit=LIMITS[4], name="unpack_attend",
    )
    grad_query, grad_key, grad_value, grad_out_proj = results[:4]
    lines = [r.reshape(-1) for r in results[4:]]

    return (outputs, input_grad, grad_query, grad_key, grad_value, grad_out_proj, grad_up, grad_down, *lines)


def solution(mesh):
    split, row, copied = P("dp", "seq", None), P("dp"), P()
    return jax.shard_map(
        body,
        mesh=mesh,
        in_specs=(split, split, row, P("dp", None)) + (copied,) * 15,
        out_specs=(split, split) + (copied,) * 15,
        check_vma=False,
    )
```

```python
import functools

import jax
import jax.numpy as jnp
from jax import lax
from jax.experimental import pallas as pl
from jax.experimental.pallas import tpu as pltpu
from jax.sharding import PartitionSpec as P

HEADS = 8
EPSILON = 1e-06
MASKED = -1e30
MIB = 1024 * 1024
LIMITS = (16, 20, 20, 26, 20)
PIECES = 16
GROUP = 4
BACK_US = 0.05
BF16 = jnp.bfloat16
F32 = jnp.float32
GELU_C = 0.7978845608028654
GELU_A = 0.044715


def nn(a, b):
    return jnp.dot(a, b, preferred_element_type=F32)


def nt(a, b):
    return lax.dot_general(a, b, (((1,), (1,)), ((), ())), preferred_element_type=F32)


def tn(a, b):
    return lax.dot_general(a, b, (((0,), (0,)), ((), ())), preferred_element_type=F32)


def normalize(values):
    center = values - jnp.mean(values, axis=-1, keepdims=True)
    scale = lax.rsqrt(jnp.mean(center * center, axis=-1, keepdims=True) + EPSILON)
    return center * scale, scale


def norm_back(cotangent, unit, scale, gain):
    g = cotangent * gain
    return scale * (
        g
        - jnp.mean(g, axis=-1, keepdims=True)
        - unit * jnp.mean(g * unit, axis=-1, keepdims=True)
    )


def segments(pos, offsets, crop, row):
    count = offsets.shape[1]
    seg = jnp.zeros(pos.shape, jnp.int32)
    for j in range(count):
        seg += (pos >= offsets[row, j]).astype(jnp.int32)
    return seg + count * (pos >= crop[row]).astype(jnp.int32)


def positions(sp, chunk, tok, shape, dim):
    start = (sp[4] ^ chunk) * (2 * tok)
    i = lax.broadcasted_iota(jnp.int32, shape, dim)
    return i + jnp.where(i < tok, start + sp[0] * tok, start + sp[1] * tok - tok)


def half_of(which, width):
    return pl.ds(pl.multiple_of(which * width, 128), width)


def padded(lines):
    return jnp.concatenate(lines + [jnp.zeros((16 - len(lines), lines[0].shape[1]), F32)], axis=0)


def load_kernel(halved, sp, *refs):
    count = len(halved)
    sources, targets, sems = refs[:count], refs[count : 2 * count], refs[2 * count :]
    copies = []
    for half, source, target, sem in zip(halved, sources, targets, sems):
        if half:
            source = source.at[:, half_of(sp[0], source.shape[1] // 2)]
        copies.append(pltpu.make_async_copy(source, target, sem))
    for copy in copies:
        copy.start()
    for copy in copies:
        copy.wait()


def chunk_kernel(chunk, last, tok, rows, *refs):
    refs = list(refs)
    first = chunk == 0
    sp, offsets, crop, xm, xo, vectors, weights = refs[:7]
    refs = refs[7:]
    if not first:
        qm_in, m_in, l_in, acc_in = refs[:4]
        refs = refs[4:]
    k_out, v_out, kt_out, nt_out = refs[:4]
    refs = refs[4:]
    if first:
        qm_out = refs.pop(0)
    if last:
        lse_out, ot_out, att_m, att_o = refs[:4]
    else:
        m_out, l_out, acc_out = refs
    half = weights.shape[2]
    heads = HEADS // 2
    size = half // heads
    chip = 2 * tok
    for at, x in ((0, xm), (tok, xo)):
        values = x[...].reshape(rows * tok, -1).astype(F32)
        unit, _ = normalize(values)
        normed = unit * vectors[0:1, :] + vectors[1:2, :]
        low = normed.astype(BF16)
        k = nn(low, weights[1])
        v = (nn(low, weights[2]) + vectors[3:4, half_of(sp[0], half)]).astype(BF16)
        if first:
            q = ((nn(low, weights[0]) + vectors[2:3, half_of(sp[0], half)]).astype(BF16).astype(F32) * size**-0.5).astype(BF16)
            lane = lax.broadcasted_iota(jnp.int32, (tok, 2 * size), 1)
        for r in range(rows):
            part = slice(r * tok, (r + 1) * tok)
            k_out[r, at : at + tok, :] = k[part].astype(BF16)
            v_out[r, at : at + tok, :] = v[part]
            kt_out[r, :, at : at + tok] = k[part].T.astype(BF16)
            nt_out[r, :, at : at + tok] = normed[part].T.astype(BF16)
            if first:
                for h in range(heads):
                    pair = q[part, (h // 2) * 2 * size : (h // 2 + 1) * 2 * size]
                    keep = (lane >= size) if h % 2 else (lane < size)
                    qm_out[r * heads + h, at : at + tok, :] = jnp.where(keep, pair, jnp.zeros_like(pair))
    qm = qm_out if first else qm_in
    for r in range(rows):
        key_seg = segments(positions(sp, chunk, tok, (chip, chip), 0), offsets, crop, r)
        query_seg = segments(positions(sp, 0, tok, (1, chip), 1), offsets, crop, r)
        bias = jnp.where(key_seg == query_seg, 0.0, MASKED)
        outs = []
        spot = [r * heads + h for h in range(heads)]
        pairs = [slice((h // 2) * 2 * size, (h // 2 + 1) * 2 * size) for h in range(heads)]
        s = [nt(k_out[r, :, pairs[h]], qm[spot[h]]) + bias for h in range(heads)]
        tops = [jnp.max(a, axis=0, keepdims=True) for a in s]
        if not first:
            olds = [m_in[at] for at in spot]
            tops = [jnp.maximum(a, b) for a, b in zip(olds, tops)]
        p = [jnp.exp(a - b) for a, b in zip(s, tops)]
        totals = [jnp.sum(a, axis=0, keepdims=True) for a in p]
        addeds = [tn(v_out[r, :, pairs[h]], p[h].astype(BF16)) for h in range(heads)]
        for h, at in enumerate(spot):
            added = addeds[h][(h % 2) * size : (h % 2 + 1) * size]
            total = totals[h]
            if not first:
                keep = jnp.exp(olds[h] - tops[h])
                total += l_in[at] * keep
                added += acc_in[at] * keep
            if last:
                lse_out[at] = tops[h] + jnp.log(total)
                out = added / total
                ot_out[at] = out
                outs.append(out)
            else:
                m_out[at] = tops[h]
                l_out[at] = total
                acc_out[at] = added
        if last:
            att = jnp.concatenate(outs, axis=0).T.astype(BF16)
            att_m[r] = att[:tok]
            att_o[r] = att[tok:]


def feed_forward_half(sp, which, normed, g, up, down, bup, hid, pre, at, vec, total, back):
    half = up.shape[1] // 2
    row = min(512, half)
    block = min(512, row)
    count = half // block
    cols = [pl.ds(pl.multiple_of(sp[which] * half + j * block, 128), block) for j in range(count)]
    for first in range(0, count, 2):
        js = range(first, min(first + 2, count))
        us = [nn(normed, up[:, cols[j]]) + bup[:, cols[j]] for j in js]
        gs = [nt(g, down[cols[j], :]) for j in js]
        outs, pres = [], []
        for j, u, back_in in zip(js, us, gs):
            square = u * u
            plus = 1.0 + jnp.tanh(u * (GELU_C + GELU_C * GELU_A * square))
            low = 0.5 * u
            hidden = (low * plus).astype(BF16)
            slope = plus * (0.5 + low * (2.0 - plus) * (GELU_C + 3 * GELU_C * GELU_A * square))
            grad = (back_in * slope).astype(BF16)
            hid[:, j * block : (j + 1) * block] = hidden
            pre[:, at + j * block : at + (j + 1) * block] = grad
            outs.append(hidden)
            pres.append(grad)
            line = jnp.sum(grad.astype(F32), axis=0, keepdims=True)
            lane = j * block % row
            vec[pl.ds(sp[which] * (half // row) + j * block // row, 1), lane : lane + block] = line
        for j, hidden, grad in zip(js, outs, pres):
            more, less = nn(hidden, down[cols[j], :]), nt(grad, up[:, cols[j]])
            total = more if total is None else total + more
            back = less if back is None else back + less
    return total, back


def ffn_first_kernel(
    sp, att_m, att_o, wo, tokens, cot, up, down, b_out, bup, gain, shift, mid_out, normed_out, send, total_out, back_out, vec
):
    rows, tok, width = tokens.shape
    flat = rows * tok
    quarter = width // 2
    mine = pl.ds(pl.multiple_of(sp[0] * quarter, 128), quarter)
    other = pl.ds(pl.multiple_of(sp[1] * quarter, 128), quarter)
    mid = (
        tokens[...].reshape(flat, width).astype(F32)
        + nn(att_m[...].reshape(flat, -1), wo[mine, :])
        + nn(att_o[...].reshape(flat, -1), wo[other, :])
        + b_out[...]
    )
    mid_out[...] = mid
    unit, _ = normalize(mid)
    normed = (unit * gain[...] + shift[...]).astype(BF16)
    normed_out[...] = normed
    half = up.shape[1] // 2
    send[:, 2 * half :] = normed
    vec[...] = jnp.zeros_like(vec)
    g = cot[...].reshape(flat, width)
    total_out[...], back_out[...] = feed_forward_half(
        sp, 1, normed, g, up, down, bup, send, send, half, vec, None, None
    )


def ffn_second_kernel(
    sp, mid_in, normed_in, cot, up, down, bup, b_down, gain, total_in, back_in, vec_in, out, hid, pre, mid_grad, branch, vec
):
    rows, tok, width = cot.shape
    flat = rows * tok
    g = cot[...].reshape(flat, width)
    vec[...] = vec_in[...]
    total, back = feed_forward_half(
        sp, 0, normed_in[...], g, up, down, bup, hid, pre, 0, vec, total_in[...], back_in[...]
    )
    mid = mid_in[...]
    out[...] = (mid + total + b_down[...]).astype(BF16).reshape(rows, tok, width)
    unit, scale = normalize(mid)
    gf = g.astype(F32)
    grad = gf + norm_back(back, unit, scale, gain[...])
    mid_grad[...] = grad
    low = grad.astype(BF16)
    branch[...] = low.reshape(rows, tok, width)
    vec[4:5, :] = jnp.sum(gf, axis=0, keepdims=True)
    vec[5:6, :] = jnp.sum(back * unit, axis=0, keepdims=True)
    vec[6:7, :] = jnp.sum(back, axis=0, keepdims=True)
    vec[7:8, :] = jnp.sum(low.astype(F32), axis=0, keepdims=True)


def ffn_grad_kernel(send, sp, hid_m, pre_m, n_m, got, g_m, g_o, d, u):
    half = hid_m.shape[1]
    width = g_m.shape[1]
    per = PIECES // 2
    rd, ru = half // PIECES, width // PIECES
    part = (sp[2] // per) ^ send
    cols = half_of(part, half // 2)
    gd = tn(hid_m[:, cols], g_m[...]) + tn(got[:, cols], g_o[...])
    part = (sp[3] // per) ^ send
    own = half_of(part, width // 2)
    others = pl.ds(pl.multiple_of(2 * half + part * (width // 2), 128), width // 2)
    gu = tn(n_m[:, own], pre_m[...]) + tn(got[:, others], got[:, half : 2 * half])
    for p in range(per):
        d[(sp[2] & (per - 1)) ^ p] = gd[p * rd : (p + 1) * rd].astype(BF16)
        at = (sp[3] & (per - 1)) ^ p
        for i in range(half // width):
            u[at, i * ru : (i + 1) * ru, :] = gu[p * ru : (p + 1) * ru, i * width : (i + 1) * width].astype(BF16)


def attend_back_kernel(stations, tok, rows_here, whole, last, *refs):
    refs = list(refs)

    def take(count):
        got = refs[:count]
        del refs[:count]
        return got

    sp, offsets, crop, br_m, br_o, wo, qm, lse, ot, weights = take(10)
    k, v, kt, norm_t = (take(stations) for _ in range(4))
    sums_in = take(5) if rows_here[0] else None
    if last:
        vectors, vec_in = take(2)
        before = take(rows_here[0])
    dn_m = take(len(rows_here))
    dn_o = take(1 if last else len(rows_here))
    if last:
        ones, twos = take(2), take(2)
    gq, gk, gv, go, sums = take(5)
    heads = HEADS // 2
    _, width, half = weights.shape
    size = half // heads
    chip = 2 * tok
    block = min(4, stations)
    blocks = stations // block

    made_here = [0.0] * 5
    for place, row in enumerate(rows_here):
        at = row if whole else 0
        branch = jnp.concatenate([br_m[at], br_o[at]], axis=0)
        do = nt(branch, wo[half_of(sp[0], half), :]).astype(BF16)
        dot = do.astype(F32).T
        lane = lax.broadcasted_iota(jnp.int32, (chip, 2 * size), 1)
        head_at = at * heads
        out_t = jnp.concatenate([ot[head_at + h] for h in range(heads)], axis=0).astype(BF16)
        go_row = nn(out_t, branch)
        query_seg = segments(positions(sp, 0, tok, (1, chip), 1), offsets, crop, row)
        biases = []
        for chunk in range(stations):
            key_seg = segments(positions(sp, chunk, tok, (chip, chip), 0), offsets, crop, row)
            biases.append(jnp.where(key_seg == query_seg, 0.0, MASKED))
        dqt = []
        dks = [[] for _ in range(blocks)]
        dvs = [[] for _ in range(blocks)]
        for pair in range(heads // 2):
            lanes = slice(pair * 2 * size, (pair + 1) * 2 * size)
            dk = [None] * blocks
            dv = [None] * blocks
            for h in (2 * pair, 2 * pair + 1):
                wide = do[:, lanes]
                dm = jnp.where((lane >= size) if h % 2 else (lane < size), wide, jnp.zeros_like(wide))
                delta = jnp.sum(ot[head_at + h] * dot[h * size : (h + 1) * size], axis=0, keepdims=True)
                dq = None
                for b in range(blocks):
                    chunks = range(b * block, (b + 1) * block)
                    keys = jnp.concatenate([k[c][at, :, lanes] for c in chunks], axis=0)
                    values = jnp.concatenate([v[c][at, :, lanes] for c in chunks], axis=0)
                    keys_t = jnp.concatenate([kt[c][at, h * size : (h + 1) * size, :] for c in chunks], axis=1)
                    bias = jnp.concatenate([biases[c] for c in chunks], axis=0)
                    p = jnp.exp(nt(keys, qm[head_at + h]) + bias - lse[head_at + h])
                    ds = (p * (nt(values, dm) - delta)).astype(BF16)
                    dv_h, dk_h = nn(p.astype(BF16), dm), nn(ds, qm[head_at + h])
                    dv[b] = dv_h if dv[b] is None else dv[b] + dv_h
                    dk[b] = dk_h if dk[b] is None else dk[b] + dk_h
                    more = nn(keys_t, ds)
                    dq = more if dq is None else dq + more
                dqt.append(dq)
            for b in range(blocks):
                dks[b].append(dk[b].astype(BF16))
                dvs[b].append(dv[b].astype(BF16))
        dq = (jnp.concatenate(dqt, axis=0) * size**-0.5).T.astype(BF16)
        gq_row = nn(norm_t[0][at], dq)
        gk_row = gv_row = sum_k = sum_v = 0.0
        for b in range(blocks):
            dk = jnp.concatenate(dks[b], axis=1)
            dv = jnp.concatenate(dvs[b], axis=1)
            normed = jnp.concatenate([norm_t[c][at] for c in range(b * block, (b + 1) * block)], axis=1)
            gk_row += nn(normed, dk)
            gv_row += nn(normed, dv)
            sum_k += jnp.sum(dk.astype(F32), axis=0, keepdims=True)
            sum_v += jnp.sum(dv.astype(F32), axis=0, keepdims=True)
            dn = nt(dk, weights[1]) + nt(dv, weights[2])
            for i in range(block):
                part = dn[i * chip : (i + 1) * chip]
                if b + i == 0:
                    part += nt(dq, weights[0])
                dn_m[place][b * block + i] = part[:tok].astype(BF16)
                dn_o[0 if last else place][(row * stations if last else 0) + b * block + i] = part[tok:].astype(BF16)
        sum_q = jnp.sum(dq.astype(F32), axis=0, keepdims=True)
        rest = jnp.zeros((5, half), F32)
        values = (gq_row, gk_row, gv_row, go_row, jnp.concatenate([sum_q, sum_v, sum_k, rest]))
        made_here = [a + b for a, b in zip(made_here, values)]
    for i, (ref, value) in enumerate(zip((gq, gk, gv, go, sums), made_here)):
        ref[...] = value if sums_in is None else value + sums_in[i][...]
    if not last:
        return

    for r, part in enumerate(before):
        dn_o[0][r * stations : (r + 1) * stations] = part[...]
    vec = refs[0]
    lane = lax.broadcasted_iota(jnp.int32, (2, width), 1)
    both = sums[0:2, :]
    both = jnp.concatenate([both, both], axis=1)
    vec[0:2, :] = jnp.where((lane >= half) == (sp[0] == 1), both, 0.0)
    vec[2:3, :] = vec_in[7:8, :]
    vec[3:4, :] = vec_in[4:5, :]
    vec[4:8, :] = vec_in[0:4, :]
    vec[10:12, :] = vec_in[5:7, :]
    vec[12:16, :] = jnp.zeros((4, width), F32)
    wide = [weights[i].astype(F32) for i in range(3)]
    shifts = sum(w * sums[i : i + 1, :] for w, i in zip(wide, (0, 2, 1)))
    gains = sum(w * g[...] for w, g in zip(wide, (gq, gk, gv)))

    def across(values):
        folded = sum(values[:, i * 128 : (i + 1) * 128] for i in range(half // 128))
        return jnp.sum(folded.T, axis=0, keepdims=True)

    shift_grad = across(shifts)
    vec[9:10, :] = shift_grad
    vec[8:9, :] = (across(gains) - vectors[1:2, :] * shift_grad) / vectors[0:1, :]
    n = width // PIECES
    low = n // 2
    per = PIECES // 2
    for slot in range(PIECES):
        one, two = ones[slot // per], twos[slot // per]
        base = slot % per * n
        piece = sp[2] ^ slot
        part = pl.ds(pl.multiple_of(piece * n, n), n)
        one[base : base + n, :half] = gq[part, :].astype(BF16)
        one[base : base + n, half:] = gk[part, :].astype(BF16)
        piece = sp[3] ^ slot
        first = pl.ds(pl.multiple_of(piece * n, n), low)
        second = pl.ds(pl.multiple_of(piece * n + low, low), low)
        two[base : base + low, :half] = gv[first, :].astype(BF16)
        two[base : base + low, half:] = gv[second, :].astype(BF16)
        two[base + low : base + n, :] = go[pl.ds(pl.multiple_of(piece * low, low), low), :].astype(BF16)
    for i, two in enumerate(twos):
        lines = [vec[pl.ds(sp[3] ^ (i * per + s), 1), :] for s in range(per)]
        two[per * n :, :] = padded(lines).astype(BF16)


def last_kernel(tokens, gain, mid_grad, *refs):
    out = refs[-1]
    rows, tok, width = tokens.shape
    flat = rows * tok
    unit, scale = normalize(tokens[...].reshape(flat, width).astype(F32))
    parts = []
    for r in range(rows):
        part = refs[r][0].astype(F32) + refs[rows][r * refs[0].shape[0]].astype(F32)
        for arrived in refs[rows + 1 : -1]:
            part += arrived[r].astype(F32)
        parts.append(part)
    grad = mid_grad[...] + norm_back(jnp.concatenate(parts, axis=0), unit, scale, gain[0:1, :])
    out[...] = grad.astype(BF16).reshape(rows, tok, width)


def unpack_ffn_kernel(far, sp, *refs):
    refs = list(refs)
    d_both, u_both = refs[0:2], refs[2:4]
    down, up, done, d_wide, u_wide, sems = refs[-6:]
    done[...] = jnp.zeros_like(done)
    _, rd, width = d_both[0].shape
    ru = up.shape[0] // PIECES
    half = down.shape[0] // 2
    count = PIECES // GROUP
    copies = []
    for which in range(2):
        for i in range(GROUP // 2):
            at = which * (GROUP // 2) + i
            group = (GROUP // 2 if far else 0) + i
            for k in range(count):
                slot = i * count + k
                place = (sp[2] ^ k) & (count - 1)
                rows = pl.ds(pl.multiple_of(place * rd, rd), rd)
                d_wide[at, rows, :] = d_both[which][slot].astype(F32)
                place = (sp[3] ^ k) & (count - 1)
                rows = pl.ds(pl.multiple_of(place * ru, ru), ru)
                for n in range(rd // ru):
                    part = u_both[which][slot, n * ru : (n + 1) * ru, :]
                    u_wide[at, rows, n * width : (n + 1) * width] = part.astype(F32)
            size = count * rd
            rows = pl.ds(pl.multiple_of(sp[which] * half + ((sp[2] // count) ^ group) * size, size), size)
            copies.append(pltpu.make_async_copy(d_wide.at[at], down.at[rows, :], sems.at[2 * at]))
            copies[-1].start()
            size = count * ru
            rows = pl.ds(pl.multiple_of(((sp[3] // count) ^ group) * size, size), size)
            copies.append(pltpu.make_async_copy(u_wide.at[at], up.at[rows, half_of(sp[which], half)], sems.at[2 * at + 1]))
            copies[-1].start()
    for copy in copies:
        copy.wait()


def unpack_attend_kernel(sp, *refs):
    gq, gk, gv, go, *lines = refs[8:]
    vec = lines.pop()
    ones, twos = (refs[0:2], refs[2:4]), (refs[4:6], refs[6:8])
    width = gq.shape[0]
    half = width // 2
    n = width // PIECES
    low = n // 2
    per = PIECES // 2
    for slot in range(PIECES):
        base = slot % per * n
        for which in range(2):
            one, two = ones[which][slot // per], twos[which][slot // per]
            cols = half_of(sp[which], half)
            piece = sp[2] ^ slot
            rows = pl.ds(pl.multiple_of(piece * n, n), n)
            gq[rows, cols] = one[base : base + n, :half].astype(F32)
            gk[rows, cols] = one[base : base + n, half:].astype(F32)
            piece = sp[3] ^ slot
            first = pl.ds(pl.multiple_of(piece * n, n), low)
            second = pl.ds(pl.multiple_of(piece * n + low, low), low)
            gv[first, cols] = two[base : base + low, :half].astype(F32)
            gv[second, cols] = two[base : base + low, half:].astype(F32)
            out_rows = pl.ds(pl.multiple_of(sp[which] * half + piece * low, low), low)
            go[out_rows, :] = two[base + low : base + n, :].astype(F32)
    for side in range(2):
        both = twos[0][side][per * n :, :].astype(F32) + twos[1][side][per * n :, :].astype(F32)
        for s in range(per):
            vec[pl.ds(sp[3] ^ (side * per + s), 1), :] = both[s : s + 1]
    for line, row in zip(lines, (0, 1, 2, 4, 3, 8, 9, 10, 11)):
        count = line.shape[1] // width
        for i in range(count):
            line[:, i * width : (i + 1) * width] = vec[row + i : row + i + 1, :]


def total(*values):
    return sum(v.astype(F32) for v in values).astype(BF16)


def sum_kernel(*refs):
    refs[-1][...] = total(*[r[...] for r in refs[:-1]])


def upper_kernel(*refs):
    count = len(refs) // 3
    for i, out in enumerate(refs[2 * count :]):
        keep, got = refs[2 * i : 2 * i + 2]
        half = keep.shape[0] // 2
        out[...] = total(keep[half:], got[half:])


def quarter_kernel(d_keep, d_got, d_last, u_keep, u_got, u_last, keep, send):
    rd = d_keep.shape[1]
    half = keep.shape[0]
    for i in range(2 * half):
        out = send if i >= half else keep
        out[i % half, :rd] = total(d_keep[i], d_got[i], d_last[i])
        out[i % half, rd:] = total(u_keep[i], u_got[i], u_last[i])


def halve_kernel(keep, got, out_keep, out_send):
    out_keep[...] = total(keep[0], got[0])
    out_send[...] = total(keep[1], got[1])


def pair_kernel(one, two, out):
    out[0] = one[...]
    out[1] = two[...]


def divide_kernel(one, two, d, u):
    rd = d.shape[1]
    for i in range(d.shape[0]):
        part = (one if i < 2 else two)[i % 2]
        d[i] = part[:rd]
        u[i] = part[rd:]


def join_kernel(*refs):
    count = len(refs) // 3
    for i, out in enumerate(refs[2 * count :]):
        one, two = refs[2 * i : 2 * i + 2]
        out[: one.shape[0]] = one[...]
        out[one.shape[0] :] = two[...]


def attend_upper_kernel(one_keep, one_got, two_keep, two_got, one, two):
    n = one.shape[0]
    one[...] = total(one_keep[n:], one_got[n:])
    two[:n] = total(two_keep[n : 2 * n], two_got[n : 2 * n])
    lines = total(two_keep[2 * n :], two_got[2 * n :]).astype(F32)
    two[n:] = fill(lines[4:8])


def fill(lines):
    return jnp.concatenate([lines, jnp.zeros((16 - lines.shape[0], lines.shape[1]), F32)], axis=0).astype(BF16)


def attend_quarter_kernel(one_keep, one_got, one_last, two_keep, two_got, two_last, keep, send):
    count = 2 * keep.shape[0]
    n = one_last.shape[0] // count
    lines = total(two_keep[2 * count * n :], two_got[2 * count * n :], two_last[count * n :]).astype(F32)
    for i in range(count):
        out = (keep, send)[i // 2]
        part = slice(i * n, (i + 1) * n)
        out[i % 2, :n] = total(one_keep[part], one_got[part], one_last[part])
        out[i % 2, n : 2 * n] = total(two_keep[part], two_got[part], two_last[part])
        out[i % 2, 2 * n :] = jnp.broadcast_to(lines[i : i + 1], (16, lines.shape[1])).astype(BF16)


def attend_divide_kernel(first, second, one, two):
    n = one.shape[0] // 4
    lines = []
    for i in range(4):
        part = (first if i < 2 else second)[i % 2]
        one[i * n : (i + 1) * n] = part[:n]
        two[i * n : (i + 1) * n] = part[n : 2 * n]
        lines.append(part[2 * n :].astype(F32)[:1])
    two[4 * n :] = padded(lines).astype(BF16)


def attend_join_kernel(one_a, one_b, two_a, two_b, one, two):
    n = one_a.shape[0]
    one[:n] = one_a[...]
    one[n:] = one_b[...]
    two[:n] = two_a[:n]
    two[n : 2 * n] = two_b[:n]
    lines = jnp.concatenate([two_a[n:].astype(F32)[:4], two_b[n:].astype(F32)[:4]], axis=0)
    two[2 * n :] = fill(lines)


def norm_grad_kernel(chunk, rows, *refs):
    out = refs[-1]
    stations = refs[0].shape[0]
    for r in range(rows):
        out[r] = total(refs[r][chunk], refs[rows][r * stations + chunk], *[a[r] for a in refs[rows + 1 : -1]])


VMEM = pl.BlockSpec(memory_space=pltpu.VMEM)
SMEM = pl.BlockSpec(memory_space=pltpu.SMEM)
HBM = pl.BlockSpec(memory_space=pltpu.HBM)
ANY = pl.BlockSpec(memory_space=pl.ANY)


def call(kernel, ins, outs, scratch=(), us=1.0, limit=16, name=None, scalars=1, specs=None, grid=(), out_specs=None, aliases=None, extra=()):
    count = len(ins)

    def body_of(*refs):
        kernel(*refs[:count], *refs[count + len(extra) :])

    return pl.pallas_call(
        body_of,
        grid=grid,
        in_specs=[SMEM] * scalars + (specs or [VMEM] * (count - scalars)) + [ANY] * len(extra),
        out_specs=out_specs or [VMEM] * len(outs),
        input_output_aliases=aliases or {},
        out_shape=list(outs),
        scratch_shapes=list(scratch),
        compiler_params=pltpu.CompilerParams(vmem_limit_bytes=limit * MIB),
        cost_estimate=pl.CostEstimate(flops=int(us * 1.1e9), bytes_accessed=0, transcendentals=0),
        name=name,
    )(*ins, *extra)


def load(sp, arrays, halved, name, limit=16):
    shapes = [a.shape[:-1] + (a.shape[-1] // (2 if h else 1),) for a, h in zip(arrays, halved)]
    return call(
        functools.partial(load_kernel, halved), [sp] + arrays, [made(s, a.dtype) for s, a in zip(shapes, arrays)],
        scratch=[pltpu.SemaphoreType.DMA] * len(arrays), us=2.0, limit=limit, name=name, specs=[HBM] * len(arrays),
    )


def made(shape, dtype):
    return jax.ShapeDtypeStruct(shape, dtype)


def exchange(array, axis, mask):
    count = lax.axis_size(axis)
    return lax.ppermute(array, axis, [(i, i ^ mask) for i in range(count)])


def merge(kernel, ins, outs, name, extra=()):
    specs = [SMEM if a.dtype == jnp.int32 else VMEM for a in ins]
    return call(kernel, list(ins), list(outs), us=0.05, limit=8, name=name, scalars=0, specs=specs, extra=extra)


def tied(*arrays):
    return lax.optimization_barrier(arrays)


class Chain:
    def __init__(self, token):
        self.token = token

    def __call__(self, function, *args, **kwargs):
        outs = list(function(*args, extra=[self.token], **kwargs))
        self.token = outs[-1]
        return outs

    def hold(self, *arrays):
        *arrays, self.token = tied(*arrays, self.token)
        return arrays


def my_id(bits):
    out = 0
    for axis, mask in bits:
        out = out * 2 + jnp.where((lax.axis_index(axis) & mask) != 0, 1, 0)
    return out


def body(
    tokens, grad_out, crop, offsets, w_query, w_key, w_value, w_out, w_up, w_down, b_query, b_value,
    b_out, b_up, b_down, gain_one, shift_one, gain_two, shift_two,
):
    rows, tok, width = tokens.shape
    seq_count, dp_count = lax.axis_size("seq"), lax.axis_size("dp")
    stations = seq_count // 2
    hidden = w_up.shape[1]
    half = width // 2
    heads = HEADS // 2
    size = half // heads
    chip = 2 * tok
    flat = rows * tok
    small = stations <= 4
    seq = lax.axis_index("seq")
    core, station = seq % 2, seq // 2
    line = lambda v: v.reshape(1, -1)

    dp_bits = [("dp", 1 << i) for i in range(dp_count.bit_length() - 1)]
    st_bits = [("seq", 2 << i) for i in range(stations.bit_length() - 1)]
    bit_x, bit_y = dp_bits[:2]
    rest = dp_bits[2:] + st_bits[2:]
    ids = [my_id([bit_x, bit_y] + st_bits[:2]), my_id([bit_y, bit_x] + st_bits[:2])]
    sp = jnp.stack([core, 1 - core, *ids, station]).astype(jnp.int32)

    mine = lambda a: lax.dynamic_slice_in_dim(a, core * half, half, a.ndim - 1)
    weights = jnp.stack([mine(w_query), mine(w_key), mine(w_value)])
    vectors = jnp.stack([gain_one, shift_one, b_query, b_value] + [jnp.zeros_like(gain_one)] * 4)
    state = []
    kept = [[None] * stations for _ in range(4)]
    blocks = {0: tokens}
    turns = [int(f"{i:0{stations.bit_length() - 1}b}"[::-1], 2) for i in range(stations)]
    for at, j in enumerate(turns):
        if j:
            low = j & -j
            block = blocks[j] = exchange(blocks[j ^ low], "seq", 2 * low)
            if at == 1 or at == stations - 1:
                block, state[-1] = tied(block, state[-1])
                blocks[j] = block
        else:
            block = tokens
        other = exchange(block, "seq", 1)
        first, last = at == 0, at == stations - 1
        ins = [sp, offsets, crop, block, other, vectors, weights] + ([] if first else state)
        outs = [
            made((rows, chip, half), BF16),
            made((rows, chip, half), BF16),
            made((rows, half, chip), BF16),
            made((rows, width, chip), BF16),
        ]
        if first:
            outs += [made((rows * heads, chip, 2 * size), BF16)]
        stat = made((rows * heads, 1, chip), F32)
        acc = made((rows * heads, size, chip), F32)
        if last:
            outs += [stat, acc, made((rows, tok, half), BF16), made((rows, tok, half), BF16)]
        else:
            outs += [stat, stat, acc]
        got = call(
            functools.partial(chunk_kernel, j, last, tok, rows), ins, outs,
            us=0.05, limit=LIMITS[0], name=f"attend_chunk_{j}", scalars=3,
        )
        for where, array in zip(kept, got[:4]):
            where[j] = array
        got = got[4:]
        if first:
            query, got = got[0], got[1:]
        if not last:
            state = [query] + list(got)
        if at == 0:
            sp_b, state[-1] = tied(sp, state[-1])
            tokens_v, g_v, wo, up, down, bo, bu, bd, gain_b, shift_b = load(
                sp_b,
                [tokens, grad_out, w_out, w_up, w_down, line(b_out), line(b_up), line(b_down), line(gain_two), line(shift_two)],
                [False] * 10, "load_feed_forward",
            )
            g_other = exchange(g_v, "seq", 1)
            state[-1], up = tied(state[-1], up)
        if at == 1:
            state[-1], g_other = tied(state[-1], g_other)
            g_other = g_other.reshape(flat, width)
    lse, out_t, att_m, att_o = got
    att_r = exchange(att_o, "seq", 1)

    wide = made((flat, width), F32)
    vec8 = made((8, width), F32)
    mid, normed_two, send, total, back, vec_a = call(
        ffn_first_kernel, [sp, att_m, att_r, wo, tokens_v, g_v, up, down, bo, bu, gain_b, shift_b],
        [wide, made((flat, width), BF16), made((flat, hidden + width), BF16), wide, wide, vec8],
        us=4.0, limit=LIMITS[1], name="feed_forward_a",
    )
    got = exchange(send, "seq", 1)
    outputs, hid_m, pre_m, mid_grad, branch, vec_ffn = call(
        ffn_second_kernel, [sp, mid, normed_two, g_v, up, down, bu, bd, gain_b, total, back, vec_a],
        [made((rows, tok, width), BF16), made((flat, hidden // 2), BF16), made((flat, hidden // 2), BF16), wide,
         made((rows, tok, width), BF16), vec8],
        us=4.0, limit=LIMITS[1], name="feed_forward_b",
    )
    branch_r = exchange(branch, "seq", 1)
    piece = made((PIECES // 2, hidden // 2 // PIECES, width), BF16)
    ins = [sp, hid_m, pre_m, normed_two, got, g_v.reshape(flat, width), g_other]
    d_send, u_send = call(
        functools.partial(ffn_grad_kernel, 1), ins, [piece, piece], us=3.0, limit=LIMITS[2], name="feed_forward_grad_sent"
    )
    d_send, u_send, branch_r = tied(d_send, u_send, branch_r)
    chain = Chain(d_send)
    d_keep, u_keep = chain(
        functools.partial(call, functools.partial(ffn_grad_kernel, 0)), ins, [piece, piece], us=0.05, limit=LIMITS[2],
        name="feed_forward_grad_kept",
    )

    q = PIECES // GROUP
    d_got, u_got = exchange(d_send, *bit_x), exchange(u_send, *bit_y)

    sums = []
    dn_m, dn_o, dn_r = [], [], []

    def together(name, *jobs):
        ins = [a for _, arrays, _ in jobs for a in arrays]
        outs = [s for _, _, shapes in jobs for s in shapes]

        def kernel(*refs):
            at, to = 0, len(ins)
            for one, arrays, shapes in jobs:
                one(*refs[at : at + len(arrays)], *refs[to : to + len(shapes)])
                at, to = at + len(arrays), to + len(shapes)

        res = iter(chain(functools.partial(merge, kernel), ins, outs, name))
        return [[next(res) for _ in shapes] for _, _, shapes in jobs]

    def norm_job(chunk, arrived):
        ins = [*dn_m, dn_r, *arrived]
        return (functools.partial(norm_grad_kernel, chunk, rows), ins, [made((rows, tok, width), BF16)])

    groups = [tuple(range(rows - 1)), (rows - 1,)] if small else [(r,) for r in range(rows)]
    for group in groups:
        r, last = group[-1], group[-1] == rows - 1
        arrays = [branch, branch_r, wo, query, lse, out_t, weights] + [a for part in kept for a in part]
        specs = [VMEM] * len(arrays)
        if not small:
            for i, a in enumerate(arrays):
                if a.ndim == 3 and a is not weights:
                    block_shape = (a.shape[0] // rows,) + a.shape[1:]
                    specs[i] = pl.BlockSpec(block_shape, functools.partial(lambda r, i: (r, 0, 0), r))
        tail = list(sums)
        if last:
            tail += [vectors, vec_ffn, *dn_o]
        part = made((stations, tok, width), BF16)
        grads = [made((width, half), F32)] * 3 + [made((half, width), F32), made((8, half), F32)]
        outs = [part] * (2 * len(group)) + grads
        scratch = []
        if last:
            outs = [part, made((rows * stations, tok, width), BF16)] + [made((width // 2, width), BF16)] * 2 + [made((width // 2 + 16, width), BF16)] * 2
            scratch = [pltpu.VMEM(g.shape, F32) for g in grads] + [pltpu.VMEM((16, width), F32)]
        run = functools.partial(call, functools.partial(attend_back_kernel, stations, tok, group, small, last))
        res = chain(
            run, [sp, offsets, crop] + arrays + tail, outs, scratch=scratch,
            us=BACK_US, limit=LIMITS[3] if small else 48, name=f"attend_back_{r}", scalars=3,
            specs=specs + [VMEM] * len(tail), grid=() if small else (1,),
        )
        if last:
            dn_m.append(res[0])
            dn_o.append(res[1])
        else:
            dn_m += res[: len(group)]
            dn_o += res[len(group) : 2 * len(group)]
            sums = list(res[2 * len(group) :])
        if r == rows - 2:
            quarters = made((q,) + piece.shape[1:], BF16)
            ((d_next, u_next),) = together(
                "add_quarters", (upper_kernel, [d_keep, d_got, u_keep, u_got], [quarters, quarters])
            )
            d_got2, u_got2 = exchange(d_next, *bit_y), exchange(u_next, *bit_x)
    one_keep, one_send, two_keep, two_send = res[2:]

    rd = hidden // 2 // PIECES
    n = width // PIECES
    ff_part, at_part = made((2 * rd, width), BF16), made((2 * n + 16, width), BF16)
    two_of = lambda a: made((2,) + a.shape, BF16)
    token_block = made((rows, tok, width), BF16)
    bit_z, bit_w = st_bits[:2]

    def over_rest(part):
        for i, (where, mask) in enumerate(rest):
            got = exchange(part, where, mask)
            ((part,),) = together(f"add_rest_{i}", (sum_kernel, [part, got], [made(part.shape, BF16)]))
        return part

    def unpack(far, d, d_other, u, u_other, before):
        ins = [sp, d, d_other, u, u_other] + before
        scratch = [
            pltpu.VMEM((GROUP, q * rd, width), F32), pltpu.VMEM((GROUP, q * width // PIECES, hidden // 2), F32),
            pltpu.SemaphoreType.DMA((2 * GROUP,)),
        ]
        return chain(
            functools.partial(call, functools.partial(unpack_ffn_kernel, far)), ins,
            [made((hidden, width), F32), made((width, hidden), F32), made((8, 128), F32)], scratch=scratch, us=0.1,
            limit=LIMITS[4], name="unpack_feed_forward", specs=[VMEM] * 4 + [HBM] * len(before),
            out_specs=[HBM] * 2 + [VMEM], aliases={5: 0, 6: 1} if before else None,
        )[:2]

    def other_core(*arrays):
        return [exchange(a, "seq", 1) for a in arrays]

    two_a, two_b = two_of(ff_part), two_of(at_part)
    ((a_keep, a_send),) = together(
        "phase_1", (quarter_kernel, [d_keep, d_got, d_got2, u_keep, u_got, u_got2], [two_a, two_a])
    )
    one_send, two_send, dn_o = chain.hold(one_send, two_send, dn_o[-1])
    a_got = exchange(a_send, *bit_z)
    one_got, two_got = exchange(one_send, *bit_x), exchange(two_send, *bit_y)
    (dn_r,) = chain.hold(*other_core(dn_o))

    one_shape, two_shape = made((4 * n, width), BF16), made((4 * n + 16, width), BF16)
    (a_keep, a_send), (one_next, two_next) = together(
        "phase_2",
        (halve_kernel, [a_keep, a_got], [ff_part] * 2),
        (attend_upper_kernel, [one_keep, one_got, two_keep, two_got], [one_shape, two_shape]),
    )
    a_got = exchange(a_send, *bit_w)
    one_got2, two_got2 = exchange(one_next, *bit_y), exchange(two_next, *bit_x)

    (a_own,), (b_keep, b_send) = together(
        "phase_3",
        (sum_kernel, [a_keep, a_got], [ff_part]),
        (attend_quarter_kernel, [one_keep, one_got, one_got2, two_keep, two_got, two_got2], [two_b, two_b]),
    )
    a_own = over_rest(a_own)
    a_near = exchange(a_own, *bit_w)
    b_got = exchange(b_send, *bit_z)

    (a_pair,), (b_keep, b_send) = together(
        "phase_4",
        (pair_kernel, [a_own, a_near], [two_a]),
        (halve_kernel, [b_keep, b_got], [at_part] * 2),
    )
    a_far = exchange(a_pair, *bit_z)
    b_got = exchange(b_send, *bit_w)

    arrived = {c: [] for c in range(stations)}
    top = stations // 2
    inner = [c for c in reversed(turns) if c not in (0, 1, top)]
    for c in inner[:-1]:
        ((moving,),) = together("norm_step", norm_job(c, arrived[c]))
        arrived[c & (c - 1)].append(exchange(moving, "seq", 2 * (c & -c)))
    c = inner[-1]
    (d_mine, u_mine), (b_own,), (moving,) = together(
        "phase_5",
        (divide_kernel, [a_pair, a_far], [quarters, quarters]),
        (sum_kernel, [b_keep, b_got], [at_part]),
        norm_job(c, arrived[c]),
    )
    b_own = over_rest(b_own)
    d_y, u_x = exchange(d_mine, *bit_y), exchange(u_mine, *bit_x)
    b_near = exchange(b_own, *bit_w)
    (moving,) = chain.hold(exchange(moving, "seq", 2 * (c & -c)))
    arrived[c & (c - 1)].append(moving)

    (d_near, u_near), (b_pair,), (moving,) = together(
        "phase_6",
        (join_kernel, [d_mine, d_y, u_mine, u_x], [piece, piece]),
        (pair_kernel, [b_own, b_near], [two_b]),
        norm_job(top, arrived[top]),
    )
    d_far, u_far = exchange(d_near, *bit_x), exchange(u_near, *bit_y)
    b_far = exchange(b_pair, *bit_z)
    moving = exchange(moving, "seq", 2 * top)
    d_far, u_far = chain.hold(d_far, u_far)

    (one_mine, two_mine), (nearest,) = together(
        "phase_7", (attend_divide_kernel, [b_pair, b_far], [one_shape, two_shape]), norm_job(1, [])
    )
    one_y, two_x = exchange(one_mine, *bit_y), exchange(two_mine, *bit_x)
    nearest = exchange(chain.hold(nearest)[0], "seq", 2)
    (moving,) = chain.hold(moving)
    ((one_near, two_near),) = together(
        "phase_8",
        (
            attend_join_kernel, [one_mine, one_y, two_mine, two_x],
            [made((8 * n, width), BF16), made((8 * n + 16, width), BF16)],
        ),
    )
    one_far, two_far = exchange(one_near, *bit_x), exchange(two_near, *bit_y)
    d_near_o, u_near_o = chain.hold(*other_core(d_near, u_near))
    grad_down, grad_up = unpack(False, d_near, d_near_o, u_near, u_near_o, [])
    d_far_o, u_far_o = chain.hold(*other_core(d_far, u_far))
    grad_down, grad_up = unpack(True, d_far, d_far_o, u_far, u_far_o, [grad_down, grad_up])
    far_held = chain.hold(one_far, two_far, nearest)
    nearest = far_held[2]
    one_near_o, two_near_o = other_core(*chain.hold(one_near, two_near))
    one_far_o, two_far_o = other_core(*far_held[:2])
    input_grad = call(
        last_kernel, [tokens_v, vectors, mid_grad, *dn_m, dn_r, *arrived[0], moving, nearest], [token_block],
        us=0.1, limit=LIMITS[4], name="input_grad", scalars=0, extra=[chain.token],
    )[0]
    one_all = [one_near, one_far, one_near_o, one_far_o]
    two_all = [two_near, two_far, two_near_o, two_far_o]
    square = made((width, width), F32)
    run = functools.partial(call, unpack_attend_kernel)
    thin = made((1, width), F32)
    results = chain(
        run, [sp] + one_all + two_all, [square] * 4 + [thin] * 3 + [made((1, hidden), F32)] + [thin] * 5,
        scratch=[pltpu.VMEM((PIECES, width), F32)], us=0.1, limit=LIMITS[4], name="unpack_attend",
    )
    grad_query, grad_key, grad_value, grad_out_proj = results[:4]
    lines = [r.reshape(-1) for r in results[4:]]

    return (outputs, input_grad, grad_query, grad_key, grad_value, grad_out_proj, grad_up, grad_down, *lines)


def solution(mesh):
    split, row, copied = P("dp", "seq", None), P("dp"), P()
    return jax.shard_map(
        body,
        mesh=mesh,
        in_specs=(split, split, row, P("dp", None)) + (copied,) * 15,
        out_specs=(split, split) + (copied,) * 15,
        check_vma=False,
    )
```

```python
import functools

import jax
import jax.numpy as jnp
from jax import lax
from jax.experimental import pallas as pl
from jax.experimental.pallas import tpu as pltpu
from jax.sharding import PartitionSpec as P

HEADS = 8
EPSILON = 1e-06
MASKED = -1e30
MIB = 1024 * 1024
LIMITS = (16, 20, 20, 26, 20)
PIECES = 16
GROUP = 4
BACK_US = 0.05
BF16 = jnp.bfloat16
F32 = jnp.float32
GELU_C = 0.7978845608028654
GELU_A = 0.044715


def nn(a, b):
    return jnp.dot(a, b, preferred_element_type=F32)


def nt(a, b):
    return lax.dot_general(a, b, (((1,), (1,)), ((), ())), preferred_element_type=F32)


def tn(a, b):
    return lax.dot_general(a, b, (((0,), (0,)), ((), ())), preferred_element_type=F32)


def normalize(values):
    center = values - jnp.mean(values, axis=-1, keepdims=True)
    scale = lax.rsqrt(jnp.mean(center * center, axis=-1, keepdims=True) + EPSILON)
    return center * scale, scale


def norm_back(cotangent, unit, scale, gain):
    g = cotangent * gain
    return scale * (
        g
        - jnp.mean(g, axis=-1, keepdims=True)
        - unit * jnp.mean(g * unit, axis=-1, keepdims=True)
    )


def segments(pos, offsets, crop, row):
    count = offsets.shape[1]
    seg = jnp.zeros(pos.shape, jnp.int32)
    for j in range(count):
        seg += (pos >= offsets[row, j]).astype(jnp.int32)
    return seg + count * (pos >= crop[row]).astype(jnp.int32)


def positions(sp, chunk, tok, shape, dim):
    start = (sp[4] ^ chunk) * (2 * tok)
    i = lax.broadcasted_iota(jnp.int32, shape, dim)
    return i + jnp.where(i < tok, start + sp[0] * tok, start + sp[1] * tok - tok)


def half_of(which, width):
    return pl.ds(pl.multiple_of(which * width, 128), width)


def padded(lines):
    return jnp.concatenate(lines + [jnp.zeros((16 - len(lines), lines[0].shape[1]), F32)], axis=0)


def load_kernel(halved, sp, *refs):
    count = len(halved)
    sources, targets, sems = refs[:count], refs[count : 2 * count], refs[2 * count :]
    copies = []
    for half, source, target, sem in zip(halved, sources, targets, sems):
        if half:
            source = source.at[:, half_of(sp[0], source.shape[1] // 2)]
        copies.append(pltpu.make_async_copy(source, target, sem))
    for copy in copies:
        copy.start()
    for copy in copies:
        copy.wait()


def chunk_kernel(chunk, last, tok, rows, *refs):
    refs = list(refs)
    first = chunk == 0
    sp, offsets, crop, xm, xo, vectors, weights = refs[:7]
    refs = refs[7:]
    if not first:
        qm_in, m_in, l_in, acc_in = refs[:4]
        refs = refs[4:]
    k_out, v_out, kt_out, nt_out = refs[:4]
    refs = refs[4:]
    if first:
        qm_out = refs.pop(0)
    if last:
        lse_out, ot_out, att_m, att_o = refs[:4]
    else:
        m_out, l_out, acc_out = refs
    half = weights.shape[2]
    heads = HEADS // 2
    size = half // heads
    chip = 2 * tok
    for at, x in ((0, xm), (tok, xo)):
        values = x[...].reshape(rows * tok, -1).astype(F32)
        unit, _ = normalize(values)
        normed = unit * vectors[0:1, :] + vectors[1:2, :]
        low = normed.astype(BF16)
        k = nn(low, weights[1])
        v = (nn(low, weights[2]) + vectors[3:4, half_of(sp[0], half)]).astype(BF16)
        if first:
            q = ((nn(low, weights[0]) + vectors[2:3, half_of(sp[0], half)]).astype(BF16).astype(F32) * size**-0.5).astype(BF16)
            lane = lax.broadcasted_iota(jnp.int32, (tok, 2 * size), 1)
        for r in range(rows):
            part = slice(r * tok, (r + 1) * tok)
            k_out[r, at : at + tok, :] = k[part].astype(BF16)
            v_out[r, at : at + tok, :] = v[part]
            kt_out[r, :, at : at + tok] = k[part].T.astype(BF16)
            nt_out[r, :, at : at + tok] = normed[part].T.astype(BF16)
            if first:
                for h in range(heads):
                    pair = q[part, (h // 2) * 2 * size : (h // 2 + 1) * 2 * size]
                    keep = (lane >= size) if h % 2 else (lane < size)
                    qm_out[r * heads + h, at : at + tok, :] = jnp.where(keep, pair, jnp.zeros_like(pair))
    qm = qm_out if first else qm_in
    for r in range(rows):
        key_seg = segments(positions(sp, chunk, tok, (chip, chip), 0), offsets, crop, r)
        query_seg = segments(positions(sp, 0, tok, (1, chip), 1), offsets, crop, r)
        bias = jnp.where(key_seg == query_seg, 0.0, MASKED)
        outs = []
        spot = [r * heads + h for h in range(heads)]
        pairs = [slice((h // 2) * 2 * size, (h // 2 + 1) * 2 * size) for h in range(heads)]
        s = [nt(k_out[r, :, pairs[h]], qm[spot[h]]) + bias for h in range(heads)]
        tops = [jnp.max(a, axis=0, keepdims=True) for a in s]
        if not first:
            olds = [m_in[at] for at in spot]
            tops = [jnp.maximum(a, b) for a, b in zip(olds, tops)]
        p = [jnp.exp(a - b) for a, b in zip(s, tops)]
        totals = [jnp.sum(a, axis=0, keepdims=True) for a in p]
        addeds = [tn(v_out[r, :, pairs[h]], p[h].astype(BF16)) for h in range(heads)]
        for h, at in enumerate(spot):
            added = addeds[h][(h % 2) * size : (h % 2 + 1) * size]
            total = totals[h]
            if not first:
                keep = jnp.exp(olds[h] - tops[h])
                total += l_in[at] * keep
                added += acc_in[at] * keep
            if last:
                lse_out[at] = tops[h] + jnp.log(total)
                out = added / total
                ot_out[at] = out
                outs.append(out)
            else:
                m_out[at] = tops[h]
                l_out[at] = total
                acc_out[at] = added
        if last:
            att = jnp.concatenate(outs, axis=0).T.astype(BF16)
            att_m[r] = att[:tok]
            att_o[r] = att[tok:]


def feed_forward_half(sp, which, normed, g, up, down, bup, hid, pre, at, vec, total, back):
    half = up.shape[1] // 2
    row = min(512, half)
    block = min(512, row)
    count = half // block
    cols = [pl.ds(pl.multiple_of(sp[which] * half + j * block, 128), block) for j in range(count)]
    for first in range(0, count, 2):
        js = range(first, min(first + 2, count))
        us = [nn(normed, up[:, cols[j]]) + bup[:, cols[j]] for j in js]
        gs = [nt(g, down[cols[j], :]) for j in js]
        outs, pres = [], []
        for j, u, back_in in zip(js, us, gs):
            square = u * u
            plus = 1.0 + jnp.tanh(u * (GELU_C + GELU_C * GELU_A * square))
            low = 0.5 * u
            hidden = (low * plus).astype(BF16)
            slope = plus * (0.5 + low * (2.0 - plus) * (GELU_C + 3 * GELU_C * GELU_A * square))
            grad = (back_in * slope).astype(BF16)
            hid[:, j * block : (j + 1) * block] = hidden
            pre[:, at + j * block : at + (j + 1) * block] = grad
            outs.append(hidden)
            pres.append(grad)
            line = jnp.sum(grad.astype(F32), axis=0, keepdims=True)
            lane = j * block % row
            vec[pl.ds(sp[which] * (half // row) + j * block // row, 1), lane : lane + block] = line
        for j, hidden, grad in zip(js, outs, pres):
            more, less = nn(hidden, down[cols[j], :]), nt(grad, up[:, cols[j]])
            total = more if total is None else total + more
            back = less if back is None else back + less
    return total, back


def ffn_first_kernel(
    sp, att_m, att_o, wo, tokens, cot, up, down, b_out, bup, gain, shift, mid_out, normed_out, send, total_out, back_out, vec
):
    rows, tok, width = tokens.shape
    flat = rows * tok
    quarter = width // 2
    mine = pl.ds(pl.multiple_of(sp[0] * quarter, 128), quarter)
    other = pl.ds(pl.multiple_of(sp[1] * quarter, 128), quarter)
    mid = (
        tokens[...].reshape(flat, width).astype(F32)
        + nn(att_m[...].reshape(flat, -1), wo[mine, :])
        + nn(att_o[...].reshape(flat, -1), wo[other, :])
        + b_out[...]
    )
    mid_out[...] = mid
    unit, _ = normalize(mid)
    normed = (unit * gain[...] + shift[...]).astype(BF16)
    normed_out[...] = normed
    half = up.shape[1] // 2
    send[:, 2 * half :] = normed
    vec[...] = jnp.zeros_like(vec)
    g = cot[...].reshape(flat, width)
    total_out[...], back_out[...] = feed_forward_half(
        sp, 1, normed, g, up, down, bup, send, send, half, vec, None, None
    )


def ffn_second_kernel(
    sp, mid_in, normed_in, cot, up, down, bup, b_down, gain, total_in, back_in, vec_in, out, hid, pre, mid_grad, branch, vec
):
    rows, tok, width = cot.shape
    flat = rows * tok
    g = cot[...].reshape(flat, width)
    vec[...] = vec_in[...]
    total, back = feed_forward_half(
        sp, 0, normed_in[...], g, up, down, bup, hid, pre, 0, vec, total_in[...], back_in[...]
    )
    mid = mid_in[...]
    out[...] = (mid + total + b_down[...]).astype(BF16).reshape(rows, tok, width)
    unit, scale = normalize(mid)
    gf = g.astype(F32)
    grad = gf + norm_back(back, unit, scale, gain[...])
    mid_grad[...] = grad
    low = grad.astype(BF16)
    branch[...] = low.reshape(rows, tok, width)
    vec[4:5, :] = jnp.sum(gf, axis=0, keepdims=True)
    vec[5:6, :] = jnp.sum(back * unit, axis=0, keepdims=True)
    vec[6:7, :] = jnp.sum(back, axis=0, keepdims=True)
    vec[7:8, :] = jnp.sum(low.astype(F32), axis=0, keepdims=True)


def ffn_grad_kernel(send, sp, hid_m, pre_m, n_m, got, g_m, g_o, d, u):
    half = hid_m.shape[1]
    width = g_m.shape[1]
    per = PIECES // 2
    rd, ru = half // PIECES, width // PIECES
    part = (sp[2] // per) ^ send
    cols = half_of(part, half // 2)
    gd = tn(hid_m[:, cols], g_m[...]) + tn(got[:, cols], g_o[...])
    part = (sp[3] // per) ^ send
    own = half_of(part, width // 2)
    others = pl.ds(pl.multiple_of(2 * half + part * (width // 2), 128), width // 2)
    gu = tn(n_m[:, own], pre_m[...]) + tn(got[:, others], got[:, half : 2 * half])
    for p in range(per):
        d[(sp[2] & (per - 1)) ^ p] = gd[p * rd : (p + 1) * rd].astype(BF16)
        at = (sp[3] & (per - 1)) ^ p
        for i in range(half // width):
            u[at, i * ru : (i + 1) * ru, :] = gu[p * ru : (p + 1) * ru, i * width : (i + 1) * width].astype(BF16)


def attend_back_kernel(stations, tok, rows_here, whole, last, *refs):
    refs = list(refs)

    def take(count):
        got = refs[:count]
        del refs[:count]
        return got

    sp, offsets, crop, br_m, br_o, wo, qm, lse, ot, weights = take(10)
    k, v, kt, norm_t = (take(stations) for _ in range(4))
    sums_in = take(5) if rows_here[0] else None
    if last:
        vectors, vec_in = take(2)
        before = take(rows_here[0])
    dn_m = take(len(rows_here))
    dn_o = take(1 if last else len(rows_here))
    if last:
        ones, twos = take(2), take(2)
    gq, gk, gv, go, sums = take(5)
    heads = HEADS // 2
    _, width, half = weights.shape
    size = half // heads
    chip = 2 * tok
    block = min(4, stations)
    blocks = stations // block

    made_here = [0.0] * 5
    for place, row in enumerate(rows_here):
        at = row if whole else 0
        branch = jnp.concatenate([br_m[at], br_o[at]], axis=0)
        do = nt(branch, wo[half_of(sp[0], half), :]).astype(BF16)
        dot = do.astype(F32).T
        lane = lax.broadcasted_iota(jnp.int32, (chip, 2 * size), 1)
        head_at = at * heads
        out_t = jnp.concatenate([ot[head_at + h] for h in range(heads)], axis=0).astype(BF16)
        go_row = nn(out_t, branch)
        query_seg = segments(positions(sp, 0, tok, (1, chip), 1), offsets, crop, row)
        biases = []
        for chunk in range(stations):
            key_seg = segments(positions(sp, chunk, tok, (chip, chip), 0), offsets, crop, row)
            biases.append(jnp.where(key_seg == query_seg, 0.0, MASKED))
        dqt = []
        dks = [[] for _ in range(blocks)]
        dvs = [[] for _ in range(blocks)]
        for pair in range(heads // 2):
            lanes = slice(pair * 2 * size, (pair + 1) * 2 * size)
            dk = [None] * blocks
            dv = [None] * blocks
            for h in (2 * pair, 2 * pair + 1):
                wide = do[:, lanes]
                dm = jnp.where((lane >= size) if h % 2 else (lane < size), wide, jnp.zeros_like(wide))
                delta = jnp.sum(ot[head_at + h] * dot[h * size : (h + 1) * size], axis=0, keepdims=True)
                dq = None
                for b in range(blocks):
                    chunks = range(b * block, (b + 1) * block)
                    keys = jnp.concatenate([k[c][at, :, lanes] for c in chunks], axis=0)
                    values = jnp.concatenate([v[c][at, :, lanes] for c in chunks], axis=0)
                    keys_t = jnp.concatenate([kt[c][at, h * size : (h + 1) * size, :] for c in chunks], axis=1)
                    bias = jnp.concatenate([biases[c] for c in chunks], axis=0)
                    p = jnp.exp(nt(keys, qm[head_at + h]) + bias - lse[head_at + h])
                    ds = (p * (nt(values, dm) - delta)).astype(BF16)
                    dv_h, dk_h = nn(p.astype(BF16), dm), nn(ds, qm[head_at + h])
                    dv[b] = dv_h if dv[b] is None else dv[b] + dv_h
                    dk[b] = dk_h if dk[b] is None else dk[b] + dk_h
                    more = nn(keys_t, ds)
                    dq = more if dq is None else dq + more
                dqt.append(dq)
            for b in range(blocks):
                dks[b].append(dk[b].astype(BF16))
                dvs[b].append(dv[b].astype(BF16))
        dq = (jnp.concatenate(dqt, axis=0) * size**-0.5).T.astype(BF16)
        gq_row = nn(norm_t[0][at], dq)
        gk_row = gv_row = sum_k = sum_v = 0.0
        for b in range(blocks):
            dk = jnp.concatenate(dks[b], axis=1)
            dv = jnp.concatenate(dvs[b], axis=1)
            normed = jnp.concatenate([norm_t[c][at] for c in range(b * block, (b + 1) * block)], axis=1)
            gk_row += nn(normed, dk)
            gv_row += nn(normed, dv)
            sum_k += jnp.sum(dk.astype(F32), axis=0, keepdims=True)
            sum_v += jnp.sum(dv.astype(F32), axis=0, keepdims=True)
            dn = nt(dk, weights[1]) + nt(dv, weights[2])
            for i in range(block):
                part = dn[i * chip : (i + 1) * chip]
                if b + i == 0:
                    part += nt(dq, weights[0])
                dn_m[place][b * block + i] = part[:tok].astype(BF16)
                dn_o[0 if last else place][(row * stations if last else 0) + b * block + i] = part[tok:].astype(BF16)
        sum_q = jnp.sum(dq.astype(F32), axis=0, keepdims=True)
        rest = jnp.zeros((5, half), F32)
        values = (gq_row, gk_row, gv_row, go_row, jnp.concatenate([sum_q, sum_v, sum_k, rest]))
        made_here = [a + b for a, b in zip(made_here, values)]
    for i, (ref, value) in enumerate(zip((gq, gk, gv, go, sums), made_here)):
        ref[...] = value if sums_in is None else value + sums_in[i][...]
    if not last:
        return

    for r, part in enumerate(before):
        dn_o[0][r * stations : (r + 1) * stations] = part[...]
    vec = refs[0]
    lane = lax.broadcasted_iota(jnp.int32, (2, width), 1)
    both = sums[0:2, :]
    both = jnp.concatenate([both, both], axis=1)
    vec[0:2, :] = jnp.where((lane >= half) == (sp[0] == 1), both, 0.0)
    vec[2:3, :] = vec_in[7:8, :]
    vec[3:4, :] = vec_in[4:5, :]
    vec[4:8, :] = vec_in[0:4, :]
    vec[10:12, :] = vec_in[5:7, :]
    vec[12:16, :] = jnp.zeros((4, width), F32)
    wide = [weights[i].astype(F32) for i in range(3)]
    shifts = sum(w * sums[i : i + 1, :] for w, i in zip(wide, (0, 2, 1)))
    gains = sum(w * g[...] for w, g in zip(wide, (gq, gk, gv)))

    def across(values):
        folded = sum(values[:, i * 128 : (i + 1) * 128] for i in range(half // 128))
        return jnp.sum(folded.T, axis=0, keepdims=True)

    shift_grad = across(shifts)
    vec[9:10, :] = shift_grad
    vec[8:9, :] = (across(gains) - vectors[1:2, :] * shift_grad) / vectors[0:1, :]
    n = width // PIECES
    low = n // 2
    per = PIECES // 2
    for slot in range(PIECES):
        one, two = ones[slot // per], twos[slot // per]
        base = slot % per * n
        piece = sp[2] ^ slot
        part = pl.ds(pl.multiple_of(piece * n, n), n)
        one[base : base + n, :half] = gq[part, :].astype(BF16)
        one[base : base + n, half:] = gk[part, :].astype(BF16)
        piece = sp[3] ^ slot
        first = pl.ds(pl.multiple_of(piece * n, n), low)
        second = pl.ds(pl.multiple_of(piece * n + low, low), low)
        two[base : base + low, :half] = gv[first, :].astype(BF16)
        two[base : base + low, half:] = gv[second, :].astype(BF16)
        two[base + low : base + n, :] = go[pl.ds(pl.multiple_of(piece * low, low), low), :].astype(BF16)
    for i, two in enumerate(twos):
        lines = [vec[pl.ds(sp[3] ^ (i * per + s), 1), :] for s in range(per)]
        two[per * n :, :] = padded(lines).astype(BF16)


def last_kernel(tokens, gain, mid_grad, *refs):
    out = refs[-1]
    rows, tok, width = tokens.shape
    flat = rows * tok
    unit, scale = normalize(tokens[...].reshape(flat, width).astype(F32))
    parts = []
    for r in range(rows):
        part = refs[r][0].astype(F32) + refs[rows][r * refs[0].shape[0]].astype(F32)
        for arrived in refs[rows + 1 : -1]:
            part += arrived[r].astype(F32)
        parts.append(part)
    grad = mid_grad[...] + norm_back(jnp.concatenate(parts, axis=0), unit, scale, gain[0:1, :])
    out[...] = grad.astype(BF16).reshape(rows, tok, width)


def unpack_ffn_kernel(far, sp, *refs):
    refs = list(refs)
    d_both, u_both = refs[0:2], refs[2:4]
    down, up, done, d_wide, u_wide, sems = refs[-6:]
    done[...] = jnp.zeros_like(done)
    _, rd, width = d_both[0].shape
    ru = up.shape[0] // PIECES
    half = down.shape[0] // 2
    count = PIECES // GROUP
    copies = []
    for which in range(2):
        for i in range(GROUP // 2):
            at = which * (GROUP // 2) + i
            group = (GROUP // 2 if far else 0) + i
            for k in range(count):
                slot = i * count + k
                place = (sp[2] ^ k) & (count - 1)
                rows = pl.ds(pl.multiple_of(place * rd, rd), rd)
                d_wide[at, rows, :] = d_both[which][slot].astype(F32)
                place = (sp[3] ^ k) & (count - 1)
                rows = pl.ds(pl.multiple_of(place * ru, ru), ru)
                for n in range(rd // ru):
                    part = u_both[which][slot, n * ru : (n + 1) * ru, :]
                    u_wide[at, rows, n * width : (n + 1) * width] = part.astype(F32)
            size = count * rd
            rows = pl.ds(pl.multiple_of(sp[which] * half + ((sp[2] // count) ^ group) * size, size), size)
            copies.append(pltpu.make_async_copy(d_wide.at[at], down.at[rows, :], sems.at[2 * at]))
            copies[-1].start()
            size = count * ru
            rows = pl.ds(pl.multiple_of(((sp[3] // count) ^ group) * size, size), size)
            copies.append(pltpu.make_async_copy(u_wide.at[at], up.at[rows, half_of(sp[which], half)], sems.at[2 * at + 1]))
            copies[-1].start()
    for copy in copies:
        copy.wait()


def unpack_attend_kernel(sp, *refs):
    gq, gk, gv, go, *lines = refs[8:]
    vec = lines.pop()
    ones, twos = (refs[0:2], refs[2:4]), (refs[4:6], refs[6:8])
    width = gq.shape[0]
    half = width // 2
    n = width // PIECES
    low = n // 2
    per = PIECES // 2
    for slot in range(PIECES):
        base = slot % per * n
        for which in range(2):
            one, two = ones[which][slot // per], twos[which][slot // per]
            cols = half_of(sp[which], half)
            piece = sp[2] ^ slot
            rows = pl.ds(pl.multiple_of(piece * n, n), n)
            gq[rows, cols] = one[base : base + n, :half].astype(F32)
            gk[rows, cols] = one[base : base + n, half:].astype(F32)
            piece = sp[3] ^ slot
            first = pl.ds(pl.multiple_of(piece * n, n), low)
            second = pl.ds(pl.multiple_of(piece * n + low, low), low)
            gv[first, cols] = two[base : base + low, :half].astype(F32)
            gv[second, cols] = two[base : base + low, half:].astype(F32)
            out_rows = pl.ds(pl.multiple_of(sp[which] * half + piece * low, low), low)
            go[out_rows, :] = two[base + low : base + n, :].astype(F32)
    for side in range(2):
        both = twos[0][side][per * n :, :].astype(F32) + twos[1][side][per * n :, :].astype(F32)
        for s in range(per):
            vec[pl.ds(sp[3] ^ (side * per + s), 1), :] = both[s : s + 1]
    for line, row in zip(lines, (0, 1, 2, 4, 3, 8, 9, 10, 11)):
        count = line.shape[1] // width
        for i in range(count):
            line[:, i * width : (i + 1) * width] = vec[row + i : row + i + 1, :]


def total(*values):
    return sum(v.astype(F32) for v in values).astype(BF16)


def sum_kernel(*refs):
    refs[-1][...] = total(*[r[...] for r in refs[:-1]])


def upper_kernel(*refs):
    count = len(refs) // 3
    for i, out in enumerate(refs[2 * count :]):
        keep, got = refs[2 * i : 2 * i + 2]
        half = keep.shape[0] // 2
        out[...] = total(keep[half:], got[half:])


def quarter_kernel(d_keep, d_got, d_last, u_keep, u_got, u_last, keep, send):
    rd = d_keep.shape[1]
    half = keep.shape[0]
    for i in range(2 * half):
        out = send if i >= half else keep
        out[i % half, :rd] = total(d_keep[i], d_got[i], d_last[i])
        out[i % half, rd:] = total(u_keep[i], u_got[i], u_last[i])


def halve_kernel(keep, got, out_keep, out_send):
    out_keep[...] = total(keep[0], got[0])
    out_send[...] = total(keep[1], got[1])


def pair_kernel(one, two, out):
    out[0] = one[...]
    out[1] = two[...]


def divide_kernel(one, two, d, u):
    rd = d.shape[1]
    for i in range(d.shape[0]):
        part = (one if i < 2 else two)[i % 2]
        d[i] = part[:rd]
        u[i] = part[rd:]


def join_kernel(*refs):
    count = len(refs) // 3
    for i, out in enumerate(refs[2 * count :]):
        one, two = refs[2 * i : 2 * i + 2]
        out[: one.shape[0]] = one[...]
        out[one.shape[0] :] = two[...]


def attend_upper_kernel(one_keep, one_got, two_keep, two_got, one, two):
    n = one.shape[0]
    one[...] = total(one_keep[n:], one_got[n:])
    two[:n] = total(two_keep[n : 2 * n], two_got[n : 2 * n])
    lines = total(two_keep[2 * n :], two_got[2 * n :]).astype(F32)
    two[n:] = fill(lines[4:8])


def fill(lines):
    return jnp.concatenate([lines, jnp.zeros((16 - lines.shape[0], lines.shape[1]), F32)], axis=0).astype(BF16)


def attend_quarter_kernel(one_keep, one_got, one_last, two_keep, two_got, two_last, keep, send):
    count = 2 * keep.shape[0]
    n = one_last.shape[0] // count
    lines = total(two_keep[2 * count * n :], two_got[2 * count * n :], two_last[count * n :]).astype(F32)
    for i in range(count):
        out = (keep, send)[i // 2]
        part = slice(i * n, (i + 1) * n)
        out[i % 2, :n] = total(one_keep[part], one_got[part], one_last[part])
        out[i % 2, n : 2 * n] = total(two_keep[part], two_got[part], two_last[part])
        out[i % 2, 2 * n :] = jnp.broadcast_to(lines[i : i + 1], (16, lines.shape[1])).astype(BF16)


def attend_divide_kernel(first, second, one, two):
    n = one.shape[0] // 4
    lines = []
    for i in range(4):
        part = (first if i < 2 else second)[i % 2]
        one[i * n : (i + 1) * n] = part[:n]
        two[i * n : (i + 1) * n] = part[n : 2 * n]
        lines.append(part[2 * n :].astype(F32)[:1])
    two[4 * n :] = padded(lines).astype(BF16)


def attend_join_kernel(one_a, one_b, two_a, two_b, one, two):
    n = one_a.shape[0]
    one[:n] = one_a[...]
    one[n:] = one_b[...]
    two[:n] = two_a[:n]
    two[n : 2 * n] = two_b[:n]
    lines = jnp.concatenate([two_a[n:].astype(F32)[:4], two_b[n:].astype(F32)[:4]], axis=0)
    two[2 * n :] = fill(lines)


def norm_grad_kernel(chunk, rows, *refs):
    out = refs[-1]
    stations = refs[0].shape[0]
    for r in range(rows):
        out[r] = total(refs[r][chunk], refs[rows][r * stations + chunk], *[a[r] for a in refs[rows + 1 : -1]])


VMEM = pl.BlockSpec(memory_space=pltpu.VMEM)
SMEM = pl.BlockSpec(memory_space=pltpu.SMEM)
HBM = pl.BlockSpec(memory_space=pltpu.HBM)
ANY = pl.BlockSpec(memory_space=pl.ANY)


def call(kernel, ins, outs, scratch=(), us=1.0, limit=16, name=None, scalars=1, specs=None, grid=(), out_specs=None, aliases=None, extra=()):
    count = len(ins)

    def body_of(*refs):
        kernel(*refs[:count], *refs[count + len(extra) :])

    return pl.pallas_call(
        body_of,
        grid=grid,
        in_specs=[SMEM] * scalars + (specs or [VMEM] * (count - scalars)) + [ANY] * len(extra),
        out_specs=out_specs or [VMEM] * len(outs),
        input_output_aliases=aliases or {},
        out_shape=list(outs),
        scratch_shapes=list(scratch),
        compiler_params=pltpu.CompilerParams(vmem_limit_bytes=limit * MIB),
        cost_estimate=pl.CostEstimate(flops=int(us * 1.1e9), bytes_accessed=0, transcendentals=0),
        name=name,
    )(*ins, *extra)


def load(sp, arrays, halved, name, limit=16):
    shapes = [a.shape[:-1] + (a.shape[-1] // (2 if h else 1),) for a, h in zip(arrays, halved)]
    return call(
        functools.partial(load_kernel, halved), [sp] + arrays, [made(s, a.dtype) for s, a in zip(shapes, arrays)],
        scratch=[pltpu.SemaphoreType.DMA] * len(arrays), us=2.0, limit=limit, name=name, specs=[HBM] * len(arrays),
    )


def made(shape, dtype):
    return jax.ShapeDtypeStruct(shape, dtype)


def exchange(array, axis, mask):
    count = lax.axis_size(axis)
    return lax.ppermute(array, axis, [(i, i ^ mask) for i in range(count)])


def merge(kernel, ins, outs, name, extra=()):
    specs = [SMEM if a.dtype == jnp.int32 else VMEM for a in ins]
    return call(kernel, list(ins), list(outs), us=0.05, limit=8, name=name, scalars=0, specs=specs, extra=extra)


def tied(*arrays):
    return lax.optimization_barrier(arrays)


class Chain:
    def __init__(self, token):
        self.token = token

    def __call__(self, function, *args, **kwargs):
        outs = list(function(*args, extra=[self.token], **kwargs))
        self.token = outs[-1]
        return outs

    def hold(self, *arrays):
        *arrays, self.token = tied(*arrays, self.token)
        return arrays


def my_id(bits):
    out = 0
    for axis, mask in bits:
        out = out * 2 + jnp.where((lax.axis_index(axis) & mask) != 0, 1, 0)
    return out


def body(
    tokens, grad_out, crop, offsets, w_query, w_key, w_value, w_out, w_up, w_down, b_query, b_value,
    b_out, b_up, b_down, gain_one, shift_one, gain_two, shift_two,
):
    rows, tok, width = tokens.shape
    seq_count, dp_count = lax.axis_size("seq"), lax.axis_size("dp")
    stations = seq_count // 2
    hidden = w_up.shape[1]
    half = width // 2
    heads = HEADS // 2
    size = half // heads
    chip = 2 * tok
    flat = rows * tok
    small = stations <= 4
    seq = lax.axis_index("seq")
    core, station = seq % 2, seq // 2
    line = lambda v: v.reshape(1, -1)

    dp_bits = [("dp", 1 << i) for i in range(dp_count.bit_length() - 1)]
    st_bits = [("seq", 2 << i) for i in range(stations.bit_length() - 1)]
    bit_x, bit_y = dp_bits[:2]
    rest = dp_bits[2:] + st_bits[2:]
    ids = [my_id([bit_x, bit_y] + st_bits[:2]), my_id([bit_y, bit_x] + st_bits[:2])]
    sp = jnp.stack([core, 1 - core, *ids, station]).astype(jnp.int32)

    mine = lambda a: lax.dynamic_slice_in_dim(a, core * half, half, a.ndim - 1)
    weights = jnp.stack([mine(w_query), mine(w_key), mine(w_value)])
    vectors = jnp.stack([gain_one, shift_one, b_query, b_value] + [jnp.zeros_like(gain_one)] * 4)
    state = []
    kept = [[None] * stations for _ in range(4)]
    blocks = {0: tokens}
    turns = [int(f"{i:0{stations.bit_length() - 1}b}"[::-1], 2) for i in range(stations)]
    for at, j in enumerate(turns):
        if j:
            low = j & -j
            block = blocks[j] = exchange(blocks[j ^ low], "seq", 2 * low)
            if at == 1 or at == stations - 1:
                block, state[-1] = tied(block, state[-1])
                blocks[j] = block
        else:
            block = tokens
        other = exchange(block, "seq", 1)
        first, last = at == 0, at == stations - 1
        ins = [sp, offsets, crop, block, other, vectors, weights] + ([] if first else state)
        outs = [
            made((rows, chip, half), BF16),
            made((rows, chip, half), BF16),
            made((rows, half, chip), BF16),
            made((rows, width, chip), BF16),
        ]
        if first:
            outs += [made((rows * heads, chip, 2 * size), BF16)]
        stat = made((rows * heads, 1, chip), F32)
        acc = made((rows * heads, size, chip), F32)
        if last:
            outs += [stat, acc, made((rows, tok, half), BF16), made((rows, tok, half), BF16)]
        else:
            outs += [stat, stat, acc]
        got = call(
            functools.partial(chunk_kernel, j, last, tok, rows), ins, outs,
            us=0.05, limit=LIMITS[0], name=f"attend_chunk_{j}", scalars=3,
        )
        for where, array in zip(kept, got[:4]):
            where[j] = array
        got = got[4:]
        if first:
            query, got = got[0], got[1:]
        if not last:
            state = [query] + list(got)
        if at == 0:
            sp_b, state[-1] = tied(sp, state[-1])
            tokens_v, g_v, wo, up, down, bo, bu, bd, gain_b, shift_b = load(
                sp_b,
                [tokens, grad_out, w_out, w_up, w_down, line(b_out), line(b_up), line(b_down), line(gain_two), line(shift_two)],
                [False] * 10, "load_feed_forward",
            )
            g_other = exchange(g_v, "seq", 1)
            state[-1], up = tied(state[-1], up)
        if at == 1:
            state[-1], g_other = tied(state[-1], g_other)
            g_other = g_other.reshape(flat, width)
    lse, out_t, att_m, att_o = got
    att_r = exchange(att_o, "seq", 1)

    wide = made((flat, width), F32)
    vec8 = made((8, width), F32)
    mid, normed_two, send, total, back, vec_a = call(
        ffn_first_kernel, [sp, att_m, att_r, wo, tokens_v, g_v, up, down, bo, bu, gain_b, shift_b],
        [wide, made((flat, width), BF16), made((flat, hidden + width), BF16), wide, wide, vec8],
        us=4.0, limit=LIMITS[1], name="feed_forward_a",
    )
    got = exchange(send, "seq", 1)
    outputs, hid_m, pre_m, mid_grad, branch, vec_ffn = call(
        ffn_second_kernel, [sp, mid, normed_two, g_v, up, down, bu, bd, gain_b, total, back, vec_a],
        [made((rows, tok, width), BF16), made((flat, hidden // 2), BF16), made((flat, hidden // 2), BF16), wide,
         made((rows, tok, width), BF16), vec8],
        us=4.0, limit=LIMITS[1], name="feed_forward_b",
    )
    branch_r = exchange(branch, "seq", 1)
    piece = made((PIECES // 2, hidden // 2 // PIECES, width), BF16)
    ins = [sp, hid_m, pre_m, normed_two, got, g_v.reshape(flat, width), g_other]
    d_send, u_send = call(
        functools.partial(ffn_grad_kernel, 1), ins, [piece, piece], us=3.0, limit=LIMITS[2], name="feed_forward_grad_sent"
    )
    d_send, u_send, branch_r = tied(d_send, u_send, branch_r)
    chain = Chain(d_send)
    d_keep, u_keep = chain(
        functools.partial(call, functools.partial(ffn_grad_kernel, 0)), ins, [piece, piece], us=0.05, limit=LIMITS[2],
        name="feed_forward_grad_kept",
    )

    q = PIECES // GROUP
    d_got, u_got = exchange(d_send, *bit_x), exchange(u_send, *bit_y)

    sums = []
    dn_m, dn_o, dn_r = [], [], []

    def together(name, *jobs):
        ins = [a for _, arrays, _ in jobs for a in arrays]
        outs = [s for _, _, shapes in jobs for s in shapes]

        def kernel(*refs):
            at, to = 0, len(ins)
            for one, arrays, shapes in jobs:
                one(*refs[at : at + len(arrays)], *refs[to : to + len(shapes)])
                at, to = at + len(arrays), to + len(shapes)

        res = iter(chain(functools.partial(merge, kernel), ins, outs, name))
        return [[next(res) for _ in shapes] for _, _, shapes in jobs]

    def norm_job(chunk, arrived):
        ins = [*dn_m, dn_r, *arrived]
        return (functools.partial(norm_grad_kernel, chunk, rows), ins, [made((rows, tok, width), BF16)])

    groups = [tuple(range(rows - 1)), (rows - 1,)] if small else [(r,) for r in range(rows)]
    for group in groups:
        r, last = group[-1], group[-1] == rows - 1
        arrays = [branch, branch_r, wo, query, lse, out_t, weights] + [a for part in kept for a in part]
        specs = [VMEM] * len(arrays)
        if not small:
            for i, a in enumerate(arrays):
                if a.ndim == 3 and a is not weights:
                    block_shape = (a.shape[0] // rows,) + a.shape[1:]
                    specs[i] = pl.BlockSpec(block_shape, functools.partial(lambda r, i: (r, 0, 0), r))
        tail = list(sums)
        if last:
            tail += [vectors, vec_ffn, *dn_o]
        part = made((stations, tok, width), BF16)
        grads = [made((width, half), F32)] * 3 + [made((half, width), F32), made((8, half), F32)]
        outs = [part] * (2 * len(group)) + grads
        scratch = []
        if last:
            outs = [part, made((rows * stations, tok, width), BF16)] + [made((width // 2, width), BF16)] * 2 + [made((width // 2 + 16, width), BF16)] * 2
            scratch = [pltpu.VMEM(g.shape, F32) for g in grads] + [pltpu.VMEM((16, width), F32)]
        run = functools.partial(call, functools.partial(attend_back_kernel, stations, tok, group, small, last))
        res = chain(
            run, [sp, offsets, crop] + arrays + tail, outs, scratch=scratch,
            us=BACK_US, limit=LIMITS[3] if small else 48, name=f"attend_back_{r}", scalars=3,
            specs=specs + [VMEM] * len(tail), grid=() if small else (1,),
        )
        if last:
            dn_m.append(res[0])
            dn_o.append(res[1])
        else:
            dn_m += res[: len(group)]
            dn_o += res[len(group) : 2 * len(group)]
            sums = list(res[2 * len(group) :])
        if r == rows - 2:
            quarters = made((q,) + piece.shape[1:], BF16)
            ((d_next, u_next),) = together(
                "add_quarters", (upper_kernel, [d_keep, d_got, u_keep, u_got], [quarters, quarters])
            )
            d_got2, u_got2 = exchange(d_next, *bit_y), exchange(u_next, *bit_x)
    one_keep, one_send, two_keep, two_send = res[2:]

    rd = hidden // 2 // PIECES
    n = width // PIECES
    ff_part, at_part = made((2 * rd, width), BF16), made((2 * n + 16, width), BF16)
    two_of = lambda a: made((2,) + a.shape, BF16)
    token_block = made((rows, tok, width), BF16)
    bit_z, bit_w = st_bits[:2]

    def over_rest(part):
        for i, (where, mask) in enumerate(rest):
            got = exchange(part, where, mask)
            ((part,),) = together(f"add_rest_{i}", (sum_kernel, [part, got], [made(part.shape, BF16)]))
        return part

    def unpack(far, d, d_other, u, u_other, before):
        ins = [sp, d, d_other, u, u_other] + before
        scratch = [
            pltpu.VMEM((GROUP, q * rd, width), F32), pltpu.VMEM((GROUP, q * width // PIECES, hidden // 2), F32),
            pltpu.SemaphoreType.DMA((2 * GROUP,)),
        ]
        return chain(
            functools.partial(call, functools.partial(unpack_ffn_kernel, far)), ins,
            [made((hidden, width), F32), made((width, hidden), F32), made((8, 128), F32)], scratch=scratch, us=0.1,
            limit=LIMITS[4], name="unpack_feed_forward", specs=[VMEM] * 4 + [HBM] * len(before),
            out_specs=[HBM] * 2 + [VMEM], aliases={5: 0, 6: 1} if before else None,
        )[:2]

    def other_core(*arrays):
        return [exchange(a, "seq", 1) for a in arrays]

    two_a, two_b = two_of(ff_part), two_of(at_part)
    ((a_keep, a_send),) = together(
        "phase_1", (quarter_kernel, [d_keep, d_got, d_got2, u_keep, u_got, u_got2], [two_a, two_a])
    )
    one_send, two_send, dn_o = chain.hold(one_send, two_send, dn_o[-1])
    a_got = exchange(a_send, *bit_z)
    one_got, two_got = exchange(one_send, *bit_x), exchange(two_send, *bit_y)
    (dn_r,) = chain.hold(*other_core(dn_o))

    one_shape, two_shape = made((4 * n, width), BF16), made((4 * n + 16, width), BF16)
    (a_keep, a_send), (one_next, two_next) = together(
        "phase_2",
        (halve_kernel, [a_keep, a_got], [ff_part] * 2),
        (attend_upper_kernel, [one_keep, one_got, two_keep, two_got], [one_shape, two_shape]),
    )
    a_got = exchange(a_send, *bit_w)
    one_got2, two_got2 = exchange(one_next, *bit_y), exchange(two_next, *bit_x)

    (a_own,), (b_keep, b_send) = together(
        "phase_3",
        (sum_kernel, [a_keep, a_got], [ff_part]),
        (attend_quarter_kernel, [one_keep, one_got, one_got2, two_keep, two_got, two_got2], [two_b, two_b]),
    )
    a_own = over_rest(a_own)
    a_near = exchange(a_own, *bit_w)
    b_got = exchange(b_send, *bit_z)

    (a_pair,), (b_keep, b_send) = together(
        "phase_4",
        (pair_kernel, [a_own, a_near], [two_a]),
        (halve_kernel, [b_keep, b_got], [at_part] * 2),
    )
    a_far = exchange(a_pair, *bit_z)
    b_got = exchange(b_send, *bit_w)

    arrived = {c: [] for c in range(stations)}
    top = stations // 2
    inner = [c for c in reversed(turns) if c not in (0, 1, top)]
    for c in inner[:-1]:
        ((moving,),) = together("norm_step", norm_job(c, arrived[c]))
        arrived[c & (c - 1)].append(exchange(moving, "seq", 2 * (c & -c)))
    c = inner[-1]
    (d_mine, u_mine), (b_own,), (moving,) = together(
        "phase_5",
        (divide_kernel, [a_pair, a_far], [quarters, quarters]),
        (sum_kernel, [b_keep, b_got], [at_part]),
        norm_job(c, arrived[c]),
    )
    b_own = over_rest(b_own)
    d_y, u_x = exchange(d_mine, *bit_y), exchange(u_mine, *bit_x)
    b_near = exchange(b_own, *bit_w)
    (moving,) = chain.hold(exchange(moving, "seq", 2 * (c & -c)))
    arrived[c & (c - 1)].append(moving)

    (d_near, u_near), (b_pair,), (moving,) = together(
        "phase_6",
        (join_kernel, [d_mine, d_y, u_mine, u_x], [piece, piece]),
        (pair_kernel, [b_own, b_near], [two_b]),
        norm_job(top, arrived[top]),
    )
    d_far, u_far = exchange(d_near, *bit_x), exchange(u_near, *bit_y)
    b_far = exchange(b_pair, *bit_z)
    moving = exchange(moving, "seq", 2 * top)
    d_far, u_far = chain.hold(d_far, u_far)

    (one_mine, two_mine), (nearest,) = together(
        "phase_7", (attend_divide_kernel, [b_pair, b_far], [one_shape, two_shape]), norm_job(1, [])
    )
    one_y, two_x = exchange(one_mine, *bit_y), exchange(two_mine, *bit_x)
    nearest = exchange(chain.hold(nearest)[0], "seq", 2)
    (moving,) = chain.hold(moving)
    ((one_near, two_near),) = together(
        "phase_8",
        (
            attend_join_kernel, [one_mine, one_y, two_mine, two_x],
            [made((8 * n, width), BF16), made((8 * n + 16, width), BF16)],
        ),
    )
    one_far, two_far = exchange(one_near, *bit_x), exchange(two_near, *bit_y)
    d_near_o, u_near_o = chain.hold(*other_core(d_near, u_near))
    grad_down, grad_up = unpack(False, d_near, d_near_o, u_near, u_near_o, [])
    d_far_o, u_far_o = chain.hold(*other_core(d_far, u_far))
    grad_down, grad_up = unpack(True, d_far, d_far_o, u_far, u_far_o, [grad_down, grad_up])
    far_held = chain.hold(one_far, two_far, nearest)
    nearest = far_held[2]
    one_near_o, two_near_o = other_core(one_near, two_near)
    one_far_o, two_far_o = other_core(*far_held[:2])
    input_grad = call(
        last_kernel, [tokens_v, vectors, mid_grad, *dn_m, dn_r, *arrived[0], moving, nearest], [token_block],
        us=0.1, limit=LIMITS[4], name="input_grad", scalars=0, extra=[chain.token],
    )[0]
    one_all = [one_near, one_far, one_near_o, one_far_o]
    two_all = [two_near, two_far, two_near_o, two_far_o]
    square = made((width, width), F32)
    run = functools.partial(call, unpack_attend_kernel)
    thin = made((1, width), F32)
    results = chain(
        run, [sp] + one_all + two_all, [square] * 4 + [thin] * 3 + [made((1, hidden), F32)] + [thin] * 5,
        scratch=[pltpu.VMEM((PIECES, width), F32)], us=0.1, limit=LIMITS[4], name="unpack_attend",
    )
    grad_query, grad_key, grad_value, grad_out_proj = results[:4]
    lines = [r.reshape(-1) for r in results[4:]]

    return (outputs, input_grad, grad_query, grad_key, grad_value, grad_out_proj, grad_up, grad_down, *lines)


def solution(mesh):
    split, row, copied = P("dp", "seq", None), P("dp"), P()
    return jax.shard_map(
        body,
        mesh=mesh,
        in_specs=(split, split, row, P("dp", None)) + (copied,) * 15,
        out_specs=(split, split) + (copied,) * 15,
        check_vma=False,
    )
```

```python
import functools

import jax
import jax.numpy as jnp
from jax import lax
from jax.experimental import pallas as pl
from jax.experimental.pallas import tpu as pltpu
from jax.sharding import PartitionSpec as P

HEADS = 8
EPSILON = 1e-06
MASKED = -1e30
MIB = 1024 * 1024
LIMITS = (16, 20, 20, 26, 20)
PIECES = 16
GROUP = 4
BACK_US = 0.05
BF16 = jnp.bfloat16
F32 = jnp.float32
GELU_C = 0.7978845608028654
GELU_A = 0.044715


def nn(a, b):
    return jnp.dot(a, b, preferred_element_type=F32)


def nt(a, b):
    return lax.dot_general(a, b, (((1,), (1,)), ((), ())), preferred_element_type=F32)


def tn(a, b):
    return lax.dot_general(a, b, (((0,), (0,)), ((), ())), preferred_element_type=F32)


def normalize(values):
    center = values - jnp.mean(values, axis=-1, keepdims=True)
    scale = lax.rsqrt(jnp.mean(center * center, axis=-1, keepdims=True) + EPSILON)
    return center * scale, scale


def norm_back(cotangent, unit, scale, gain):
    g = cotangent * gain
    return scale * (
        g
        - jnp.mean(g, axis=-1, keepdims=True)
        - unit * jnp.mean(g * unit, axis=-1, keepdims=True)
    )


def segments(pos, offsets, crop, row):
    count = offsets.shape[1]
    seg = jnp.zeros(pos.shape, jnp.int32)
    for j in range(count):
        seg += (pos >= offsets[row, j]).astype(jnp.int32)
    return seg + count * (pos >= crop[row]).astype(jnp.int32)


def positions(sp, chunk, tok, shape, dim):
    start = (sp[4] ^ chunk) * (2 * tok)
    i = lax.broadcasted_iota(jnp.int32, shape, dim)
    return i + jnp.where(i < tok, start + sp[0] * tok, start + sp[1] * tok - tok)


def half_of(which, width):
    return pl.ds(pl.multiple_of(which * width, 128), width)


def padded(lines):
    return jnp.concatenate(lines + [jnp.zeros((16 - len(lines), lines[0].shape[1]), F32)], axis=0)


def load_kernel(halved, sp, *refs):
    count = len(halved)
    sources, targets, sems = refs[:count], refs[count : 2 * count], refs[2 * count :]
    copies = []
    for half, source, target, sem in zip(halved, sources, targets, sems):
        if half:
            source = source.at[:, half_of(sp[0], source.shape[1] // 2)]
        copies.append(pltpu.make_async_copy(source, target, sem))
    for copy in copies:
        copy.start()
    for copy in copies:
        copy.wait()


def chunk_kernel(chunk, last, tok, rows, *refs):
    refs = list(refs)
    first = chunk == 0
    sp, offsets, crop, xm, xo, vectors, weights = refs[:7]
    refs = refs[7:]
    if not first:
        qm_in, m_in, l_in, acc_in = refs[:4]
        refs = refs[4:]
    k_out, v_out, kt_out, nt_out = refs[:4]
    refs = refs[4:]
    if first:
        qm_out = refs.pop(0)
    if last:
        lse_out, ot_out, att_m, att_o = refs[:4]
    else:
        m_out, l_out, acc_out = refs
    half = weights.shape[2]
    heads = HEADS // 2
    size = half // heads
    chip = 2 * tok
    for at, x in ((0, xm), (tok, xo)):
        values = x[...].reshape(rows * tok, -1).astype(F32)
        unit, _ = normalize(values)
        normed = unit * vectors[0:1, :] + vectors[1:2, :]
        low = normed.astype(BF16)
        k = nn(low, weights[1])
        v = (nn(low, weights[2]) + vectors[3:4, half_of(sp[0], half)]).astype(BF16)
        if first:
            q = ((nn(low, weights[0]) + vectors[2:3, half_of(sp[0], half)]).astype(BF16).astype(F32) * size**-0.5).astype(BF16)
            lane = lax.broadcasted_iota(jnp.int32, (tok, 2 * size), 1)
        for r in range(rows):
            part = slice(r * tok, (r + 1) * tok)
            k_out[r, at : at + tok, :] = k[part].astype(BF16)
            v_out[r, at : at + tok, :] = v[part]
            kt_out[r, :, at : at + tok] = k[part].T.astype(BF16)
            nt_out[r, :, at : at + tok] = normed[part].T.astype(BF16)
            if first:
                for h in range(heads):
                    pair = q[part, (h // 2) * 2 * size : (h // 2 + 1) * 2 * size]
                    keep = (lane >= size) if h % 2 else (lane < size)
                    qm_out[r * heads + h, at : at + tok, :] = jnp.where(keep, pair, jnp.zeros_like(pair))
    qm = qm_out if first else qm_in
    for r in range(rows):
        key_seg = segments(positions(sp, chunk, tok, (chip, chip), 0), offsets, crop, r)
        query_seg = segments(positions(sp, 0, tok, (1, chip), 1), offsets, crop, r)
        bias = jnp.where(key_seg == query_seg, 0.0, MASKED)
        outs = []
        spot = [r * heads + h for h in range(heads)]
        pairs = [slice((h // 2) * 2 * size, (h // 2 + 1) * 2 * size) for h in range(heads)]
        s = [nt(k_out[r, :, pairs[h]], qm[spot[h]]) + bias for h in range(heads)]
        tops = [jnp.max(a, axis=0, keepdims=True) for a in s]
        if not first:
            olds = [m_in[at] for at in spot]
            tops = [jnp.maximum(a, b) for a, b in zip(olds, tops)]
        p = [jnp.exp(a - b) for a, b in zip(s, tops)]
        totals = [jnp.sum(a, axis=0, keepdims=True) for a in p]
        addeds = [tn(v_out[r, :, pairs[h]], p[h].astype(BF16)) for h in range(heads)]
        for h, at in enumerate(spot):
            added = addeds[h][(h % 2) * size : (h % 2 + 1) * size]
            total = totals[h]
            if not first:
                keep = jnp.exp(olds[h] - tops[h])
                total += l_in[at] * keep
                added += acc_in[at] * keep
            if last:
                lse_out[at] = tops[h] + jnp.log(total)
                out = added / total
                ot_out[at] = out
                outs.append(out)
            else:
                m_out[at] = tops[h]
                l_out[at] = total
                acc_out[at] = added
        if last:
            att = jnp.concatenate(outs, axis=0).T.astype(BF16)
            att_m[r] = att[:tok]
            att_o[r] = att[tok:]


def feed_forward_half(sp, which, normed, g, up, down, bup, hid, pre, at, vec, total, back):
    half = up.shape[1] // 2
    row = min(512, half)
    block = min(512, row)
    count = half // block
    cols = [pl.ds(pl.multiple_of(sp[which] * half + j * block, 128), block) for j in range(count)]
    for first in range(0, count, 2):
        js = range(first, min(first + 2, count))
        us = [nn(normed, up[:, cols[j]]) + bup[:, cols[j]] for j in js]
        gs = [nt(g, down[cols[j], :]) for j in js]
        outs, pres = [], []
        for j, u, back_in in zip(js, us, gs):
            square = u * u
            plus = 1.0 + jnp.tanh(u * (GELU_C + GELU_C * GELU_A * square))
            low = 0.5 * u
            hidden = (low * plus).astype(BF16)
            slope = plus * (0.5 + low * (2.0 - plus) * (GELU_C + 3 * GELU_C * GELU_A * square))
            grad = (back_in * slope).astype(BF16)
            hid[:, j * block : (j + 1) * block] = hidden
            pre[:, at + j * block : at + (j + 1) * block] = grad
            outs.append(hidden)
            pres.append(grad)
            line = jnp.sum(grad.astype(F32), axis=0, keepdims=True)
            lane = j * block % row
            vec[pl.ds(sp[which] * (half // row) + j * block // row, 1), lane : lane + block] = line
        for j, hidden, grad in zip(js, outs, pres):
            more, less = nn(hidden, down[cols[j], :]), nt(grad, up[:, cols[j]])
            total = more if total is None else total + more
            back = less if back is None else back + less
    return total, back


def ffn_first_kernel(
    sp, att_m, att_o, wo, tokens, cot, up, down, b_out, bup, gain, shift, mid_out, normed_out, send, total_out, back_out, vec
):
    rows, tok, width = tokens.shape
    flat = rows * tok
    quarter = width // 2
    mine = pl.ds(pl.multiple_of(sp[0] * quarter, 128), quarter)
    other = pl.ds(pl.multiple_of(sp[1] * quarter, 128), quarter)
    mid = (
        tokens[...].reshape(flat, width).astype(F32)
        + nn(att_m[...].reshape(flat, -1), wo[mine, :])
        + nn(att_o[...].reshape(flat, -1), wo[other, :])
        + b_out[...]
    )
    mid_out[...] = mid
    unit, _ = normalize(mid)
    normed = (unit * gain[...] + shift[...]).astype(BF16)
    normed_out[...] = normed
    half = up.shape[1] // 2
    send[:, 2 * half :] = normed
    vec[...] = jnp.zeros_like(vec)
    g = cot[...].reshape(flat, width)
    total_out[...], back_out[...] = feed_forward_half(
        sp, 1, normed, g, up, down, bup, send, send, half, vec, None, None
    )


def ffn_second_kernel(
    sp, mid_in, normed_in, cot, up, down, bup, b_down, gain, total_in, back_in, vec_in, out, hid, pre, mid_grad, branch, vec
):
    rows, tok, width = cot.shape
    flat = rows * tok
    g = cot[...].reshape(flat, width)
    vec[...] = vec_in[...]
    total, back = feed_forward_half(
        sp, 0, normed_in[...], g, up, down, bup, hid, pre, 0, vec, total_in[...], back_in[...]
    )
    mid = mid_in[...]
    out[...] = (mid + total + b_down[...]).astype(BF16).reshape(rows, tok, width)
    unit, scale = normalize(mid)
    gf = g.astype(F32)
    grad = gf + norm_back(back, unit, scale, gain[...])
    mid_grad[...] = grad
    low = grad.astype(BF16)
    branch[...] = low.reshape(rows, tok, width)
    vec[4:5, :] = jnp.sum(gf, axis=0, keepdims=True)
    vec[5:6, :] = jnp.sum(back * unit, axis=0, keepdims=True)
    vec[6:7, :] = jnp.sum(back, axis=0, keepdims=True)
    vec[7:8, :] = jnp.sum(low.astype(F32), axis=0, keepdims=True)


def ffn_grad_kernel(send, sp, hid_m, pre_m, n_m, got, g_m, g_o, d, u):
    half = hid_m.shape[1]
    width = g_m.shape[1]
    per = PIECES // 2
    rd, ru = half // PIECES, width // PIECES
    part = (sp[2] // per) ^ send
    cols = half_of(part, half // 2)
    gd = tn(hid_m[:, cols], g_m[...]) + tn(got[:, cols], g_o[...])
    part = (sp[3] // per) ^ send
    own = half_of(part, width // 2)
    others = pl.ds(pl.multiple_of(2 * half + part * (width // 2), 128), width // 2)
    gu = tn(n_m[:, own], pre_m[...]) + tn(got[:, others], got[:, half : 2 * half])
    for p in range(per):
        d[(sp[2] & (per - 1)) ^ p] = gd[p * rd : (p + 1) * rd].astype(BF16)
        at = (sp[3] & (per - 1)) ^ p
        for i in range(half // width):
            u[at, i * ru : (i + 1) * ru, :] = gu[p * ru : (p + 1) * ru, i * width : (i + 1) * width].astype(BF16)


def attend_back_kernel(stations, tok, rows_here, whole, last, *refs):
    refs = list(refs)

    def take(count):
        got = refs[:count]
        del refs[:count]
        return got

    sp, offsets, crop, br_m, br_o, wo, qm, lse, ot, weights = take(10)
    k, v, kt, norm_t = (take(stations) for _ in range(4))
    sums_in = take(5) if rows_here[0] else None
    if last:
        vectors, vec_in = take(2)
        before = take(rows_here[0])
    dn_m = take(len(rows_here))
    dn_o = take(1 if last else len(rows_here))
    if last:
        ones, twos = take(2), take(2)
    gq, gk, gv, go, sums = take(5)
    heads = HEADS // 2
    _, width, half = weights.shape
    size = half // heads
    chip = 2 * tok
    block = min(4, stations)
    blocks = stations // block

    made_here = [0.0] * 5
    for place, row in enumerate(rows_here):
        at = row if whole else 0
        branch = jnp.concatenate([br_m[at], br_o[at]], axis=0)
        do = nt(branch, wo[half_of(sp[0], half), :]).astype(BF16)
        dot = do.astype(F32).T
        lane = lax.broadcasted_iota(jnp.int32, (chip, 2 * size), 1)
        head_at = at * heads
        out_t = jnp.concatenate([ot[head_at + h] for h in range(heads)], axis=0).astype(BF16)
        go_row = nn(out_t, branch)
        query_seg = segments(positions(sp, 0, tok, (1, chip), 1), offsets, crop, row)
        biases = []
        for chunk in range(stations):
            key_seg = segments(positions(sp, chunk, tok, (chip, chip), 0), offsets, crop, row)
            biases.append(jnp.where(key_seg == query_seg, 0.0, MASKED))
        dqt = []
        dks = [[] for _ in range(blocks)]
        dvs = [[] for _ in range(blocks)]
        for pair in range(heads // 2):
            lanes = slice(pair * 2 * size, (pair + 1) * 2 * size)
            dk = [None] * blocks
            dv = [None] * blocks
            for h in (2 * pair, 2 * pair + 1):
                wide = do[:, lanes]
                dm = jnp.where((lane >= size) if h % 2 else (lane < size), wide, jnp.zeros_like(wide))
                delta = jnp.sum(ot[head_at + h] * dot[h * size : (h + 1) * size], axis=0, keepdims=True)
                dq = None
                for b in range(blocks):
                    chunks = range(b * block, (b + 1) * block)
                    keys = jnp.concatenate([k[c][at, :, lanes] for c in chunks], axis=0)
                    values = jnp.concatenate([v[c][at, :, lanes] for c in chunks], axis=0)
                    keys_t = jnp.concatenate([kt[c][at, h * size : (h + 1) * size, :] for c in chunks], axis=1)
                    bias = jnp.concatenate([biases[c] for c in chunks], axis=0)
                    p = jnp.exp(nt(keys, qm[head_at + h]) + bias - lse[head_at + h])
                    ds = (p * (nt(values, dm) - delta)).astype(BF16)
                    dv_h, dk_h = nn(p.astype(BF16), dm), nn(ds, qm[head_at + h])
                    dv[b] = dv_h if dv[b] is None else dv[b] + dv_h
                    dk[b] = dk_h if dk[b] is None else dk[b] + dk_h
                    more = nn(keys_t, ds)
                    dq = more if dq is None else dq + more
                dqt.append(dq)
            for b in range(blocks):
                dks[b].append(dk[b].astype(BF16))
                dvs[b].append(dv[b].astype(BF16))
        dq = (jnp.concatenate(dqt, axis=0) * size**-0.5).T.astype(BF16)
        gq_row = nn(norm_t[0][at], dq)
        gk_row = gv_row = sum_k = sum_v = 0.0
        for b in range(blocks):
            dk = jnp.concatenate(dks[b], axis=1)
            dv = jnp.concatenate(dvs[b], axis=1)
            normed = jnp.concatenate([norm_t[c][at] for c in range(b * block, (b + 1) * block)], axis=1)
            gk_row += nn(normed, dk)
            gv_row += nn(normed, dv)
            sum_k += jnp.sum(dk.astype(F32), axis=0, keepdims=True)
            sum_v += jnp.sum(dv.astype(F32), axis=0, keepdims=True)
            dn = nt(dk, weights[1]) + nt(dv, weights[2])
            for i in range(block):
                part = dn[i * chip : (i + 1) * chip]
                if b + i == 0:
                    part += nt(dq, weights[0])
                dn_m[place][b * block + i] = part[:tok].astype(BF16)
                dn_o[0 if last else place][(row * stations if last else 0) + b * block + i] = part[tok:].astype(BF16)
        sum_q = jnp.sum(dq.astype(F32), axis=0, keepdims=True)
        rest = jnp.zeros((5, half), F32)
        values = (gq_row, gk_row, gv_row, go_row, jnp.concatenate([sum_q, sum_v, sum_k, rest]))
        made_here = [a + b for a, b in zip(made_here, values)]
    for i, (ref, value) in enumerate(zip((gq, gk, gv, go, sums), made_here)):
        ref[...] = value if sums_in is None else value + sums_in[i][...]
    if not last:
        return

    for r, part in enumerate(before):
        dn_o[0][r * stations : (r + 1) * stations] = part[...]
    vec = refs[0]
    lane = lax.broadcasted_iota(jnp.int32, (2, width), 1)
    both = sums[0:2, :]
    both = jnp.concatenate([both, both], axis=1)
    vec[0:2, :] = jnp.where((lane >= half) == (sp[0] == 1), both, 0.0)
    vec[2:3, :] = vec_in[7:8, :]
    vec[3:4, :] = vec_in[4:5, :]
    vec[4:8, :] = vec_in[0:4, :]
    vec[10:12, :] = vec_in[5:7, :]
    vec[12:16, :] = jnp.zeros((4, width), F32)
    wide = [weights[i].astype(F32) for i in range(3)]
    shifts = sum(w * sums[i : i + 1, :] for w, i in zip(wide, (0, 2, 1)))
    gains = sum(w * g[...] for w, g in zip(wide, (gq, gk, gv)))

    def across(values):
        folded = sum(values[:, i * 128 : (i + 1) * 128] for i in range(half // 128))
        return jnp.sum(folded.T, axis=0, keepdims=True)

    shift_grad = across(shifts)
    vec[9:10, :] = shift_grad
    vec[8:9, :] = (across(gains) - vectors[1:2, :] * shift_grad) / vectors[0:1, :]
    n = width // PIECES
    low = n // 2
    per = PIECES // 2
    for slot in range(PIECES):
        one, two = ones[slot // per], twos[slot // per]
        base = slot % per * n
        piece = sp[2] ^ slot
        part = pl.ds(pl.multiple_of(piece * n, n), n)
        one[base : base + n, :half] = gq[part, :].astype(BF16)
        one[base : base + n, half:] = gk[part, :].astype(BF16)
        piece = sp[3] ^ slot
        first = pl.ds(pl.multiple_of(piece * n, n), low)
        second = pl.ds(pl.multiple_of(piece * n + low, low), low)
        two[base : base + low, :half] = gv[first, :].astype(BF16)
        two[base : base + low, half:] = gv[second, :].astype(BF16)
        two[base + low : base + n, :] = go[pl.ds(pl.multiple_of(piece * low, low), low), :].astype(BF16)
    for i, two in enumerate(twos):
        lines = [vec[pl.ds(sp[3] ^ (i * per + s), 1), :] for s in range(per)]
        two[per * n :, :] = padded(lines).astype(BF16)


def last_kernel(tokens, gain, mid_grad, *refs):
    out = refs[-1]
    rows, tok, width = tokens.shape
    flat = rows * tok
    unit, scale = normalize(tokens[...].reshape(flat, width).astype(F32))
    parts = []
    for r in range(rows):
        part = refs[r][0].astype(F32) + refs[rows][r * refs[0].shape[0]].astype(F32)
        for arrived in refs[rows + 1 : -1]:
            part += arrived[r].astype(F32)
        parts.append(part)
    grad = mid_grad[...] + norm_back(jnp.concatenate(parts, axis=0), unit, scale, gain[0:1, :])
    out[...] = grad.astype(BF16).reshape(rows, tok, width)


def unpack_ffn_kernel(far, sp, *refs):
    refs = list(refs)
    d_both, u_both = refs[0:2], refs[2:4]
    down, up, done, d_wide, u_wide, sems = refs[-6:]
    done[...] = jnp.zeros_like(done)
    _, rd, width = d_both[0].shape
    ru = up.shape[0] // PIECES
    half = down.shape[0] // 2
    count = PIECES // GROUP
    copies = []
    for which in range(2):
        for i in range(GROUP // 2):
            at = which * (GROUP // 2) + i
            group = (GROUP // 2 if far else 0) + i
            for k in range(count):
                slot = i * count + k
                place = (sp[2] ^ k) & (count - 1)
                rows = pl.ds(pl.multiple_of(place * rd, rd), rd)
                d_wide[at, rows, :] = d_both[which][slot].astype(F32)
                place = (sp[3] ^ k) & (count - 1)
                rows = pl.ds(pl.multiple_of(place * ru, ru), ru)
                for n in range(rd // ru):
                    part = u_both[which][slot, n * ru : (n + 1) * ru, :]
                    u_wide[at, rows, n * width : (n + 1) * width] = part.astype(F32)
            size = count * rd
            rows = pl.ds(pl.multiple_of(sp[which] * half + ((sp[2] // count) ^ group) * size, size), size)
            copies.append(pltpu.make_async_copy(d_wide.at[at], down.at[rows, :], sems.at[2 * at]))
            copies[-1].start()
            size = count * ru
            rows = pl.ds(pl.multiple_of(((sp[3] // count) ^ group) * size, size), size)
            copies.append(pltpu.make_async_copy(u_wide.at[at], up.at[rows, half_of(sp[which], half)], sems.at[2 * at + 1]))
            copies[-1].start()
    for copy in copies:
        copy.wait()


def unpack_attend_kernel(sp, *refs):
    gq, gk, gv, go, *lines = refs[8:]
    vec = lines.pop()
    ones, twos = (refs[0:2], refs[2:4]), (refs[4:6], refs[6:8])
    width = gq.shape[0]
    half = width // 2
    n = width // PIECES
    low = n // 2
    per = PIECES // 2
    for slot in range(PIECES):
        base = slot % per * n
        for which in range(2):
            one, two = ones[which][slot // per], twos[which][slot // per]
            cols = half_of(sp[which], half)
            piece = sp[2] ^ slot
            rows = pl.ds(pl.multiple_of(piece * n, n), n)
            gq[rows, cols] = one[base : base + n, :half].astype(F32)
            gk[rows, cols] = one[base : base + n, half:].astype(F32)
            piece = sp[3] ^ slot
            first = pl.ds(pl.multiple_of(piece * n, n), low)
            second = pl.ds(pl.multiple_of(piece * n + low, low), low)
            gv[first, cols] = two[base : base + low, :half].astype(F32)
            gv[second, cols] = two[base : base + low, half:].astype(F32)
            out_rows = pl.ds(pl.multiple_of(sp[which] * half + piece * low, low), low)
            go[out_rows, :] = two[base + low : base + n, :].astype(F32)
    for side in range(2):
        both = twos[0][side][per * n :, :].astype(F32) + twos[1][side][per * n :, :].astype(F32)
        for s in range(per):
            vec[pl.ds(sp[3] ^ (side * per + s), 1), :] = both[s : s + 1]
    for line, row in zip(lines, (0, 1, 2, 4, 3, 8, 9, 10, 11)):
        count = line.shape[1] // width
        for i in range(count):
            line[:, i * width : (i + 1) * width] = vec[row + i : row + i + 1, :]


def total(*values):
    return sum(v.astype(F32) for v in values).astype(BF16)


def sum_kernel(*refs):
    refs[-1][...] = total(*[r[...] for r in refs[:-1]])


def upper_kernel(*refs):
    count = len(refs) // 3
    for i, out in enumerate(refs[2 * count :]):
        keep, got = refs[2 * i : 2 * i + 2]
        half = keep.shape[0] // 2
        out[...] = total(keep[half:], got[half:])


def quarter_kernel(d_keep, d_got, d_last, u_keep, u_got, u_last, keep, send):
    rd = d_keep.shape[1]
    half = keep.shape[0]
    for i in range(2 * half):
        out = send if i >= half else keep
        out[i % half, :rd] = total(d_keep[i], d_got[i], d_last[i])
        out[i % half, rd:] = total(u_keep[i], u_got[i], u_last[i])


def halve_kernel(keep, got, out_keep, out_send):
    out_keep[...] = total(keep[0], got[0])
    out_send[...] = total(keep[1], got[1])


def pair_kernel(one, two, out):
    out[0] = one[...]
    out[1] = two[...]


def divide_kernel(one, two, d, u):
    rd = d.shape[1]
    for i in range(d.shape[0]):
        part = (one if i < 2 else two)[i % 2]
        d[i] = part[:rd]
        u[i] = part[rd:]


def join_kernel(*refs):
    count = len(refs) // 3
    for i, out in enumerate(refs[2 * count :]):
        one, two = refs[2 * i : 2 * i + 2]
        out[: one.shape[0]] = one[...]
        out[one.shape[0] :] = two[...]


def attend_upper_kernel(one_keep, one_got, two_keep, two_got, one, two):
    n = one.shape[0]
    one[...] = total(one_keep[n:], one_got[n:])
    two[:n] = total(two_keep[n : 2 * n], two_got[n : 2 * n])
    lines = total(two_keep[2 * n :], two_got[2 * n :]).astype(F32)
    two[n:] = fill(lines[4:8])


def fill(lines):
    return jnp.concatenate([lines, jnp.zeros((16 - lines.shape[0], lines.shape[1]), F32)], axis=0).astype(BF16)


def attend_quarter_kernel(one_keep, one_got, one_last, two_keep, two_got, two_last, keep, send):
    count = 2 * keep.shape[0]
    n = one_last.shape[0] // count
    lines = total(two_keep[2 * count * n :], two_got[2 * count * n :], two_last[count * n :]).astype(F32)
    for i in range(count):
        out = (keep, send)[i // 2]
        part = slice(i * n, (i + 1) * n)
        out[i % 2, :n] = total(one_keep[part], one_got[part], one_last[part])
        out[i % 2, n : 2 * n] = total(two_keep[part], two_got[part], two_last[part])
        out[i % 2, 2 * n :] = jnp.broadcast_to(lines[i : i + 1], (16, lines.shape[1])).astype(BF16)


def attend_divide_kernel(first, second, one, two):
    n = one.shape[0] // 4
    lines = []
    for i in range(4):
        part = (first if i < 2 else second)[i % 2]
        one[i * n : (i + 1) * n] = part[:n]
        two[i * n : (i + 1) * n] = part[n : 2 * n]
        lines.append(part[2 * n :].astype(F32)[:1])
    two[4 * n :] = padded(lines).astype(BF16)


def attend_join_kernel(one_a, one_b, two_a, two_b, one, two):
    n = one_a.shape[0]
    one[:n] = one_a[...]
    one[n:] = one_b[...]
    two[:n] = two_a[:n]
    two[n : 2 * n] = two_b[:n]
    lines = jnp.concatenate([two_a[n:].astype(F32)[:4], two_b[n:].astype(F32)[:4]], axis=0)
    two[2 * n :] = fill(lines)


def norm_grad_kernel(chunk, rows, *refs):
    out = refs[-1]
    stations = refs[0].shape[0]
    for r in range(rows):
        out[r] = total(refs[r][chunk], refs[rows][r * stations + chunk], *[a[r] for a in refs[rows + 1 : -1]])


VMEM = pl.BlockSpec(memory_space=pltpu.VMEM)
SMEM = pl.BlockSpec(memory_space=pltpu.SMEM)
HBM = pl.BlockSpec(memory_space=pltpu.HBM)
ANY = pl.BlockSpec(memory_space=pl.ANY)


def call(kernel, ins, outs, scratch=(), us=1.0, limit=16, name=None, scalars=1, specs=None, grid=(), out_specs=None, aliases=None, extra=()):
    count = len(ins)

    def body_of(*refs):
        kernel(*refs[:count], *refs[count + len(extra) :])

    return pl.pallas_call(
        body_of,
        grid=grid,
        in_specs=[SMEM] * scalars + (specs or [VMEM] * (count - scalars)) + [ANY] * len(extra),
        out_specs=out_specs or [VMEM] * len(outs),
        input_output_aliases=aliases or {},
        out_shape=list(outs),
        scratch_shapes=list(scratch),
        compiler_params=pltpu.CompilerParams(vmem_limit_bytes=limit * MIB),
        cost_estimate=pl.CostEstimate(flops=int(us * 1.1e9), bytes_accessed=0, transcendentals=0),
        name=name,
    )(*ins, *extra)


def load(sp, arrays, halved, name, limit=16):
    shapes = [a.shape[:-1] + (a.shape[-1] // (2 if h else 1),) for a, h in zip(arrays, halved)]
    return call(
        functools.partial(load_kernel, halved), [sp] + arrays, [made(s, a.dtype) for s, a in zip(shapes, arrays)],
        scratch=[pltpu.SemaphoreType.DMA] * len(arrays), us=2.0, limit=limit, name=name, specs=[HBM] * len(arrays),
    )


def made(shape, dtype):
    return jax.ShapeDtypeStruct(shape, dtype)


def exchange(array, axis, mask):
    count = lax.axis_size(axis)
    return lax.ppermute(array, axis, [(i, i ^ mask) for i in range(count)])


def merge(kernel, ins, outs, name, extra=()):
    specs = [SMEM if a.dtype == jnp.int32 else VMEM for a in ins]
    return call(kernel, list(ins), list(outs), us=0.05, limit=8, name=name, scalars=0, specs=specs, extra=extra)


def tied(*arrays):
    return lax.optimization_barrier(arrays)


class Chain:
    def __init__(self, token):
        self.token = token

    def __call__(self, function, *args, **kwargs):
        outs = list(function(*args, extra=[self.token], **kwargs))
        self.token = outs[-1]
        return outs

    def hold(self, *arrays):
        *arrays, self.token = tied(*arrays, self.token)
        return arrays


def my_id(bits):
    out = 0
    for axis, mask in bits:
        out = out * 2 + jnp.where((lax.axis_index(axis) & mask) != 0, 1, 0)
    return out


def body(
    tokens, grad_out, crop, offsets, w_query, w_key, w_value, w_out, w_up, w_down, b_query, b_value,
    b_out, b_up, b_down, gain_one, shift_one, gain_two, shift_two,
):
    rows, tok, width = tokens.shape
    seq_count, dp_count = lax.axis_size("seq"), lax.axis_size("dp")
    stations = seq_count // 2
    hidden = w_up.shape[1]
    half = width // 2
    heads = HEADS // 2
    size = half // heads
    chip = 2 * tok
    flat = rows * tok
    small = stations <= 4
    seq = lax.axis_index("seq")
    core, station = seq % 2, seq // 2
    line = lambda v: v.reshape(1, -1)

    dp_bits = [("dp", 1 << i) for i in range(dp_count.bit_length() - 1)]
    st_bits = [("seq", 2 << i) for i in range(stations.bit_length() - 1)]
    bit_x, bit_y = dp_bits[:2]
    rest = dp_bits[2:] + st_bits[2:]
    ids = [my_id([bit_x, bit_y] + st_bits[:2]), my_id([bit_y, bit_x] + st_bits[:2])]
    sp = jnp.stack([core, 1 - core, *ids, station]).astype(jnp.int32)

    mine = lambda a: lax.dynamic_slice_in_dim(a, core * half, half, a.ndim - 1)
    weights = jnp.stack([mine(w_query), mine(w_key), mine(w_value)])
    vectors = jnp.stack([gain_one, shift_one, b_query, b_value] + [jnp.zeros_like(gain_one)] * 4)
    state = []
    kept = [[None] * stations for _ in range(4)]
    blocks = {0: tokens}
    turns = [int(f"{i:0{stations.bit_length() - 1}b}"[::-1], 2) for i in range(stations)]
    for at, j in enumerate(turns):
        if j:
            low = j & -j
            block = blocks[j] = exchange(blocks[j ^ low], "seq", 2 * low)
            if at == 1 or at == stations - 1:
                block, state[-1] = tied(block, state[-1])
                blocks[j] = block
        else:
            block = tokens
        other = exchange(block, "seq", 1)
        first, last = at == 0, at == stations - 1
        ins = [sp, offsets, crop, block, other, vectors, weights] + ([] if first else state)
        outs = [
            made((rows, chip, half), BF16),
            made((rows, chip, half), BF16),
            made((rows, half, chip), BF16),
            made((rows, width, chip), BF16),
        ]
        if first:
            outs += [made((rows * heads, chip, 2 * size), BF16)]
        stat = made((rows * heads, 1, chip), F32)
        acc = made((rows * heads, size, chip), F32)
        if last:
            outs += [stat, acc, made((rows, tok, half), BF16), made((rows, tok, half), BF16)]
        else:
            outs += [stat, stat, acc]
        got = call(
            functools.partial(chunk_kernel, j, last, tok, rows), ins, outs,
            us=0.05, limit=LIMITS[0], name=f"attend_chunk_{j}", scalars=3,
        )
        for where, array in zip(kept, got[:4]):
            where[j] = array
        got = got[4:]
        if first:
            query, got = got[0], got[1:]
        if not last:
            state = [query] + list(got)
        if at == 0:
            sp_b, state[-1] = tied(sp, state[-1])
            tokens_v, g_v, wo, up, down, bo, bu, bd, gain_b, shift_b = load(
                sp_b,
                [tokens, grad_out, w_out, w_up, w_down, line(b_out), line(b_up), line(b_down), line(gain_two), line(shift_two)],
                [False] * 10, "load_feed_forward",
            )
            g_other = exchange(g_v, "seq", 1)
            state[-1], up = tied(state[-1], up)
        if at == 1:
            state[-1], g_other = tied(state[-1], g_other)
            g_other = g_other.reshape(flat, width)
    lse, out_t, att_m, att_o = got
    att_r = exchange(att_o, "seq", 1)

    wide = made((flat, width), F32)
    vec8 = made((8, width), F32)
    mid, normed_two, send, total, back, vec_a = call(
        ffn_first_kernel, [sp, att_m, att_r, wo, tokens_v, g_v, up, down, bo, bu, gain_b, shift_b],
        [wide, made((flat, width), BF16), made((flat, hidden + width), BF16), wide, wide, vec8],
        us=4.0, limit=LIMITS[1], name="feed_forward_a",
    )
    got = exchange(send, "seq", 1)
    outputs, hid_m, pre_m, mid_grad, branch, vec_ffn = call(
        ffn_second_kernel, [sp, mid, normed_two, g_v, up, down, bu, bd, gain_b, total, back, vec_a],
        [made((rows, tok, width), BF16), made((flat, hidden // 2), BF16), made((flat, hidden // 2), BF16), wide,
         made((rows, tok, width), BF16), vec8],
        us=4.0, limit=LIMITS[1], name="feed_forward_b",
    )
    branch_r = exchange(branch, "seq", 1)
    piece = made((PIECES // 2, hidden // 2 // PIECES, width), BF16)
    ins = [sp, hid_m, pre_m, normed_two, got, g_v.reshape(flat, width), g_other]
    d_send, u_send = call(
        functools.partial(ffn_grad_kernel, 1), ins, [piece, piece], us=3.0, limit=LIMITS[2], name="feed_forward_grad_sent"
    )
    d_send, u_send, branch_r = tied(d_send, u_send, branch_r)
    chain = Chain(d_send)
    d_keep, u_keep = chain(
        functools.partial(call, functools.partial(ffn_grad_kernel, 0)), ins, [piece, piece], us=0.05, limit=LIMITS[2],
        name="feed_forward_grad_kept",
    )

    q = PIECES // GROUP
    d_got, u_got = exchange(d_send, *bit_x), exchange(u_send, *bit_y)

    sums = []
    dn_m, dn_o, dn_r = [], [], []

    def together(name, *jobs):
        ins = [a for _, arrays, _ in jobs for a in arrays]
        outs = [s for _, _, shapes in jobs for s in shapes]

        def kernel(*refs):
            at, to = 0, len(ins)
            for one, arrays, shapes in jobs:
                one(*refs[at : at + len(arrays)], *refs[to : to + len(shapes)])
                at, to = at + len(arrays), to + len(shapes)

        res = iter(chain(functools.partial(merge, kernel), ins, outs, name))
        return [[next(res) for _ in shapes] for _, _, shapes in jobs]

    def norm_job(chunk, arrived):
        ins = [*dn_m, dn_r, *arrived]
        return (functools.partial(norm_grad_kernel, chunk, rows), ins, [made((rows, tok, width), BF16)])

    groups = [tuple(range(rows - 1)), (rows - 1,)] if small else [(r,) for r in range(rows)]
    for group in groups:
        r, last = group[-1], group[-1] == rows - 1
        arrays = [branch, branch_r, wo, query, lse, out_t, weights] + [a for part in kept for a in part]
        specs = [VMEM] * len(arrays)
        if not small:
            for i, a in enumerate(arrays):
                if a.ndim == 3 and a is not weights:
                    block_shape = (a.shape[0] // rows,) + a.shape[1:]
                    specs[i] = pl.BlockSpec(block_shape, functools.partial(lambda r, i: (r, 0, 0), r))
        tail = list(sums)
        if last:
            tail += [vectors, vec_ffn, *dn_o]
        part = made((stations, tok, width), BF16)
        grads = [made((width, half), F32)] * 3 + [made((half, width), F32), made((8, half), F32)]
        outs = [part] * (2 * len(group)) + grads
        scratch = []
        if last:
            outs = [part, made((rows * stations, tok, width), BF16)] + [made((width // 2, width), BF16)] * 2 + [made((width // 2 + 16, width), BF16)] * 2
            scratch = [pltpu.VMEM(g.shape, F32) for g in grads] + [pltpu.VMEM((16, width), F32)]
        run = functools.partial(call, functools.partial(attend_back_kernel, stations, tok, group, small, last))
        res = chain(
            run, [sp, offsets, crop] + arrays + tail, outs, scratch=scratch,
            us=BACK_US, limit=LIMITS[3] if small else 48, name=f"attend_back_{r}", scalars=3,
            specs=specs + [VMEM] * len(tail), grid=() if small else (1,),
        )
        if last:
            dn_m.append(res[0])
            dn_o.append(res[1])
        else:
            dn_m += res[: len(group)]
            dn_o += res[len(group) : 2 * len(group)]
            sums = list(res[2 * len(group) :])
        if r == rows - 2:
            quarters = made((q,) + piece.shape[1:], BF16)
            ((d_next, u_next),) = together(
                "add_quarters", (upper_kernel, [d_keep, d_got, u_keep, u_got], [quarters, quarters])
            )
            d_got2, u_got2 = exchange(d_next, *bit_y), exchange(u_next, *bit_x)
    one_keep, one_send, two_keep, two_send = res[2:]

    rd = hidden // 2 // PIECES
    n = width // PIECES
    ff_part, at_part = made((2 * rd, width), BF16), made((2 * n + 16, width), BF16)
    two_of = lambda a: made((2,) + a.shape, BF16)
    token_block = made((rows, tok, width), BF16)
    bit_z, bit_w = st_bits[:2]

    def over_rest(part):
        for i, (where, mask) in enumerate(rest):
            got = exchange(part, where, mask)
            ((part,),) = together(f"add_rest_{i}", (sum_kernel, [part, got], [made(part.shape, BF16)]))
        return part

    def unpack(far, d, d_other, u, u_other, before):
        ins = [sp, d, d_other, u, u_other] + before
        scratch = [
            pltpu.VMEM((GROUP, q * rd, width), F32), pltpu.VMEM((GROUP, q * width // PIECES, hidden // 2), F32),
            pltpu.SemaphoreType.DMA((2 * GROUP,)),
        ]
        return chain(
            functools.partial(call, functools.partial(unpack_ffn_kernel, far)), ins,
            [made((hidden, width), F32), made((width, hidden), F32), made((8, 128), F32)], scratch=scratch, us=0.1,
            limit=LIMITS[4], name="unpack_feed_forward", specs=[VMEM] * 4 + [HBM] * len(before),
            out_specs=[HBM] * 2 + [VMEM], aliases={5: 0, 6: 1} if before else None,
        )[:2]

    def other_core(*arrays):
        return [exchange(a, "seq", 1) for a in arrays]

    two_a, two_b = two_of(ff_part), two_of(at_part)
    ((a_keep, a_send),) = together(
        "phase_1", (quarter_kernel, [d_keep, d_got, d_got2, u_keep, u_got, u_got2], [two_a, two_a])
    )
    one_send, two_send = chain.hold(one_send, two_send)
    a_got = exchange(a_send, *bit_z)
    one_got, two_got = exchange(one_send, *bit_x), exchange(two_send, *bit_y)

    one_shape, two_shape = made((4 * n, width), BF16), made((4 * n + 16, width), BF16)
    (a_keep, a_send), (one_next, two_next) = together(
        "phase_2",
        (halve_kernel, [a_keep, a_got], [ff_part] * 2),
        (attend_upper_kernel, [one_keep, one_got, two_keep, two_got], [one_shape, two_shape]),
    )
    a_got = exchange(a_send, *bit_w)
    one_got2, two_got2 = exchange(one_next, *bit_y), exchange(two_next, *bit_x)

    (a_own,), (b_keep, b_send) = together(
        "phase_3",
        (sum_kernel, [a_keep, a_got], [ff_part]),
        (attend_quarter_kernel, [one_keep, one_got, one_got2, two_keep, two_got, two_got2], [two_b, two_b]),
    )
    (dn_r,) = chain.hold(*other_core(*chain.hold(dn_o[-1])))
    a_own = over_rest(a_own)
    a_near = exchange(a_own, *bit_w)
    b_got = exchange(b_send, *bit_z)

    (a_pair,), (b_keep, b_send) = together(
        "phase_4",
        (pair_kernel, [a_own, a_near], [two_a]),
        (halve_kernel, [b_keep, b_got], [at_part] * 2),
    )
    a_far = exchange(a_pair, *bit_z)
    b_got = exchange(b_send, *bit_w)

    arrived = {c: [] for c in range(stations)}
    top = stations // 2
    inner = [c for c in reversed(turns) if c not in (0, 1, top)]
    for c in inner[:-1]:
        ((moving,),) = together("norm_step", norm_job(c, arrived[c]))
        arrived[c & (c - 1)].append(exchange(moving, "seq", 2 * (c & -c)))
    c = inner[-1]
    (d_mine, u_mine), (b_own,), (moving,) = together(
        "phase_5",
        (divide_kernel, [a_pair, a_far], [quarters, quarters]),
        (sum_kernel, [b_keep, b_got], [at_part]),
        norm_job(c, arrived[c]),
    )
    b_own = over_rest(b_own)
    d_y, u_x = exchange(d_mine, *bit_y), exchange(u_mine, *bit_x)
    b_near = exchange(b_own, *bit_w)
    (moving,) = chain.hold(exchange(moving, "seq", 2 * (c & -c)))
    arrived[c & (c - 1)].append(moving)

    (d_near, u_near), (b_pair,), (moving,) = together(
        "phase_6",
        (join_kernel, [d_mine, d_y, u_mine, u_x], [piece, piece]),
        (pair_kernel, [b_own, b_near], [two_b]),
        norm_job(top, arrived[top]),
    )
    d_far, u_far = exchange(d_near, *bit_x), exchange(u_near, *bit_y)
    b_far = exchange(b_pair, *bit_z)
    moving = exchange(moving, "seq", 2 * top)
    d_far, u_far = chain.hold(d_far, u_far)

    (one_mine, two_mine), (nearest,) = together(
        "phase_7", (attend_divide_kernel, [b_pair, b_far], [one_shape, two_shape]), norm_job(1, [])
    )
    one_y, two_x = exchange(one_mine, *bit_y), exchange(two_mine, *bit_x)
    nearest = exchange(chain.hold(nearest)[0], "seq", 2)
    (moving,) = chain.hold(moving)
    ((one_near, two_near),) = together(
        "phase_8",
        (
            attend_join_kernel, [one_mine, one_y, two_mine, two_x],
            [made((8 * n, width), BF16), made((8 * n + 16, width), BF16)],
        ),
    )
    one_far, two_far = exchange(one_near, *bit_x), exchange(two_near, *bit_y)
    d_near_o, u_near_o = chain.hold(*other_core(d_near, u_near))
    grad_down, grad_up = unpack(False, d_near, d_near_o, u_near, u_near_o, [])
    d_far_o, u_far_o = chain.hold(*other_core(d_far, u_far))
    grad_down, grad_up = unpack(True, d_far, d_far_o, u_far, u_far_o, [grad_down, grad_up])
    far_held = chain.hold(one_far, two_far, nearest)
    nearest = far_held[2]
    one_near_o, two_near_o = other_core(*chain.hold(one_near, two_near))
    one_far_o, two_far_o = other_core(*far_held[:2])
    input_grad = call(
        last_kernel, [tokens_v, vectors, mid_grad, *dn_m, dn_r, *arrived[0], moving, nearest], [token_block],
        us=0.1, limit=LIMITS[4], name="input_grad", scalars=0, extra=[chain.token],
    )[0]
    one_all = [one_near, one_far, one_near_o, one_far_o]
    two_all = [two_near, two_far, two_near_o, two_far_o]
    square = made((width, width), F32)
    run = functools.partial(call, unpack_attend_kernel)
    thin = made((1, width), F32)
    results = chain(
        run, [sp] + one_all + two_all, [square] * 4 + [thin] * 3 + [made((1, hidden), F32)] + [thin] * 5,
        scratch=[pltpu.VMEM((PIECES, width), F32)], us=0.1, limit=LIMITS[4], name="unpack_attend",
    )
    grad_query, grad_key, grad_value, grad_out_proj = results[:4]
    lines = [r.reshape(-1) for r in results[4:]]

    return (outputs, input_grad, grad_query, grad_key, grad_value, grad_out_proj, grad_up, grad_down, *lines)


def solution(mesh):
    split, row, copied = P("dp", "seq", None), P("dp"), P()
    return jax.shard_map(
        body,
        mesh=mesh,
        in_specs=(split, split, row, P("dp", None)) + (copied,) * 15,
        out_specs=(split, split) + (copied,) * 15,
        check_vma=False,
    )
```
